32 devices in a mesh: dp: 8 (over z, x), mp: 4 (over y, core).
Axes of the slice: x: 2, y: 2, z: 4, core: 2. Of those that a mesh axis runs over, the one named last changes fastest.
Arguments:
- tokens: bfloat16 [16384, 1024], P('dp', 'mp'), may hold values from -6 to 6
- cotangent: bfloat16 [2448, 1024], P('dp', 'mp'), may hold values from -8 to 8
- mask_rows: int32 [16, 153], P('dp'), may hold values from 0 to 1023, as said below
- genome: int32 [16], P('dp'), may hold values from 0 to 15
- group_tokens: int32 [16], replicated, may hold values from 1000 to 29999
- owner: int32 [8], replicated, may hold values from 0 to 7, each once
- qkv_master: float32 [3, 1024, 1024], P(None, 'dp', 'mp'), may hold values from -0.1875 to 0.1875
- qkv_first: float32 [3, 1024, 1024], P(None, 'dp', 'mp'), may hold values from -384 to 384
- qkv_second: float32 [3, 1024, 1024], P(None, 'dp', 'mp'), may hold values from 1762.56 to 21150.72
- qkv_average: float32 [3, 1024, 1024], P(None, 'dp', 'mp'), may hold values from -0.1875 to 0.1875
- proj_master: float32 [1024, 1024], P('mp', 'dp'), may hold values from -3.5 to 3.5
- proj_first: float32 [1024, 1024], P('mp', 'dp'), may hold values from -20 to 20
- proj_second: float32 [1024, 1024], P('mp', 'dp'), may hold values from 4.78125 to 57.375
- proj_average: float32 [1024, 1024], P('mp', 'dp'), may hold values from -3.5 to 3.5
- gate_up_master: float32 [2, 1024, 4096], P(None, 'dp', 'mp'), may hold values from -0.1875 to 0.1875
- gate_up_first: float32 [2, 1024, 4096], P(None, 'dp', 'mp'), may hold values from -96 to 96
- gate_up_second: float32 [2, 1024, 4096], P(None, 'dp', 'mp'), may hold values from 110.16 to 1321.92
- gate_up_average: float32 [2, 1024, 4096], P(None, 'dp', 'mp'), may hold values from -0.1875 to 0.1875
- down_master: float32 [4096, 1024], P('mp', 'dp'), may hold values from -0.09375 to 0.09375
- down_first: float32 [4096, 1024], P('mp', 'dp'), may hold values from -192 to 192
- down_second: float32 [4096, 1024], P('mp', 'dp'), may hold values from 440.64 to 5287.68
- down_average: float32 [4096, 1024], P('mp', 'dp'), may hold values from -0.09375 to 0.09375
- gains_master: float32 [2, 1024], P(None, 'dp'), may hold values from 0.5 to 1.5
- gains_first: float32 [2, 1024], P(None, 'dp'), may hold values from -384 to 384
- gains_second: float32 [2, 1024], P(None, 'dp'), may hold values from 2068.56 to 24822.72
- gains_average: float32 [2, 1024], P(None, 'dp'), may hold values from 0.5 to 1.5
Outputs:
- output: bfloat16 [16384, 1024], P('dp', 'mp')
- input_grad: bfloat16 [16384, 1024], P('dp', 'mp')
- qkv_grad: float32 [3, 1024, 1024], P(None, 'dp', 'mp')
- qkv_new: float32 [3, 1024, 1024], P(None, 'dp', 'mp')
- qkv_first_new: float32 [3, 1024, 1024], P(None, 'dp', 'mp')
- qkv_second_new: float32 [3, 1024, 1024], P(None, 'dp', 'mp')
- qkv_average_new: float32 [3, 1024, 1024], P(None, 'dp', 'mp')
- qkv_copy: bfloat16 [3, 1024, 1024], P(None, 'dp', 'mp')
- proj_grad: float32 [1024, 1024], P('mp', 'dp')
- proj_new: float32 [1024, 1024], P('mp', 'dp')
- proj_first_new: float32 [1024, 1024], P('mp', 'dp')
- proj_second_new: float32 [1024, 1024], P('mp', 'dp')
- proj_average_new: float32 [1024, 1024], P('mp', 'dp')
- proj_copy: bfloat16 [1024, 1024], P('mp', 'dp')
- gate_up_grad: float32 [2, 1024, 4096], P(None, 'dp', 'mp')
- gate_up_new: float32 [2, 1024, 4096], P(None, 'dp', 'mp')
- gate_up_first_new: float32 [2, 1024, 4096], P(None, 'dp', 'mp')
- gate_up_second_new: float32 [2, 1024, 4096], P(None, 'dp', 'mp')
- gate_up_average_new: float32 [2, 1024, 4096], P(None, 'dp', 'mp')
- gate_up_copy: bfloat16 [2, 1024, 4096], P(None, 'dp', 'mp')
- down_grad: float32 [4096, 1024], P('mp', 'dp')
- down_new: float32 [4096, 1024], P('mp', 'dp')
- down_first_new: float32 [4096, 1024], P('mp', 'dp')
- down_second_new: float32 [4096, 1024], P('mp', 'dp')
- down_average_new: float32 [4096, 1024], P('mp', 'dp')
- down_copy: bfloat16 [4096, 1024], P('mp', 'dp')
- gains_grad: float32 [2, 1024], P(None, 'dp')
- gains_new: float32 [2, 1024], P(None, 'dp')
- gains_first_new: float32 [2, 1024], P(None, 'dp')
- gains_second_new: float32 [2, 1024], P(None, 'dp')
- gains_average_new: float32 [2, 1024], P(None, 'dp')
- gains_copy: bfloat16 [2, 1024], P(None, 'dp')
The draws below stay inside these ranges and needn't reach their ends.
Inputs may be any that keep to these rules, and one draw needn't show every extreme that they name: `mask_rows`: each row lists 153 distinct positions of its window. A permutation: index j of dp holds block owner[j] of the model-width dimension of every weight.
All inputs are finite; a program needn't handle non-finite values.
Results may differ from the reference program's by a relative error of at most 0.017.
Values may be sent and summed in bfloat16 or wider, within the bound.
No kernel may reach another device: no remote copies, remote signals or barrier semaphores. Data moves between devices by JAX's collectives and lax.ppermute only.
A program may use at most 192 MiB of HBM per device.

```python
import math
import jax
import jax.numpy as jnp
from jax import lax

D = 1024
FF = 4096
HEADS = 16
HEAD_DIM = 64
SEQ = 1024
NGROUP = 16
STEP = 7
NMASK = 153
N_WIN = 16
TOKENS = 16384
MASKED = 2448
N_DP = 8


def draw_mask_rows(key, part):
    key = jax.random.fold_in(key, 11)
    window_keys = jax.random.split(key, N_WIN)

    def one_window(window_key):
        return jax.random.permutation(window_key, SEQ)[:NMASK]
    return jax.vmap(one_window)(window_keys).astype(jnp.int32)


def plant(entries, own_key, low, top_value):
    place = [jax.random.randint(jax.random.fold_in(own_key, axis), (), 0, length) for axis, length in enumerate(entries.shape)]
    main_axis = entries.shape.index(max(entries.shape))
    beside = place[:main_axis] + [(place[main_axis] + 1) % entries.shape[main_axis]] + place[main_axis + 1:]
    return entries.at[tuple(place)].set(low).at[tuple(beside)].set(top_value)


def raised(result, stream_key, source, target, shards_of, factor):
    owner, partner = [(jnp.arange(result.shape[dim]) // (result.shape[dim] // shards_of)).reshape([-1 if axis == dim else 1 for axis in range(result.ndim)]) for dim in (source, target)]
    chosen = jax.random.permutation(stream_key, shards_of)[partner]
    strong = (owner == chosen) | (owner == (partner + shards_of // 2) % shards_of)
    return jnp.where(strong, factor * result, result)


def block_levels(key, shape, cuts, least, high):
    level = 1.0
    for axis_at, blocks in cuts:
        heights = jax.random.uniform(jax.random.fold_in(jax.random.fold_in(key, 6), axis_at), (blocks,), jnp.float32, least / len(cuts), high / len(cuts))
        level = level * jnp.repeat(jnp.exp(heights), shape[axis_at] // blocks).reshape((-1,) + (1,) * (len(shape) - 1 - axis_at))
    return level


def scatter_about(stream_key, extent, deviation, most, cuts=(), held_as=jnp.bfloat16):
    values = jax.random.normal(stream_key, extent, jnp.float32) * deviation
    if len(cuts) > 0:
        values = block_levels(stream_key, extent, cuts, -0.22, 0.18) * values
    return jnp.clip(values, min=-most, max=most).astype(held_as)


def gaussian_with(stream_key, shape, width, bound, cuts, heavy, kind=jnp.bfloat16):
    drawn = width * jax.random.normal(stream_key, shape, jnp.float32)
    if cuts:
        drawn = drawn * block_levels(stream_key, shape, cuts, -0.22, 0.18)
    return jnp.clip(raised(drawn, jax.random.fold_in(stream_key, 3), *heavy), -bound, bound).astype(kind)


def setup_inputs(seed: int = 0) -> dict:
    arg_keys = jax.random.split(jax.random.key(seed), 27)
    return {
        "tokens": scatter_about(arg_keys[0], (TOKENS, D), 1.0, 6.0, ((0, 8), (1, 4))),
        "cotangent": gaussian_with(arg_keys[1], (MASKED, D), 1.0, 8.0, ((0, 8), (1, 4)), (0, 1, 8, 2.0)),
        "mask_rows": draw_mask_rows(jax.random.fold_in(arg_keys[26], 71), 0),
        "genome": plant(jax.random.randint(arg_keys[3], (N_WIN,), 0, NGROUP), jax.random.fold_in(arg_keys[3], 1), 0, NGROUP - 1).astype(jnp.int32),
        "group_tokens": plant(jax.random.randint(arg_keys[4], (NGROUP,), 1000, 30000), jax.random.fold_in(arg_keys[4], 1), 1000, 29999).astype(jnp.int32),
        "owner": jax.random.permutation(arg_keys[5], N_DP).astype(jnp.int32),
        "qkv_master": scatter_about(arg_keys[6], (3, D, D), D ** -0.5, 0.1875, ((1, 8), (2, 4)), jnp.float32),
        "qkv_first": scatter_about(arg_keys[7], (3, D, D), (1.2 * MASKED ** 0.5), 384.0, ((1, 8), (2, 4)), jnp.float32),
        "qkv_second": jnp.clip(jnp.exp(math.log(21150.72) - 2.4849066 * jax.random.uniform(arg_keys[8], (3, D, D), jnp.float32) ** block_levels(arg_keys[8], (3, D, D), ((1, 8), (2, 4)), -0.2, 0.2)), 1762.56, 21150.72),
        "qkv_average": scatter_about(arg_keys[9], (3, D, D), D ** -0.5, 0.1875, ((1, 8), (2, 4)), jnp.float32),
        "proj_master": scatter_about(arg_keys[10], (D, D), (3 * D / SEQ) ** -0.5, 3.5, ((0, 4), (1, 8)), jnp.float32),
        "proj_first": scatter_about(arg_keys[11], (D, D), (2.0 * (MASKED / SEQ) ** 0.5), 20.0, ((0, 4), (1, 8)), jnp.float32),
        "proj_second": jnp.clip(jnp.exp(math.log(57.375) - 2.4849066 * jax.random.uniform(arg_keys[12], (D, D), jnp.float32) ** block_levels(arg_keys[12], (D, D), ((0, 4), (1, 8)), -0.2, 0.2)), 4.78125, 57.375),
        "proj_average": scatter_about(arg_keys[13], (D, D), (3 * D / SEQ) ** -0.5, 3.5, ((0, 4), (1, 8)), jnp.float32),
        "gate_up_master": scatter_about(arg_keys[14], (2, D, FF), D ** -0.5, 0.1875, ((1, 8), (2, 4)), jnp.float32),
        "gate_up_first": scatter_about(arg_keys[15], (2, D, FF), (0.3 * MASKED ** 0.5), 96.0, ((1, 8), (2, 4)), jnp.float32),
        "gate_up_second": jnp.clip(jnp.exp(math.log(1321.92) - 2.4849066 * jax.random.uniform(arg_keys[16], (2, D, FF), jnp.float32) ** block_levels(arg_keys[16], (2, D, FF), ((1, 8), (2, 4)), -0.2, 0.2)), 110.16, 1321.92),
        "gate_up_average": scatter_about(arg_keys[17], (2, D, FF), D ** -0.5, 0.1875, ((1, 8), (2, 4)), jnp.float32),
        "down_master": scatter_about(arg_keys[18], (FF, D), FF ** -0.5, 0.09375, ((0, 4), (1, 8)), jnp.float32),
        "down_first": scatter_about(arg_keys[19], (FF, D), (0.6 * MASKED ** 0.5), 192.0, ((0, 4), (1, 8)), jnp.float32),
        "down_second": jnp.clip(jnp.exp(math.log(5287.68) - 2.4849066 * jax.random.uniform(arg_keys[20], (FF, D), jnp.float32) ** block_levels(arg_keys[20], (FF, D), ((0, 4), (1, 8)), -0.2, 0.2)), 440.64, 5287.68),
        "down_average": scatter_about(arg_keys[21], (FF, D), FF ** -0.5, 0.09375, ((0, 4), (1, 8)), jnp.float32),
        "gains_master": jnp.clip(1.0 + 0.1 * jax.random.normal(arg_keys[22], (2, D), jnp.float32), 0.5, 1.5),
        "gains_first": scatter_about(arg_keys[23], (2, D), (1.3 * MASKED ** 0.5), 384.0, ((1, 8),), jnp.float32),
        "gains_second": jnp.clip(jnp.exp(math.log(24822.72) - 2.4849066 * jax.random.uniform(arg_keys[24], (2, D), jnp.float32) ** block_levels(arg_keys[24], (2, D), ((1, 8),), -0.2, 0.2)), 2068.56, 24822.72),
        "gains_average": jnp.clip(1.0 + 0.1 * jax.random.normal(arg_keys[25], (2, D), jnp.float32), 0.5, 1.5),
    }


EPS = 1e-05
THETA = 10000.0
BETA_ONE = 0.5
BETA_TWO = 0.5
ADAM_EPS = 1e-08
DECAY_RATE = 0.1
EMA_RATE = 0.6
GAIN_RATE = 0.4

@jax.custom_vjp
def low(v):
    return lax.optimization_barrier(v.astype(jnp.bfloat16)).astype(jnp.float32)

@jax.custom_vjp
def low_back(v):
    return v

def low_keep(v):
    return (low(v), None)

def low_pass(kept, grad):
    return (grad,)

def back_keep(v):
    return (v, None)

def back_low(kept, grad):
    return (low(grad),)
low.defvjp(low_keep, low_pass)
low_back.defvjp(back_keep, back_low)

def highest(left, right):
    return jnp.dot(left, right, precision=lax.Precision.HIGHEST, preferred_element_type=jnp.float32)

def rms_scale(values):
    return lax.rsqrt(lax.optimization_barrier(jnp.mean(values * values, axis=-1, keepdims=True)) + EPS)

def rotary_tables():
    half_dim = HEAD_DIM // 2
    frequency = THETA ** (-jnp.arange(half_dim, dtype=jnp.float32) / half_dim)
    angles = jnp.arange(SEQ, dtype=jnp.float32)[:, None] * frequency[None, :]
    return (jnp.cos(angles), jnp.sin(angles))

def rotate(values, cosine_rows, sine_rows):
    half_dim = values.shape[-1] // 2
    first_half = values[..., :half_dim]
    second_half = values[..., half_dim:]
    return jnp.concatenate([first_half * cosine_rows - second_half * sine_rows, second_half * cosine_rows + first_half * sine_rows], axis=-1)

def reorder(values, block_order):
    moved_axis = jnp.moveaxis(values, 1, 0)
    shaped = moved_axis.reshape((N_DP, moved_axis.shape[0] // N_DP) + moved_axis.shape[1:])
    taken = jnp.take(shaped, block_order, axis=0).reshape(moved_axis.shape)
    return jnp.moveaxis(taken, 0, 1)

def layer_forward(tokens_in, qkv_w, proj_w, gate_up_w, down_w, gains_w):
    cosine_table, sine_table = rotary_tables()
    cosine_rows = cosine_table[:, None, :]
    sine_rows = sine_table[:, None, :]
    heads_shape = (SEQ, HEADS, HEAD_DIM)
    norm_one = low(tokens_in * rms_scale(tokens_in) * gains_w[0])
    queries = low(rotate(low_back(highest(norm_one, qkv_w[0])).reshape(heads_shape), cosine_rows, sine_rows))
    keys_rot = low(rotate(low_back(highest(norm_one, qkv_w[1])).reshape(heads_shape), cosine_rows, sine_rows))
    values_in = low(low_back(highest(norm_one, qkv_w[2]))).reshape(heads_shape)
    scores = low_back(jnp.einsum('qhd,khd->hqk', queries, keys_rot, precision=lax.Precision.HIGHEST, preferred_element_type=jnp.float32) * HEAD_DIM ** (-0.5))
    probability = low(jax.nn.softmax(scores, axis=-1))
    attended = jnp.einsum('hqk,khd->qhd', probability, values_in, precision=lax.Precision.HIGHEST, preferred_element_type=jnp.float32).reshape(SEQ, D)
    attended = low(low_back(attended))
    residual = tokens_in + low_back(highest(attended, proj_w))
    norm_two = low(residual * rms_scale(residual) * gains_w[1])
    gate_act = low_back(highest(norm_two, gate_up_w[0]))
    upward = low_back(highest(norm_two, gate_up_w[1]))
    hidden = low(jax.nn.silu(gate_act) * upward)
    return residual + low_back(highest(hidden, down_w))

def adam_step(summed, master, first_old, second, average, step_rate, weight_decay):
    new_first = BETA_ONE * first_old + (1.0 - BETA_ONE) * summed
    new_second = BETA_TWO * second + (1.0 - BETA_TWO) * summed * summed
    update = new_first / (1.0 - BETA_ONE ** STEP) / (jnp.sqrt(new_second / (1.0 - BETA_TWO ** STEP)) + ADAM_EPS)
    new_master = master - step_rate * (update + weight_decay * master)
    new_average = EMA_RATE * average + (1.0 - EMA_RATE) * new_master
    return (summed, new_master, new_first, new_second, new_average, new_master.astype(jnp.bfloat16))

def reference(tokens, cotangent, mask_rows, genome, group_tokens, owner, qkv_master, qkv_first, qkv_second, qkv_average, proj_master, proj_first, proj_second, proj_average, gate_up_master, gate_up_first, gate_up_second, gate_up_average, down_master, down_first, down_second, down_average, gains_master, gains_first, gains_second, gains_average):
    inverse = jnp.argsort(owner).astype(jnp.int32)
    masters = (qkv_master, proj_master, gate_up_master, down_master, gains_master)
    weights_used = tuple((reorder(master, inverse).astype(jnp.bfloat16).astype(jnp.float32) for master in masters))
    counts = group_tokens.astype(jnp.float32)
    window_scale = NGROUP * counts[genome] / jnp.sum(counts)
    token_windows = tokens.astype(jnp.float32).reshape(N_WIN, SEQ, D)
    cot_windows = cotangent.astype(jnp.float32).reshape(N_WIN, NMASK, D)

    def one_window(totals, window_items):
        window_tokens, window_cot, window_rows, window_weight = window_items
        outcome, pullback = jax.vjp(layer_forward, window_tokens, *weights_used)
        seed_grad = jnp.zeros((SEQ, D), jnp.float32).at[window_rows].set(window_weight * window_cot)
        pulled = pullback(seed_grad)
        totals = tuple((running + pulled_grad for running, pulled_grad in zip(totals, pulled[1:])))
        return (totals, (outcome.astype(jnp.bfloat16), pulled[0].astype(jnp.bfloat16)))
    zero_grads = tuple((jnp.zeros_like(weight) for weight in weights_used))
    totals, (outcomes, input_grads) = lax.scan(one_window, zero_grads, (token_windows, cot_windows, mask_rows, window_scale))
    qkv_out = adam_step(reorder(totals[0], owner), qkv_master, qkv_first, qkv_second, qkv_average, D ** (-0.5), DECAY_RATE)
    proj_out = adam_step(reorder(totals[1], owner), proj_master, proj_first, proj_second, proj_average, (3.0 * D / SEQ) ** (-0.5), DECAY_RATE)
    gate_up_out = adam_step(reorder(totals[2], owner), gate_up_master, gate_up_first, gate_up_second, gate_up_average, D ** (-0.5), DECAY_RATE)
    down_out = adam_step(reorder(totals[3], owner), down_master, down_first, down_second, down_average, FF ** (-0.5), DECAY_RATE)
    gains_out = adam_step(reorder(totals[4], owner), gains_master, gains_first, gains_second, gains_average, GAIN_RATE, 0.0)
    return (outcomes.reshape(N_WIN * SEQ, D), input_grads.reshape(N_WIN * SEQ, D), *qkv_out, *proj_out, *gate_up_out, *down_out, *gains_out)
```

```python
import functools

import jax
import jax.numpy as jnp
from jax import lax
from jax.experimental import pallas as pl
from jax.experimental.pallas import tpu as pltpu
from jax.sharding import PartitionSpec as P

D = 1024
FF = 4096
HEAD_DIM = 64
SEQ = 1024
NGROUP = 16
STEP = 7

EPS = 1e-05
THETA = 10000.0
BETA_ONE = 0.5
BETA_TWO = 0.5
ADAM_EPS = 1e-08
DECAY_RATE = 0.1
EMA_RATE = 0.6
GAIN_RATE = 0.4

BF = jnp.bfloat16
F32 = jnp.float32
LANES = 128
TILE = 256
MIB = 1024 * 1024
SOFT = 1.4426950408889634 * HEAD_DIM**-0.5


def dot(a, b):
    return lax.dot_general(a, b, (((1,), (0,)), ((), ())), preferred_element_type=F32)


def dot_t(a, b):
    return lax.dot_general(a, b, (((1,), (1,)), ((), ())), preferred_element_type=F32)


def dot_l(a, b):
    return lax.dot_general(a, b, (((0,), (0,)), ((), ())), preferred_element_type=F32)


def params(mib, dims=None):
    return pltpu.CompilerParams(vmem_limit_bytes=mib * MIB, dimension_semantics=dims)


def swap(x, axis, bit):
    n = lax.axis_size(axis)
    return lax.ppermute(x, axis, [(i, i ^ bit) for i in range(n)])


def gather_mp(x):
    far = swap(x, "mp", 2)
    near = swap(x, "mp", 1)
    return [x, near, far, swap(far, "mp", 1)]


def whole(shape):
    return pl.BlockSpec(shape, lambda *_: (0,) * len(shape), pipeline_mode=pl.Buffered(1))


def cut(block, where):
    return pl.BlockSpec(block, where)


def rotary_tables(positions):
    half_dim = HEAD_DIM // 2
    frequency = THETA ** (-jnp.arange(half_dim, dtype=F32) / half_dim)
    angles = positions.astype(F32)[:, None] * frequency[None, :]
    cosine, sine = jnp.cos(angles), jnp.sin(angles)
    return (
        jnp.concatenate([cosine] * 4, axis=1),
        jnp.concatenate([-sine, sine, -sine, sine], axis=1),
    )


def turn(x, cos, sin, sign):
    lane = lax.broadcasted_iota(jnp.int32, (x.shape[0], LANES), 1)
    low = (lane % HEAD_DIM) < HEAD_DIM // 2
    parts = []
    for start in range(0, x.shape[1], LANES):
        v = x[:, start : start + LANES]
        other = jnp.where(
            low, pltpu.roll(v, LANES - HEAD_DIM // 2, 1), pltpu.roll(v, HEAD_DIM // 2, 1)
        )
        parts.append(v * cos + (sign * sin) * other)
    return jnp.concatenate(parts, axis=1)


def place_kernel(pos_ref, *refs):
    out = refs[-1]
    for p, piece in enumerate(refs[:-1]):
        rows = piece.shape[1]
        out[:, pl.ds(pl.multiple_of(pos_ref[p], rows), rows), :] = piece[...]


def place_pieces(pos, pieces):
    k, bs, n = pieces[0].shape
    total = bs * len(pieces)
    return pl.pallas_call(
        place_kernel,
        grid_spec=pltpu.PrefetchScalarGridSpec(
            num_scalar_prefetch=1,
            grid=(1,),
            in_specs=[pl.BlockSpec((k, bs, n), lambda i, pos: (0, 0, 0))] * len(pieces),
            out_specs=pl.BlockSpec((k, total, n), lambda i, pos: (0, 0, 0)),
        ),
        out_shape=jax.ShapeDtypeStruct((k, total, n), pieces[0].dtype),
        compiler_params=params(24),
    )(pos, *pieces)


def place_stack_kernel(pos_ref, in_ref, out_ref):
    out_ref[0] = in_ref[0, 0]


def place_stack(pos, stack):
    count, k, bs, n = stack.shape
    return pl.pallas_call(
        place_stack_kernel,
        grid_spec=pltpu.PrefetchScalarGridSpec(
            num_scalar_prefetch=1,
            grid=(count, k),
            in_specs=[pl.BlockSpec((1, 1, bs, n), lambda j, w, pos: (j, w, 0, 0))],
            out_specs=pl.BlockSpec((1, bs, n), lambda j, w, pos: (w, pos[j] // bs, 0)),
        ),
        out_shape=jax.ShapeDtypeStruct((k, count * bs, n), stack.dtype),
        compiler_params=params(16),
    )(pos, stack)


def qkv_kernel(x0, x1, x2, x3, g_ref, w_ref, cos_ref, sin_ref, oh_ref,
               qkv_ref, norm_ref, trow_ref, qrow_ref, tacc, qacc):
    step = pl.program_id(0)
    x = jnp.concatenate([x0[...], x1[...], x2[...], x3[...]], axis=1)
    xf = x.astype(F32)
    scale = lax.rsqrt(jnp.mean(xf * xf, axis=1, keepdims=True) + EPS)
    norm = (xf * scale * g_ref[...]).astype(BF)
    norm_ref[...] = norm
    cos, sin = cos_ref[...], sin_ref[...]
    q = turn(dot(norm, w_ref[0]), cos, sin, 1.0).astype(BF)
    qkv_ref[0] = q
    qkv_ref[1] = turn(dot(norm, w_ref[1]), cos, sin, 1.0).astype(BF)
    qkv_ref[2] = dot(norm, w_ref[2]).astype(BF)
    oh = oh_ref[...]

    @pl.when(step == 0)
    def _():
        tacc[...] = jnp.zeros_like(tacc)
        qacc[...] = jnp.zeros_like(qacc)

    tacc[...] += dot(oh, x)
    qacc[...] += dot(oh, q)

    @pl.when(step == pl.num_programs(0) - 1)
    def _():
        trow_ref[...] = tacc[...].astype(BF)
        qrow_ref[...] = qacc[...].astype(BF)


def qkv_call(pieces, w, gain, weights, cos, sin, onehot):
    share = pieces[0].shape[1]
    rows = onehot.shape[0]
    tiles = SEQ // TILE
    return pl.pallas_call(
        qkv_kernel,
        grid=(tiles,),
        in_specs=[cut((TILE, share), lambda i: (w * tiles + i, 0))] * 4
        + [
            whole((1, D)),
            whole((4, D, share)),
            cut((TILE, LANES), lambda i: (i, 0)),
            cut((TILE, LANES), lambda i: (i, 0)),
            cut((rows, TILE), lambda i: (0, i)),
        ],
        out_specs=[
            cut((3, TILE, share), lambda i: (0, i, 0)),
            cut((TILE, D), lambda i: (i, 0)),
            cut((rows, D), lambda i: (0, 0)),
            cut((rows, share), lambda i: (0, 0)),
        ],
        out_shape=[
            jax.ShapeDtypeStruct((3, SEQ, share), BF),
            jax.ShapeDtypeStruct((SEQ, D), BF),
            jax.ShapeDtypeStruct((rows, D), BF),
            jax.ShapeDtypeStruct((rows, share), BF),
        ],
        scratch_shapes=[pltpu.VMEM((rows, D), F32), pltpu.VMEM((rows, share), F32)],
        compiler_params=params(32),
        cost_estimate=pl.CostEstimate(
            flops=2 * SEQ * D * 3 * share, bytes_accessed=8 * MIB, transcendentals=0
        ),
    )(*pieces, gain, weights, cos, sin, onehot)


def attend_kernel(q_ref, k_ref, v_ref, oh_ref, ctx_ref, crow_ref, acc):
    step = pl.program_id(0)
    lane = lax.broadcasted_iota(jnp.int32, (TILE, LANES), 1)
    first = lane < HEAD_DIM
    ones = jnp.ones((SEQ, LANES), BF)
    parts = []
    for start in range(0, q_ref.shape[2], LANES):
        q = q_ref[0, :, start : start + LANES]
        k = k_ref[0, :, start : start + LANES]
        v = jnp.concatenate([v_ref[0, :, start : start + LANES], ones], axis=1)
        heads = []
        for mine in (first, jnp.logical_not(first)):
            scores = dot_t(jnp.where(mine, q, jnp.zeros_like(q)), k)
            top = jnp.max(scores, axis=1, keepdims=True)
            weight = jnp.exp2((scores - top) * SOFT).astype(BF)
            mixed = dot(weight, v)
            heads.append(mixed[:, :LANES] / mixed[:, LANES:])
        parts.append(jnp.where(first, heads[0], heads[1]))
    context = jnp.concatenate(parts, axis=1).astype(BF)
    ctx_ref[...] = context

    @pl.when(step == 0)
    def _():
        acc[...] = jnp.zeros_like(acc)

    acc[...] += dot(oh_ref[...], context)

    @pl.when(step == pl.num_programs(0) - 1)
    def _():
        crow_ref[...] = acc[...].astype(BF)


def attend_call(qkv, onehot):
    share = qkv.shape[2]
    rows = onehot.shape[0]
    return pl.pallas_call(
        attend_kernel,
        grid=(SEQ // TILE,),
        in_specs=[
            cut((1, TILE, share), lambda i: (0, i, 0)),
            cut((1, SEQ, share), lambda i: (1, 0, 0)),
            cut((1, SEQ, share), lambda i: (2, 0, 0)),
            cut((rows, TILE), lambda i: (0, i)),
        ],
        out_specs=[
            cut((TILE, share), lambda i: (i, 0)),
            cut((rows, share), lambda i: (0, 0)),
        ],
        out_shape=[
            jax.ShapeDtypeStruct((SEQ, share), BF),
            jax.ShapeDtypeStruct((rows, share), BF),
        ],
        scratch_shapes=[pltpu.VMEM((rows, share), F32)],
        compiler_params=params(32),
        cost_estimate=pl.CostEstimate(
            flops=16 * SEQ * SEQ * share, bytes_accessed=3 * MIB, transcendentals=4 * SEQ * SEQ
        ),
    )(qkv, qkv, qkv, onehot)


def attended(context_pieces, wo_refs):
    share = context_pieces[0].shape[1]
    chunks = [None] * 4
    for r, (piece, wo) in enumerate(zip(context_pieces, wo_refs, strict=True)):
        for c in range(4):
            own = c ^ r
            term = dot_t(piece, wo[c * share : (c + 1) * share, :])
            chunks[own] = term if chunks[own] is None else chunks[own] + term
    return jnp.concatenate(chunks, axis=1)


def ffn_kernel(x0, x1, x2, x3, c0, c1, c2, c3, o0, o1, o2, o3, g_ref, w_ref,
               send_ref, keep_ref, res_ref):
    share = x0.shape[1]
    x = jnp.concatenate([x0[...], x1[...], x2[...], x3[...]], axis=1).astype(F32)
    residual = x + attended([c0[...], c1[...], c2[...], c3[...]], [o0, o1, o2, o3])
    scale = lax.rsqrt(jnp.mean(residual * residual, axis=1, keepdims=True) + EPS)
    norm = (residual * scale * g_ref[...]).astype(BF)
    res_ref[...] = residual[:, :share]
    total = None
    width = w_ref.shape[2]
    for start in range(0, width, TILE):
        gate = dot(norm, w_ref[0, :, start : start + TILE])
        up = dot(norm, w_ref[1, :, start : start + TILE])
        hidden = (gate * jax.nn.sigmoid(gate) * up).astype(BF)
        term = dot_t(hidden, w_ref[2, :, start : start + TILE])
        total = term if total is None else total + term
    out = total.astype(BF)
    send_ref[...] = jnp.concatenate([out[:, share : 2 * share], out[:, 3 * share :]], axis=1)
    keep_ref[...] = jnp.concatenate([out[:, :share], out[:, 2 * share : 3 * share]], axis=1)


def ffn_call(pieces, w, contexts, wo, gain, weights):
    share = pieces[0].shape[1]
    width = weights.shape[2]
    tiles = SEQ // TILE
    return pl.pallas_call(
        ffn_kernel,
        grid=(tiles,),
        in_specs=[cut((TILE, share), lambda i: (w * tiles + i, 0))] * 4
        + [cut((TILE, share), lambda i: (i, 0))] * 4
        + [whole((D, share))] * 4
        + [whole((1, D)), whole((3, D, width))],
        out_specs=[
            cut((TILE, 2 * share), lambda i: (i, 0)),
            cut((TILE, 2 * share), lambda i: (i, 0)),
            cut((TILE, share), lambda i: (i, 0)),
        ],
        out_shape=[
            jax.ShapeDtypeStruct((SEQ, 2 * share), BF),
            jax.ShapeDtypeStruct((SEQ, 2 * share), BF),
            jax.ShapeDtypeStruct((SEQ, share), F32),
        ],
        compiler_params=params(40),
        cost_estimate=pl.CostEstimate(
            flops=8 * SEQ * D * D, bytes_accessed=16 * MIB, transcendentals=SEQ * width
        ),
    )(*pieces, *contexts, *wo, gain, weights)


def rows_kernel(t_ref, c0, c1, c2, c3, o0, o1, o2, o3, g_ref, seed_ref, w_ref,
                norm_ref, hid_ref, gg_ref, ug_ref, send_ref, keep_ref, unit_ref, scale_ref, acc):
    step = pl.program_id(0)
    share = c0.shape[1]

    @pl.when(step == 0)
    def _():
        residual = t_ref[...].astype(F32) + attended(
            [c0[...], c1[...], c2[...], c3[...]], [o0, o1, o2, o3]
        )
        scale = lax.rsqrt(jnp.mean(residual * residual, axis=1, keepdims=True) + EPS)
        unit = residual * scale
        unit_ref[...] = unit
        scale_ref[...] = jnp.broadcast_to(scale, scale_ref.shape)
        norm_ref[...] = (residual * scale * g_ref[...]).astype(BF)
        acc[...] = jnp.zeros_like(acc)

    norm = norm_ref[...]
    gate = dot(norm, w_ref[0])
    up = dot(norm, w_ref[1])
    sigmoid = jax.nn.sigmoid(gate)
    silu = gate * sigmoid
    hid_ref[...] = (silu * up).astype(BF)
    hidden_grad = dot(seed_ref[...], w_ref[2])
    gate_grad = (hidden_grad * up * sigmoid * (1.0 + gate * (1.0 - sigmoid))).astype(BF)
    up_grad = (hidden_grad * silu).astype(BF)
    gg_ref[...] = gate_grad
    ug_ref[...] = up_grad
    acc[...] += dot_t(gate_grad, w_ref[0]) + dot_t(up_grad, w_ref[1])

    @pl.when(step == pl.num_programs(0) - 1)
    def _():
        out = acc[...].astype(BF)
        send_ref[...] = jnp.concatenate([out[:, share : 2 * share], out[:, 3 * share :]], axis=1)
        keep_ref[...] = jnp.concatenate([out[:, :share], out[:, 2 * share : 3 * share]], axis=1)


def rows_call(token_rows, context_rows, wo, gain, seed, weights):
    rows = token_rows.shape[0]
    share = context_rows[0].shape[1]
    width = weights.shape[2]
    part = 256
    fixed = lambda shape: pl.BlockSpec(shape, lambda i: (0,) * len(shape))
    return pl.pallas_call(
        rows_kernel,
        grid=(width // part,),
        in_specs=[whole((rows, D))]
        + [whole((rows, share))] * 4
        + [whole((D, share))] * 4
        + [whole((1, D)), whole((rows, D)), cut((3, D, part), lambda i: (0, 0, i))],
        out_specs=[
            fixed((rows, D)),
            cut((rows, part), lambda i: (0, i)),
            cut((rows, part), lambda i: (0, i)),
            cut((rows, part), lambda i: (0, i)),
            fixed((rows, 2 * share)),
            fixed((rows, 2 * share)),
            fixed((rows, D)),
            fixed((rows, LANES)),
        ],
        out_shape=[
            jax.ShapeDtypeStruct((rows, D), BF),
            jax.ShapeDtypeStruct((rows, width), BF),
            jax.ShapeDtypeStruct((rows, width), BF),
            jax.ShapeDtypeStruct((rows, width), BF),
            jax.ShapeDtypeStruct((rows, 2 * share), BF),
            jax.ShapeDtypeStruct((rows, 2 * share), BF),
            jax.ShapeDtypeStruct((rows, D), F32),
            jax.ShapeDtypeStruct((rows, LANES), F32),
        ],
        scratch_shapes=[pltpu.VMEM((rows, D), F32)],
        compiler_params=params(40),
        cost_estimate=pl.CostEstimate(
            flops=12 * rows * D * D, bytes_accessed=12 * MIB, transcendentals=rows * width
        ),
    )(token_rows, *context_rows, *wo, gain, seed, weights)


def pack_kernel(pos_ref, lhs_ref, rhs_ref, out_ref):
    out_ref[0] = dot_l(lhs_ref[...], rhs_ref[...]).astype(BF)


def pack_send(pos, lhs, rhs):
    count = pos.shape[0]
    rows, n = rhs.shape
    return pl.pallas_call(
        pack_kernel,
        grid_spec=pltpu.PrefetchScalarGridSpec(
            num_scalar_prefetch=1,
            grid=(count,),
            in_specs=[
                pl.BlockSpec((rows, LANES), lambda i, pos: (0, pos[i] // LANES)),
                pl.BlockSpec((rows, n), lambda i, pos: (0, 0)),
            ],
            out_specs=pl.BlockSpec((1, LANES, n), lambda i, pos: (i, 0, 0)),
        ),
        out_shape=jax.ShapeDtypeStruct((count, LANES, n), BF),
        compiler_params=params(24),
        cost_estimate=pl.CostEstimate(
            flops=2 * rows * n * LANES * count, bytes_accessed=2 * MIB, transcendentals=0
        ),
    )(pos, lhs, rhs)


def pack_add_kernel(pos_ref, lhs_ref, rhs_ref, recv_ref, *outs):
    step = pl.program_id(0)
    value = dot_l(lhs_ref[...], rhs_ref[...]) + recv_ref[0].astype(F32)
    for k, out in enumerate(outs):

        @pl.when(step == k)
        def _(out=out):
            out[...] = value.astype(out.dtype)


def pack_keep(pos, lhs, rhs, received):
    count = pos.shape[0]
    rows, n = rhs.shape
    fixed = pl.BlockSpec((LANES, n), lambda i, pos: (0, 0))
    return pl.pallas_call(
        pack_add_kernel,
        grid_spec=pltpu.PrefetchScalarGridSpec(
            num_scalar_prefetch=1,
            grid=(count,),
            in_specs=[
                pl.BlockSpec((rows, LANES), lambda i, pos: (0, pos[i] // LANES)),
                pl.BlockSpec((rows, n), lambda i, pos: (0, 0)),
                pl.BlockSpec((1, LANES, n), lambda i, pos: (i, 0, 0)),
            ],
            out_specs=[fixed] * count,
        ),
        out_shape=[
            jax.ShapeDtypeStruct((LANES, n), F32 if k == 0 else BF) for k in range(count)
        ],
        compiler_params=params(24),
        cost_estimate=pl.CostEstimate(
            flops=2 * rows * n * LANES * count, bytes_accessed=3 * MIB, transcendentals=0
        ),
    )(pos, lhs, rhs, received)


def back_kernel(q_ref, do_ref, k_ref, v_ref, oh_ref, cosm_ref, sinm_ref, cos_ref, sin_ref, out_ref):
    rows, share = q_ref.shape
    lane = lax.broadcasted_iota(jnp.int32, (rows, LANES), 1)
    first = lane < HEAD_DIM
    scale = HEAD_DIM**-0.5
    dq_parts, dk_parts, dv_parts = [], [], []
    for start in range(0, share, LANES):
        q = q_ref[:, start : start + LANES]
        do = do_ref[:, start : start + LANES]
        k = k_ref[0, :, start : start + LANES]
        v = v_ref[0, :, start : start + LANES]
        dqs, dk, dv = [], None, None
        for mine in (first, jnp.logical_not(first)):
            qm = jnp.where(mine, q, jnp.zeros_like(q))
            dm = jnp.where(mine, do, jnp.zeros_like(do))
            scores = dot_t(qm, k)
            top = jnp.max(scores, axis=1, keepdims=True)
            weight = jnp.exp2((scores - top) * SOFT)
            prob = weight * (1.0 / jnp.sum(weight, axis=1, keepdims=True))
            prob_grad = dot_t(dm, v)
            delta = jnp.sum(prob * prob_grad, axis=1, keepdims=True)
            score_grad = (prob * (prob_grad - delta)).astype(BF)
            dqs.append(dot(score_grad, k))
            term = dot_l(score_grad, qm)
            dk = term if dk is None else dk + term
            term = dot_l(prob.astype(BF), dm)
            dv = term if dv is None else dv + term
        dq_parts.append(jnp.where(first, dqs[0], dqs[1]) * scale)
        dk_parts.append(dk * scale)
        dv_parts.append(dv)
    dq = turn(jnp.concatenate(dq_parts, axis=1), cosm_ref[...], sinm_ref[...], -1.0).astype(BF)
    out_ref[:, :share] = dot_l(oh_ref[...], dq).astype(BF)
    dk = turn(jnp.concatenate(dk_parts, axis=1), cos_ref[...], sin_ref[...], -1.0)
    out_ref[:, share : 2 * share] = dk.astype(BF)
    out_ref[:, 2 * share :] = jnp.concatenate(dv_parts, axis=1).astype(BF)


def back_call(q_rows, context_grad, w, qkv, onehot, cosm, sinm, cos, sin):
    rows, share = q_rows.shape
    here = lambda shape: pl.BlockSpec(shape, lambda i: (w,) + (0,) * (len(shape) - 1))
    zero = lambda shape: pl.BlockSpec(shape, lambda i: (0,) * len(shape))
    return pl.pallas_call(
        back_kernel,
        grid=(1,),
        in_specs=[
            zero((rows, share)),
            here((rows, share)),
            pl.BlockSpec((1, SEQ, share), lambda i: (1, 0, 0)),
            pl.BlockSpec((1, SEQ, share), lambda i: (2, 0, 0)),
            zero((rows, SEQ)),
            here((rows, LANES)),
            here((rows, LANES)),
            zero((SEQ, LANES)),
            zero((SEQ, LANES)),
        ],
        out_specs=zero((SEQ, 3 * share)),
        out_shape=jax.ShapeDtypeStruct((SEQ, 3 * share), BF),
        compiler_params=params(40),
        cost_estimate=pl.CostEstimate(
            flops=40 * rows * SEQ * share, bytes_accessed=4 * MIB, transcendentals=4 * rows * SEQ
        ),
    )(q_rows, context_grad, qkv, qkv, onehot, cosm, sinm, cos, sin)


def first_grad_kernel(d_ref, w_ref, x0, x1, x2, x3, g_ref, send_ref, keep_ref, dot_ref, col_ref):
    share = x0.shape[1]
    grad = None
    for t in range(3):
        term = dot_t(d_ref[:, t * share : (t + 1) * share], w_ref[t])
        grad = term if grad is None else grad + term
    x = jnp.concatenate([x0[...], x1[...], x2[...], x3[...]], axis=1).astype(F32)
    scale = lax.rsqrt(jnp.mean(x * x, axis=1, keepdims=True) + EPS)
    gz = grad * (x * scale)
    dot_ref[...] = jnp.sum(gz * g_ref[...], axis=1, keepdims=True)
    out = grad.astype(BF)
    send_ref[...] = jnp.concatenate([out[:, share : 2 * share], out[:, 3 * share :]], axis=1)
    keep_ref[...] = jnp.concatenate([out[:, :share], out[:, 2 * share : 3 * share]], axis=1)

    @pl.when(pl.program_id(0) == 0)
    def _():
        col_ref[...] = jnp.zeros_like(col_ref)

    col_ref[...] += jnp.sum(gz, axis=0, keepdims=True)


def first_grad_call(dqkv, weights, pieces, w, gain):
    share = pieces[0].shape[1]
    tiles = SEQ // TILE
    return pl.pallas_call(
        first_grad_kernel,
        grid=(tiles,),
        in_specs=[cut((TILE, 3 * share), lambda i: (i, 0)), whole((4, D, share))]
        + [cut((TILE, share), lambda i: (w * tiles + i, 0))] * 4
        + [whole((1, D))],
        out_specs=[
            cut((TILE, 2 * share), lambda i: (i, 0)),
            cut((TILE, 2 * share), lambda i: (i, 0)),
            cut((TILE, 1), lambda i: (i, 0)),
            pl.BlockSpec((1, D), lambda i: (0, 0)),
        ],
        out_shape=[
            jax.ShapeDtypeStruct((SEQ, 2 * share), BF),
            jax.ShapeDtypeStruct((SEQ, 2 * share), BF),
            jax.ShapeDtypeStruct((SEQ, 1), F32),
            jax.ShapeDtypeStruct((1, D), F32),
        ],
        compiler_params=params(32),
        cost_estimate=pl.CostEstimate(
            flops=6 * SEQ * D * share, bytes_accessed=8 * MIB, transcendentals=0
        ),
    )(dqkv, weights, *pieces, gain)


def adam_step(summed, master, first_old, second, average, step_rate, weight_decay):
    new_first = BETA_ONE * first_old + (1.0 - BETA_ONE) * summed
    new_second = BETA_TWO * second + (1.0 - BETA_TWO) * summed * summed
    update = (
        new_first
        / (1.0 - BETA_ONE**STEP)
        / (jnp.sqrt(new_second / (1.0 - BETA_TWO**STEP)) + ADAM_EPS)
    )
    new_master = master - step_rate * (update + weight_decay * master)
    new_average = EMA_RATE * average + (1.0 - EMA_RATE) * new_master
    return (summed, new_master, new_first, new_second, new_average, new_master.astype(BF))


def scatter_mp(send, keep):
    share = keep.shape[1] // 2
    near = swap(send, "mp", 1)
    half = keep.astype(F32) + near.astype(F32)
    far = swap(half[:, share:].astype(BF), "mp", 2)
    return half[:, :share] + far.astype(F32)


def local(
    tokens,
    cotangent,
    mask_rows,
    genome,
    group_tokens,
    owner,
    qkv_master,
    qkv_first,
    qkv_second,
    qkv_average,
    proj_master,
    proj_first,
    proj_second,
    proj_average,
    gate_up_master,
    gate_up_first,
    gate_up_second,
    gate_up_average,
    down_master,
    down_first,
    down_second,
    down_average,
    gains_master,
    gains_first,
    gains_second,
    gains_average,
    short=None,
):
    ndp = lax.axis_size("dp")
    me = lax.axis_index("dp")
    m = lax.axis_index("mp")
    share = tokens.shape[1]
    block = qkv_master.shape[1]
    windows, masked = mask_rows.shape
    rows = -(-masked // 32) * 32
    if short is None:
        short = ndp == 8 and block == LANES

    def start(b):
        at = b * block
        return ((at // share) ^ m) * share + at % share

    device = jnp.arange(ndp, dtype=jnp.int32)
    owner_x = jnp.sum(
        jnp.where((device[:, None] ^ me) == device[None, :], owner[None, :], 0), axis=1
    )
    pos = start(owner)
    pos_x = start(owner_x)

    attn_block = jnp.concatenate(
        [qkv_master.astype(BF), proj_master.T.astype(BF)[None]], axis=0
    )
    ffn_block = jnp.concatenate(
        [gate_up_master.astype(BF), down_master.T.astype(BF)[None]], axis=0
    )
    ffn_stack = lax.all_gather(ffn_block, "dp", axis=0, tiled=False)
    far = swap(tokens, "mp", 2)
    near = swap(tokens, "mp", 1)
    if short:
        z_pieces = [attn_block] + [swap(attn_block, "dp", bit) for bit in (2, 4, 6)]
        x_pieces = [swap(piece, "dp", 1) for piece in z_pieces]
        order = [None] * 8
        for k in range(4):
            order[2 * k], order[2 * k + 1] = z_pieces[k], x_pieces[k]
        attn_w = place_pieces(pos_x, order)
    else:
        attn_w = place_stack(pos, lax.all_gather(attn_block, "dp", axis=0, tiled=False))
    gains_x = gains_master.astype(BF)[:, None, :]
    bit = 1
    while bit < ndp:
        gains_x = jnp.concatenate([gains_x, swap(gains_x, "dp", bit)], axis=1)
        bit *= 2
    slot = (device * block)[:, None] == pos_x[None, :]
    gains = jnp.sum(
        jnp.where(slot[None, :, :, None], gains_x.astype(F32)[:, None], 0.0), axis=2
    ).reshape(2, 1, D)

    tokens_p = [tokens, near, far, swap(far, "mp", 1)]
    padded = jnp.pad(mask_rows, ((0, 0), (0, rows - masked)), constant_values=-1)
    onehot = (
        padded[:, :, None] == lax.broadcasted_iota(jnp.int32, (1, 1, SEQ), 2)
    ).astype(BF)
    cos, sin = rotary_tables(jnp.arange(SEQ))
    cosm, sinm = rotary_tables(padded.reshape(-1))
    qkv, norm_one, token_rows, q_rows, context, context_rows = [], [], [], [], [], []
    for w in range(windows):
        a, b, c, d = qkv_call(tokens_p, w, gains[0], attn_w, cos, sin, onehot[w])
        qkv.append(a)
        norm_one.append(b)
        token_rows.append(c)
        q_rows.append(d)
    for w in range(windows):
        a, b = attend_call(qkv[w], onehot[w])
        context.append(a)
        context_rows.append(b)
    wo_p = gather_mp(attn_w[3])
    context_p = [gather_mp(c) for c in context]
    context_rows = jnp.concatenate(context_rows, axis=0)
    context_rows_p = gather_mp(context_rows)
    token_rows = jnp.concatenate(token_rows, axis=0)

    cot = jnp.pad(cotangent.reshape(windows, masked, share), ((0, 0), (0, rows - masked), (0, 0)))
    cot = jnp.concatenate(gather_mp(cot.reshape(windows * rows, share)), axis=1)
    counts = group_tokens.astype(F32)
    picked = jnp.sum(
        jnp.where(
            genome[:, None] == jnp.arange(NGROUP, dtype=jnp.int32)[None, :], counts[None, :], 0.0
        ),
        axis=1,
    )
    window_scale = NGROUP * picked / jnp.sum(counts)
    seed = jnp.repeat(window_scale, rows)[:, None] * cot.astype(F32)
    seed_low = seed.astype(BF)

    ffn_w = place_stack(pos, ffn_stack)
    norm_rows, hidden_rows, gate_grad, up_grad, n2_send, n2_keep, unit, scale_rows = rows_call(
        token_rows, context_rows_p, wo_p, gains[1], seed_low, ffn_w
    )

    def reduce_blocks(lhs, rhs, after=None):
        if short:
            send = pack_send(pos_x[1::2], lhs, rhs)
            if after is not None:
                send, _ = lax.optimization_barrier((send, after))
            received = swap(send, "dp", 1)
            terms = pack_keep(pos_x[0::2], lhs, rhs, received)
            total = terms[0]
            for k in range(1, 4):
                total = total + swap(terms[k], "dp", 2 * k).astype(F32)
            return total, received
        grad = dot_l(lhs, rhs).reshape(ndp, block, rhs.shape[1])
        grad = jnp.take(grad, pos // block, axis=0, mode="clip")
        summed = lax.psum_scatter(grad, "dp", scatter_dimension=0, tiled=True)
        return summed[0], None

    down_sum, after = reduce_blocks(seed_low, hidden_rows)
    gate_sum, after = reduce_blocks(norm_rows, gate_grad, after)
    up_sum, after = reduce_blocks(norm_rows, up_grad, after)

    n2_half = n2_keep.astype(F32) + swap(n2_send, "mp", 1).astype(F32)
    n2_far = swap(n2_half.astype(BF), "mp", 2).astype(F32)
    n2_own = n2_half + jnp.concatenate([n2_far[:, share:], n2_far[:, :share]], axis=1)
    n2_near = swap(n2_own.astype(BF), "mp", 1).astype(F32)
    n2_grad = jnp.concatenate(
        [n2_own[:, :share], n2_near[:, :share], n2_own[:, share:], n2_near[:, share:]], axis=1
    )
    gain_two = jnp.sum(n2_grad * unit, axis=0)
    scaled = n2_grad * gains[1]
    residual_grad = seed + scale_rows[:, :1] * (
        scaled - unit * jnp.mean(scaled * unit, axis=1, keepdims=True)
    )
    attn_seed = residual_grad.astype(BF)
    context_grad = dot(attn_seed, attn_w[3]).astype(BF)

    dqkv = [
        back_call(q_rows[w], context_grad, w, qkv[w], onehot[w], cosm, sinm, cos, sin)
        for w in range(windows)
    ]
    dqkv_all = jnp.concatenate(dqkv, axis=0)
    norm_all = jnp.concatenate(norm_one, axis=0)
    proj_sum, after = reduce_blocks(attn_seed, context_rows, after)
    qkv_sum, after = reduce_blocks(norm_all, dqkv_all, after)

    outputs = []
    for w in range(windows):
        send, keep, residual = ffn_call(
            tokens_p, w, [piece for piece in context_p[w]], wo_p, gains[1], ffn_w
        )
        outputs.append((residual + scatter_mp(send, keep)).astype(BF))
    output = jnp.concatenate(outputs, axis=0)

    own_gain = gains[0][:, :share]
    high = attn_seed[:, :share]
    low = (residual_grad[:, :share] - high.astype(F32)).astype(BF)
    gain_one = None
    inputs = []
    for w in range(windows):
        send, keep, row_dot, col = first_grad_call(dqkv[w], attn_w, tokens_p, w, gains[0])
        gain_one = col if gain_one is None else gain_one + col
        n1_own = scatter_mp(send, keep)
        row_dot = row_dot[:, 0]
        row_dot = row_dot + swap(row_dot, "mp", 1)
        row_dot = row_dot + swap(row_dot, "mp", 2)
        x_own = lax.slice_in_dim(tokens, w * SEQ, (w + 1) * SEQ, axis=0).astype(F32)
        sq = jnp.zeros((SEQ,), F32)
        for piece in tokens_p:
            part = lax.slice_in_dim(piece, w * SEQ, (w + 1) * SEQ, axis=0).astype(F32)
            sq = sq + jnp.sum(part * part, axis=1)
        scale = lax.rsqrt(sq / D + EPS)[:, None]
        part = slice(w * rows, (w + 1) * rows)
        back = dot_l(onehot[w], jnp.concatenate([high[part], low[part]], axis=1))
        back = back[:, :share] + back[:, share:]
        inputs.append(
            (back + scale * (n1_own * own_gain - x_own * scale * (row_dot[:, None] / D))).astype(BF)
        )
    input_grad = jnp.concatenate(inputs, axis=0)

    gain_two = gain_two * (1.0 / lax.axis_size("mp"))
    gains_part = jnp.stack([gain_one[0], gain_two]).reshape(2, 4, share)
    chunk = jnp.arange(4, dtype=jnp.int32)
    natural = jnp.sum(
        jnp.where(
            ((chunk[:, None] ^ m) == chunk[None, :])[None, :, :, None], gains_part[:, None], 0.0
        ),
        axis=2,
    ).reshape(2, ndp, block)
    for axis in ("mp", "dp"):
        bit = 1
        while bit < lax.axis_size(axis):
            natural = natural + swap(natural, axis, bit)
            bit *= 2
    own_block = jnp.sum(jnp.where(device == me, owner, 0))
    gains_sum = jnp.sum(jnp.where((device == own_block)[None, :, None], natural, 0.0), axis=1)

    qkv_sum = jnp.moveaxis(qkv_sum.reshape(block, 3, share), 1, 0)
    gate_up_sum = jnp.stack([gate_sum, up_sum])
    qkv_out = adam_step(
        qkv_sum, qkv_master, qkv_first, qkv_second, qkv_average, D ** (-0.5), DECAY_RATE
    )
    proj_out = adam_step(
        proj_sum.T,
        proj_master,
        proj_first,
        proj_second,
        proj_average,
        (3.0 * D / SEQ) ** (-0.5),
        DECAY_RATE,
    )
    gate_up_out = adam_step(
        gate_up_sum,
        gate_up_master,
        gate_up_first,
        gate_up_second,
        gate_up_average,
        D ** (-0.5),
        DECAY_RATE,
    )
    down_out = adam_step(
        down_sum.T, down_master, down_first, down_second, down_average, FF ** (-0.5), DECAY_RATE
    )
    gains_out = adam_step(
        gains_sum, gains_master, gains_first, gains_second, gains_average, GAIN_RATE, 0.0
    )
    return (output, input_grad, *qkv_out, *proj_out, *gate_up_out, *down_out, *gains_out)


def solution(mesh, short=None):
    tokens = P("dp", "mp")
    cols = P(None, "dp", "mp")
    lines = P("mp", "dp")
    gains = P(None, "dp")
    in_specs = (tokens, tokens, P("dp", None), P("dp"), P(), P())
    in_specs += (cols,) * 4 + (lines,) * 4 + (cols,) * 4 + (lines,) * 4 + (gains,) * 4
    out_specs = (tokens, tokens)
    out_specs += (cols,) * 6 + (lines,) * 6 + (cols,) * 6 + (lines,) * 6 + (gains,) * 6
    return jax.shard_map(
        functools.partial(local, short=short),
        mesh=mesh,
        in_specs=in_specs,
        out_specs=out_specs,
        check_vma=False,
    )
```

```python
import functools

import jax
import jax.numpy as jnp
from jax import lax
from jax.experimental import pallas as pl
from jax.experimental.pallas import tpu as pltpu
from jax.sharding import PartitionSpec as P

D = 1024
FF = 4096
HEAD_DIM = 64
SEQ = 1024
NGROUP = 16
STEP = 7

EPS = 1e-05
THETA = 10000.0
BETA_ONE = 0.5
BETA_TWO = 0.5
ADAM_EPS = 1e-08
DECAY_RATE = 0.1
EMA_RATE = 0.6
GAIN_RATE = 0.4

BF = jnp.bfloat16
F32 = jnp.float32
LANES = 128
TILE = 256
TALL = 512
MIB = 1024 * 1024
SOFT = 1.4426950408889634 * HEAD_DIM**-0.5


def dot(a, b):
    return lax.dot_general(a, b, (((1,), (0,)), ((), ())), preferred_element_type=F32)


def dot_t(a, b):
    return lax.dot_general(a, b, (((1,), (1,)), ((), ())), preferred_element_type=F32)


def dot_l(a, b):
    return lax.dot_general(a, b, (((0,), (0,)), ((), ())), preferred_element_type=F32)


def params(mib, dims=None):
    return pltpu.CompilerParams(vmem_limit_bytes=mib * MIB, dimension_semantics=dims)


def swap(x, axis, bit):
    n = lax.axis_size(axis)
    return lax.ppermute(x, axis, [(i, i ^ bit) for i in range(n)])


def gather_mp(x):
    far = swap(x, "mp", 2)
    near = swap(x, "mp", 1)
    return [x, near, far, swap(far, "mp", 1)]


def whole(shape):
    return pl.BlockSpec(shape, lambda *_: (0,) * len(shape), pipeline_mode=pl.Buffered(1))


def cut(block, where):
    return pl.BlockSpec(block, where)


def rotary_tables(positions):
    half_dim = HEAD_DIM // 2
    frequency = THETA ** (-jnp.arange(half_dim, dtype=F32) / half_dim)
    angles = positions.astype(F32)[:, None] * frequency[None, :]
    cosine, sine = jnp.cos(angles), jnp.sin(angles)
    return (
        jnp.concatenate([cosine] * 4, axis=1),
        jnp.concatenate([-sine, sine, -sine, sine], axis=1),
    )


def turn(x, cos, sin, sign):
    lane = lax.broadcasted_iota(jnp.int32, (x.shape[0], LANES), 1)
    low = (lane % HEAD_DIM) < HEAD_DIM // 2
    parts = []
    for start in range(0, x.shape[1], LANES):
        v = x[:, start : start + LANES]
        other = jnp.where(
            low, pltpu.roll(v, LANES - HEAD_DIM // 2, 1), pltpu.roll(v, HEAD_DIM // 2, 1)
        )
        parts.append(v * cos + (sign * sin) * other)
    return jnp.concatenate(parts, axis=1)


def place_kernel(pos_ref, *refs):
    out, gains = refs[-2:]
    for p, piece in enumerate(refs[:-2]):
        bs = out.shape[1] // (len(refs) - 2)
        at = pl.multiple_of(pos_ref[p], bs)
        for k in range(4):
            out[k, pl.ds(at, bs), :] = piece[k * bs : (k + 1) * bs, :]
        gains[:, pl.ds(at, bs)] = piece[4 * bs : 4 * bs + 16, :bs].astype(F32)[:2, :]


def place_pieces(pos, pieces, bs):
    rows, n = pieces[0].shape
    total = bs * len(pieces)
    return pl.pallas_call(
        place_kernel,
        name="place_attention",
        grid_spec=pltpu.PrefetchScalarGridSpec(
            num_scalar_prefetch=1,
            grid=(1,),
            in_specs=[pl.BlockSpec((rows, n), lambda i, pos: (0, 0))] * len(pieces),
            out_specs=[
                pl.BlockSpec((4, total, n), lambda i, pos: (0, 0, 0)),
                pl.BlockSpec((2, total), lambda i, pos: (0, 0)),
            ],
        ),
        out_shape=[
            jax.ShapeDtypeStruct((4, total, n), BF),
            jax.ShapeDtypeStruct((2, total), F32),
        ],
        compiler_params=params(24),
    )(pos, *pieces)


def flip_kernel(in_ref, out_ref):
    out_ref[0] = in_ref[0].T


def flip(stack):
    k, a, b = stack.shape
    return pl.pallas_call(
        flip_kernel,
        name="flip",
        grid=(k,),
        in_specs=[cut((1, a, b), lambda i: (i, 0, 0))],
        out_specs=cut((1, b, a), lambda i: (i, 0, 0)),
        out_shape=jax.ShapeDtypeStruct((k, b, a), stack.dtype),
        compiler_params=params(16),
    )(stack)


def place_ffn_kernel(pos_ref, in_ref, wide_ref, down_ref):
    wide_ref[...] = in_ref[0, :2]
    down_ref[...] = in_ref[0, 2].T


def place_ffn(pos, stack):
    count, k, bs, n = stack.shape
    return pl.pallas_call(
        place_ffn_kernel,
        name="place_feed_forward",
        grid_spec=pltpu.PrefetchScalarGridSpec(
            num_scalar_prefetch=1,
            grid=(count,),
            in_specs=[pl.BlockSpec((1, k, bs, n), lambda j, pos: (j, 0, 0, 0))],
            out_specs=[
                pl.BlockSpec((2, bs, n), lambda j, pos: (0, pos[j] // bs, 0)),
                pl.BlockSpec((n, bs), lambda j, pos: (0, pos[j] // bs)),
            ],
        ),
        out_shape=[
            jax.ShapeDtypeStruct((2, count * bs, n), stack.dtype),
            jax.ShapeDtypeStruct((n, count * bs), stack.dtype),
        ],
        compiler_params=params(16),
    )(pos, stack)


def place_stack_kernel(pos_ref, in_ref, out_ref):
    out_ref[0] = in_ref[0, 0]


def place_stack(pos, stack):
    count, k, bs, n = stack.shape
    return pl.pallas_call(
        place_stack_kernel,
        name="place_stack",
        grid_spec=pltpu.PrefetchScalarGridSpec(
            num_scalar_prefetch=1,
            grid=(count, k),
            in_specs=[pl.BlockSpec((1, 1, bs, n), lambda j, w, pos: (j, w, 0, 0))],
            out_specs=pl.BlockSpec((1, bs, n), lambda j, w, pos: (w, pos[j] // bs, 0)),
        ),
        out_shape=jax.ShapeDtypeStruct((k, count * bs, n), stack.dtype),
        compiler_params=params(16),
    )(pos, stack)


def qkv_kernel(x0, x1, x2, x3, g_ref, w_ref, cos_ref, sin_ref, oh_ref,
               qkv_ref, norm_ref, scale_ref, trow_ref, qrow_ref, tacc, qacc):
    step = pl.program_id(1)
    x = jnp.concatenate([x0[...], x1[...], x2[...], x3[...]], axis=1)
    xf = x.astype(F32)
    scale = lax.rsqrt(jnp.mean(xf * xf, axis=1, keepdims=True) + EPS)
    scale_ref[...] = scale
    norm = (xf * scale * g_ref[...]).astype(BF)
    norm_ref[...] = norm
    cos, sin = cos_ref[...], sin_ref[...]
    q = turn(dot(norm, w_ref[0]), cos, sin, 1.0).astype(BF)
    qkv_ref[0] = q
    qkv_ref[1] = turn(dot(norm, w_ref[1]), cos, sin, 1.0).astype(BF)
    qkv_ref[2] = dot(norm, w_ref[2]).astype(BF)
    oh = oh_ref[0]

    @pl.when(step == 0)
    def _():
        tacc[...] = jnp.zeros_like(tacc)
        qacc[...] = jnp.zeros_like(qacc)

    tacc[...] += dot(oh, x)
    qacc[...] += dot(oh, q)

    @pl.when(step == pl.num_programs(1) - 1)
    def _():
        trow_ref[...] = tacc[...].astype(BF)
        qrow_ref[...] = qacc[...].astype(BF)


def qkv_call(pieces, gain, weights, cos, sin, onehot):
    count, share = pieces[0].shape
    windows, rows, _ = onehot.shape
    tiles = SEQ // TALL
    tile = lambda w, i: (w * tiles + i, 0)
    return pl.pallas_call(
        qkv_kernel,
        name="qkv",
        grid=(windows, tiles),
        in_specs=[cut((TALL, share), tile)] * 4
        + [
            whole((1, D)),
            whole((4, D, share)),
            cut((TALL, LANES), lambda w, i: (i, 0)),
            cut((TALL, LANES), lambda w, i: (i, 0)),
            cut((1, rows, TALL), lambda w, i: (w, 0, i)),
        ],
        out_specs=[
            cut((3, TALL, share), lambda w, i: (0, w * tiles + i, 0)),
            cut((TALL, D), tile),
            cut((TALL, 1), tile),
            cut((rows, D), lambda w, i: (w, 0)),
            cut((rows, share), lambda w, i: (w, 0)),
        ],
        out_shape=[
            jax.ShapeDtypeStruct((3, count, share), BF),
            jax.ShapeDtypeStruct((count, D), BF),
            jax.ShapeDtypeStruct((count, 1), F32),
            jax.ShapeDtypeStruct((windows * rows, D), BF),
            jax.ShapeDtypeStruct((windows * rows, share), BF),
        ],
        scratch_shapes=[pltpu.VMEM((rows, D), F32), pltpu.VMEM((rows, share), F32)],
        compiler_params=params(32),
        cost_estimate=pl.CostEstimate(
            flops=1000, bytes_accessed=1000, transcendentals=0
        ),
    )(*pieces, gain, weights, cos, sin, onehot)


def attend_kernel(q_ref, k_ref, v_ref, oh_ref, ctx_ref, crow_ref, acc, turned):
    step = pl.program_id(1)
    lane = lax.broadcasted_iota(jnp.int32, (TILE, LANES), 1)
    first = lane < HEAD_DIM
    ones = jnp.ones((SEQ, LANES), BF)

    @pl.when(step == 0)
    def _():
        acc[...] = jnp.zeros_like(acc)
        turned[...] = k_ref[0].T

    parts = []
    for start in range(0, q_ref.shape[2], LANES):
        q = q_ref[0, :, start : start + LANES]
        k = turned[start : start + LANES, :]
        v = jnp.concatenate([v_ref[0, :, start : start + LANES], ones], axis=1)
        heads = []
        for mine in (first, jnp.logical_not(first)):
            scores = dot(jnp.where(mine, q, jnp.zeros_like(q)), k)
            top = jnp.max(scores, axis=1, keepdims=True)
            weight = jnp.exp2((scores - top) * SOFT).astype(BF)
            mixed = dot(weight, v)
            heads.append(mixed[:, :LANES] / mixed[:, LANES:])
        parts.append(jnp.where(first, heads[0], heads[1]))
    context = jnp.concatenate(parts, axis=1).astype(BF)
    ctx_ref[...] = context
    acc[...] += dot(oh_ref[0], context)

    @pl.when(step == pl.num_programs(1) - 1)
    def _():
        crow_ref[...] = acc[...].astype(BF)


def attend_call(qkv, onehot):
    count, share = qkv.shape[1:]
    windows, rows, _ = onehot.shape
    tiles = SEQ // TILE
    return pl.pallas_call(
        attend_kernel,
        name="attend",
        grid=(windows, tiles),
        in_specs=[
            cut((1, TILE, share), lambda w, i: (0, w * tiles + i, 0)),
            cut((1, SEQ, share), lambda w, i: (1, w, 0)),
            cut((1, SEQ, share), lambda w, i: (2, w, 0)),
            cut((1, rows, TILE), lambda w, i: (w, 0, i)),
        ],
        out_specs=[
            cut((TILE, share), lambda w, i: (w * tiles + i, 0)),
            cut((rows, share), lambda w, i: (w, 0)),
        ],
        out_shape=[
            jax.ShapeDtypeStruct((count, share), BF),
            jax.ShapeDtypeStruct((windows * rows, share), BF),
        ],
        scratch_shapes=[pltpu.VMEM((rows, share), F32), pltpu.VMEM((share, SEQ), BF)],
        compiler_params=params(32),
        cost_estimate=pl.CostEstimate(
            flops=1000, bytes_accessed=1000, transcendentals=0
        ),
    )(qkv, qkv, qkv, onehot)


def split_chunks(value, send_ref, keep_ref, far_ref):
    share = keep_ref.shape[1]
    out = value.astype(BF)
    send_ref[:, :share] = out[:, share : 2 * share]
    send_ref[:, share:] = out[:, 3 * share :]
    keep_ref[...] = out[:, :share]
    far_ref[...] = out[:, 2 * share : 3 * share]


def join_wo(out, pieces):
    share = pieces[0].shape[0]
    for r, piece in enumerate(pieces):
        for c in range(4):
            out[r * share : (r + 1) * share, c * share : (c + 1) * share] = piece[
                :, (c ^ r) * share : ((c ^ r) + 1) * share
            ]


def rows_first_kernel(t_ref, c0, c1, c2, c3, o0, o1, o2, o3, g_ref, norm_ref, unit_ref, scale_ref, wo):
    join_wo(wo, (o0, o1, o2, o3))
    context = jnp.concatenate([c0[...], c1[...], c2[...], c3[...]], axis=1)
    residual = t_ref[...].astype(F32) + dot(context, wo[...])
    scale = lax.rsqrt(jnp.mean(residual * residual, axis=1, keepdims=True) + EPS)
    unit = residual * scale
    unit_ref[...] = unit
    scale_ref[...] = jnp.broadcast_to(scale, scale_ref.shape)
    norm_ref[...] = (unit * g_ref[...]).astype(BF)


def rows_first_call(token_rows, contexts, wo, gain):
    rows = token_rows.shape[0]
    fixed = lambda shape: pl.BlockSpec(shape, lambda i: (0,) * len(shape))
    args = (token_rows, *contexts, *wo, gain)
    return pl.pallas_call(
        rows_first_kernel,
        name="rows_first",
        grid=(1,),
        in_specs=[fixed(a.shape) for a in args],
        out_specs=[fixed((rows, D)), fixed((rows, D)), fixed((rows, LANES))],
        out_shape=[
            jax.ShapeDtypeStruct((rows, D), BF),
            jax.ShapeDtypeStruct((rows, D), F32),
            jax.ShapeDtypeStruct((rows, LANES), F32),
        ],
        scratch_shapes=[pltpu.VMEM((D, D), BF)],
        compiler_params=params(24),
        cost_estimate=pl.CostEstimate(
            flops=1000, bytes_accessed=1000, transcendentals=0
        ),
    )(*args)


def ffn_kernel(x0, x1, x2, x3, c0, c1, c2, c3, o0, o1, o2, o3, g_ref, w_ref, d_ref,
               send_ref, keep_ref, far_ref, res_ref, wo):
    share = x0.shape[1]

    @pl.when(pl.program_id(0) == 0)
    def _():
        join_wo(wo, (o0, o1, o2, o3))

    x = jnp.concatenate([x0[...], x1[...], x2[...], x3[...]], axis=1).astype(F32)
    context = jnp.concatenate([c0[...], c1[...], c2[...], c3[...]], axis=1)
    residual = x + dot(context, wo[...])
    scale = lax.rsqrt(jnp.mean(residual * residual, axis=1, keepdims=True) + EPS)
    norm = (residual * scale * g_ref[...]).astype(BF)
    res_ref[...] = residual[:, :share]
    total = None
    width = w_ref.shape[2]
    for start in range(0, width, TILE):
        gate = dot(norm, w_ref[0, :, start : start + TILE])
        up = dot(norm, w_ref[1, :, start : start + TILE])
        hidden = (gate * jax.nn.sigmoid(gate) * up).astype(BF)
        term = dot(hidden, d_ref[start : start + TILE, :])
        total = term if total is None else total + term
    split_chunks(total, send_ref, keep_ref, far_ref)


def ffn_call(pieces, contexts, wo, gain, weights, down):
    count, share = pieces[0].shape
    width = weights.shape[2]
    tile = lambda i: (i, 0)
    return pl.pallas_call(
        ffn_kernel,
        name="feed_forward",
        grid=(count // TALL,),
        in_specs=[cut((TALL, share), tile)] * 8
        + [whole((share, D))] * 4
        + [whole((1, D)), whole((2, D, width)), whole((width, D))],
        out_specs=[
            cut((TALL, 2 * share), tile),
            cut((TALL, share), tile),
            cut((TALL, share), tile),
            cut((TALL, share), tile),
        ],
        out_shape=[
            jax.ShapeDtypeStruct((count, 2 * share), BF),
            jax.ShapeDtypeStruct((count, share), BF),
            jax.ShapeDtypeStruct((count, share), BF),
            jax.ShapeDtypeStruct((count, share), F32),
        ],
        scratch_shapes=[pltpu.VMEM((D, D), BF)],
        compiler_params=params(48),
        cost_estimate=pl.CostEstimate(
            flops=1000, bytes_accessed=1000, transcendentals=0
        ),
    )(*pieces, *contexts, *wo, gain, weights, down)


def rows_kernel(n_ref, seed_ref, w_ref, d_ref,
                hid_ref, gg_ref, ug_ref, send_ref, keep_ref, far_ref, acc):
    step = pl.program_id(0)

    @pl.when(step == 0)
    def _():
        acc[...] = jnp.zeros_like(acc)

    norm = n_ref[...]
    gate = dot(norm, w_ref[0])
    up = dot(norm, w_ref[1])
    sigmoid = jax.nn.sigmoid(gate)
    silu = gate * sigmoid
    hid_ref[...] = (silu * up).astype(BF)
    hidden_grad = dot_t(seed_ref[...], d_ref[...])
    gate_grad = (hidden_grad * up * sigmoid * (1.0 + gate * (1.0 - sigmoid))).astype(BF)
    up_grad = (hidden_grad * silu).astype(BF)
    gg_ref[...] = gate_grad
    ug_ref[...] = up_grad
    acc[...] += dot_t(gate_grad, w_ref[0]) + dot_t(up_grad, w_ref[1])

    @pl.when(step == pl.num_programs(0) - 1)
    def _():
        split_chunks(acc[...], send_ref, keep_ref, far_ref)


def rows_call(norm_rows, seed, weights, down):
    rows = norm_rows.shape[0]
    width = weights.shape[2]
    share = D // 4
    part = 256
    fixed = lambda shape: pl.BlockSpec(shape, lambda i: (0,) * len(shape))
    return pl.pallas_call(
        rows_kernel,
        name="masked_rows",
        grid=(width // part,),
        in_specs=[whole((rows, D)), whole((rows, D))]
        + [cut((2, D, part), lambda i: (0, 0, i)), cut((part, D), lambda i: (i, 0))],
        out_specs=[
            cut((rows, part), lambda i: (0, i)),
            cut((rows, part), lambda i: (0, i)),
            cut((rows, part), lambda i: (0, i)),
            fixed((rows, 2 * share)),
            fixed((rows, share)),
            fixed((rows, share)),
        ],
        out_shape=[
            jax.ShapeDtypeStruct((rows, width), BF),
            jax.ShapeDtypeStruct((rows, width), BF),
            jax.ShapeDtypeStruct((rows, width), BF),
            jax.ShapeDtypeStruct((rows, 2 * share), BF),
            jax.ShapeDtypeStruct((rows, share), BF),
            jax.ShapeDtypeStruct((rows, share), BF),
        ],
        scratch_shapes=[pltpu.VMEM((rows, D), F32)],
        compiler_params=params(32),
        cost_estimate=pl.CostEstimate(
            flops=1000, bytes_accessed=1000, transcendentals=0
        ),
    )(norm_rows, seed, weights, down)


def seed_kernel(own_ref, near_ref, seed_ref, unit_ref, scale_ref, g_ref, w_ref,
                low_ref, own_seed_ref, ctx_ref, gain_ref):
    share = own_ref.shape[1] // 2
    own, near = own_ref[...], near_ref[...]
    grad = jnp.concatenate(
        [own[:, :share], near[:, :share], own[:, share:], near[:, share:]], axis=1
    ).astype(F32)
    unit = unit_ref[...].astype(F32)
    gain_ref[...] = jnp.sum(grad * unit, axis=0, keepdims=True)
    scaled = grad * g_ref[...]
    back = seed_ref[...] + scale_ref[:, :1] * (
        scaled - unit * jnp.mean(scaled * unit, axis=1, keepdims=True)
    )
    low = back.astype(BF)
    low_ref[...] = low
    high = low[:, :share]
    own_seed_ref[:, :share] = high
    own_seed_ref[:, share:] = (back[:, :share] - high.astype(F32)).astype(BF)
    ctx_ref[...] = dot(low, w_ref[0]).astype(BF)


def seed_call(own, near, seed, unit, scale, gain, weights):
    rows = own.shape[0]
    share = own.shape[1] // 2
    fixed = lambda shape: pl.BlockSpec(shape, lambda i: (0,) * len(shape))
    return pl.pallas_call(
        seed_kernel,
        name="seed_back",
        grid=(1,),
        in_specs=[fixed(a.shape) for a in (own, near, seed, unit, scale, gain)]
        + [pl.BlockSpec((1, D, share), lambda i: (3, 0, 0))],
        out_specs=[fixed((rows, D)), fixed((rows, 2 * share)), fixed((rows, share)), fixed((1, D))],
        out_shape=[
            jax.ShapeDtypeStruct((rows, D), BF),
            jax.ShapeDtypeStruct((rows, 2 * share), BF),
            jax.ShapeDtypeStruct((rows, share), BF),
            jax.ShapeDtypeStruct((1, D), F32),
        ],
        compiler_params=params(24),
        cost_estimate=pl.CostEstimate(
            flops=1000, bytes_accessed=1000, transcendentals=0
        ),
    )(own, near, seed, unit, scale, gain, weights)


def chosen(ref, pos_ref, blocks):
    return jnp.concatenate(
        [ref[:, pl.ds(pl.multiple_of(pos_ref[b], LANES), LANES)] for b in blocks], axis=1
    )


def pack_kernel(halves, rhs_count, pos_ref, lhs_ref, *refs):
    rhs, outs = refs[:rhs_count], refs[rhs_count:]
    size = 8 // halves
    for h, out in enumerate(outs):
        left = chosen(lhs_ref, pos_ref, range(h * size, (h + 1) * size))
        at = 0
        for right in rhs:
            for start in range(0, right.shape[1], 512):
                value = dot_l(left, right[:, start : start + 512]).astype(BF)
                for b in range(size):
                    out[b, :, at + start : at + start + 512] = value[b * LANES : (b + 1) * LANES]
            at += right.shape[1]


def pack(pos, lhs, rhs, halves, name):
    rows = lhs.shape[0]
    n = sum(r.shape[1] for r in rhs)
    size = 8 // halves
    zero = lambda i, pos: (0, 0)
    return pl.pallas_call(
        functools.partial(pack_kernel, halves, len(rhs)),
        name="pack_" + name,
        grid_spec=pltpu.PrefetchScalarGridSpec(
            num_scalar_prefetch=1,
            grid=(1,),
            in_specs=[pl.BlockSpec(a.shape, zero) for a in (lhs, *rhs)],
            out_specs=[pl.BlockSpec((size, LANES, n), lambda i, pos: (0, 0, 0))] * halves,
        ),
        out_shape=[jax.ShapeDtypeStruct((size, LANES, n), BF)] * halves,
        compiler_params=params(32),
        cost_estimate=pl.CostEstimate(
            flops=1000, bytes_accessed=1000, transcendentals=0
        ),
    )(pos, lhs, *rhs)


def pack_attention_kernel(pos_ref, norm_ref, d_ref, seed_ref, ctx_ref, gain_ref, send_ref, keep_ref, acc):
    step = pl.program_id(0)
    n = d_ref.shape[1]
    value = dot_l(chosen(norm_ref, pos_ref, range(8)), d_ref[...])

    @pl.when(step == 0)
    def _():
        acc[...] = value
        proj = dot_l(chosen(seed_ref, pos_ref, range(8)), ctx_ref[...]).astype(BF)
        for b in range(8):
            out = (send_ref, keep_ref)[b // 4]
            out[b % 4, :LANES, n:] = proj[b * LANES : (b + 1) * LANES]
            gain = gain_ref[:, pl.ds(pl.multiple_of(pos_ref[b], LANES), LANES)].astype(BF)
            out[b % 4, LANES:, :] = jnp.zeros((16, out.shape[2]), BF)
            out[b % 4, LANES:, :LANES] = jnp.broadcast_to(gain, (16, LANES))

    @pl.when(step > 0)
    def _():
        acc[...] += value

    @pl.when(step == pl.num_programs(0) - 1)
    def _():
        for b in range(8):
            out = (send_ref, keep_ref)[b // 4]
            out[b % 4, :LANES, :n] = acc[b * LANES : (b + 1) * LANES, :].astype(BF)


def pack_attention(pos, norm, dqkv, seed, context_rows, gain):
    count = norm.shape[0]
    rows, share = context_rows.shape
    n = dqkv.shape[1]
    tile = lambda i, pos: (i, 0)
    zero = lambda i, pos: (0, 0)
    return pl.pallas_call(
        pack_attention_kernel,
        name="pack_attention",
        grid_spec=pltpu.PrefetchScalarGridSpec(
            num_scalar_prefetch=1,
            grid=(count // TALL,),
            in_specs=[
                pl.BlockSpec((TALL, D), tile),
                pl.BlockSpec((TALL, n), tile),
                pl.BlockSpec((rows, D), zero),
                pl.BlockSpec((rows, share), zero),
                pl.BlockSpec((1, D), zero),
            ],
            out_specs=[pl.BlockSpec((4, LANES + 16, n + share), lambda i, pos: (0, 0, 0))] * 2,
            scratch_shapes=[pltpu.VMEM((D, n), F32)],
        ),
        out_shape=[jax.ShapeDtypeStruct((4, LANES + 16, n + share), BF)] * 2,
        compiler_params=params(32),
        cost_estimate=pl.CostEstimate(
            flops=1000, bytes_accessed=1000, transcendentals=0
        ),
    )(pos, norm, dqkv, seed, context_rows, gain)


def add_terms_kernel(keep_ref, recv_ref, *outs):
    for k, out in enumerate(outs):
        out[...] = (keep_ref[k].astype(F32) + recv_ref[k].astype(F32)).astype(out.dtype)


def add_terms(keep, received, name):
    count, rows, n = keep.shape
    block = pl.BlockSpec((count, rows, 512), lambda i: (0, 0, i))
    return pl.pallas_call(
        add_terms_kernel,
        name="add_" + name,
        grid=(n // 512,),
        in_specs=[block] * 2,
        out_specs=[pl.BlockSpec((rows, 512), lambda i: (0, i))] * count,
        out_shape=[jax.ShapeDtypeStruct((rows, n), F32 if k == 0 else BF) for k in range(count)],
        compiler_params=params(16),
    )(keep, received)


def back_kernel(q_ref, do_ref, a_ref, k_ref, v_ref, oh_ref, cosm_ref, sinm_ref, cos_ref, sin_ref,
                out_ref, dot_ref):
    rows, share = q_ref.shape
    lane = lax.broadcasted_iota(jnp.int32, (rows, LANES), 1)
    first = lane < HEAD_DIM
    scale = HEAD_DIM**-0.5
    dq_parts, dk_parts, dv_parts = [], [], []
    for start in range(0, share, LANES):
        q = q_ref[:, start : start + LANES]
        do = do_ref[:, start : start + LANES]
        k = k_ref[0, :, start : start + LANES]
        v = v_ref[0, :, start : start + LANES]
        dqs, dk, dv = [], None, None
        for mine in (first, jnp.logical_not(first)):
            qm = jnp.where(mine, q, jnp.zeros_like(q))
            dm = jnp.where(mine, do, jnp.zeros_like(do))
            scores = dot_t(qm, k)
            top = jnp.max(scores, axis=1, keepdims=True)
            weight = jnp.exp2((scores - top) * SOFT)
            prob = weight * (1.0 / jnp.sum(weight, axis=1, keepdims=True))
            prob_grad = dot_t(dm, v)
            delta = jnp.sum(prob * prob_grad, axis=1, keepdims=True)
            score_grad = (prob * (prob_grad - delta)).astype(BF)
            dqs.append(dot(score_grad, k))
            term = dot_l(score_grad, qm)
            dk = term if dk is None else dk + term
            term = dot_l(prob.astype(BF), dm)
            dv = term if dv is None else dv + term
        dq_parts.append(jnp.where(first, dqs[0], dqs[1]) * scale)
        dk_parts.append(dk * scale)
        dv_parts.append(dv)
    dq = jnp.concatenate(dq_parts, axis=1)
    dk = jnp.concatenate(dk_parts, axis=1)
    dv = jnp.concatenate(dv_parts, axis=1)
    both = jnp.concatenate(
        [turn(dq, cosm_ref[...], sinm_ref[...], -1.0).astype(BF), dq.astype(BF)], axis=1
    )
    both = dot_l(oh_ref[0], both)
    out_ref[:, :share] = both[:, :share].astype(BF)
    out_ref[:, share : 2 * share] = turn(dk, cos_ref[...], sin_ref[...], -1.0).astype(BF)
    out_ref[:, 2 * share :] = dv.astype(BF)
    terms = both[:, share:] * a_ref[0].astype(F32)
    terms = terms + dk * k_ref[0].astype(F32) + dv * v_ref[0].astype(F32)
    high = terms.astype(BF)
    low = (terms - high.astype(F32)).astype(BF)
    ones = jnp.ones((16, share), BF)
    dot_ref[...] = (dot_t(ones, high) + dot_t(ones, low))[:1]


def back_call(q_rows, context_grad, qkv, onehot, cosm, sinm, cos, sin):
    windows, rows, _ = onehot.shape
    count, share = qkv.shape[1:]
    mine = lambda w: (w, 0)
    fixed = lambda w: (0, 0)
    return pl.pallas_call(
        back_kernel,
        name="attend_back",
        grid=(windows,),
        in_specs=[
            cut((rows, share), mine),
            cut((rows, share), mine),
            cut((1, SEQ, share), lambda w: (0, w, 0)),
            cut((1, SEQ, share), lambda w: (1, w, 0)),
            cut((1, SEQ, share), lambda w: (2, w, 0)),
            cut((1, rows, SEQ), lambda w: (w, 0, 0)),
            cut((rows, LANES), mine),
            cut((rows, LANES), mine),
            cut((SEQ, LANES), fixed),
            cut((SEQ, LANES), fixed),
        ],
        out_specs=[cut((SEQ, 3 * share), mine), cut((1, SEQ), lambda w: (0, w))],
        out_shape=[
            jax.ShapeDtypeStruct((count, 3 * share), BF),
            jax.ShapeDtypeStruct((1, count), F32),
        ],
        compiler_params=params(40),
        cost_estimate=pl.CostEstimate(
            flops=1000, bytes_accessed=1000, transcendentals=0
        ),
    )(q_rows, context_grad, qkv, qkv, qkv, onehot, cosm, sinm, cos, sin)


def first_grad_kernel(d_ref, w_ref, send_ref, keep_ref, far_ref):
    share = keep_ref.shape[1]
    grad = None
    for t in range(3):
        term = dot(d_ref[:, t * share : (t + 1) * share], w_ref[t])
        grad = term if grad is None else grad + term
    split_chunks(grad, send_ref, keep_ref, far_ref)


def first_grad_call(dqkv, weights):
    count = dqkv.shape[0]
    share = dqkv.shape[1] // 3
    tile = lambda i: (i, 0)
    return pl.pallas_call(
        first_grad_kernel,
        name="first_grad",
        grid=(count // TALL,),
        in_specs=[cut((TALL, 3 * share), tile), whole((3, share, D))],
        out_specs=[
            cut((TALL, 2 * share), tile),
            cut((TALL, share), tile),
            cut((TALL, share), tile),
        ],
        out_shape=[
            jax.ShapeDtypeStruct((count, 2 * share), BF),
            jax.ShapeDtypeStruct((count, share), BF),
            jax.ShapeDtypeStruct((count, share), BF),
        ],
        compiler_params=params(32),
        cost_estimate=pl.CostEstimate(
            flops=1000, bytes_accessed=1000, transcendentals=0
        ),
    )(dqkv, weights)


def input_kernel(x_ref, s_ref, dot_ref, keep_ref, near_ref, far_ref, g_ref, oh_ref, hl_ref, out_ref):
    share = x_ref.shape[1]
    grad = keep_ref[...].astype(F32) + near_ref[...].astype(F32) + far_ref[...].astype(F32)
    scale = s_ref[...]
    column = jnp.broadcast_to(dot_ref[...], (8, dot_ref.shape[1])).T[:, :1]
    back = dot_l(oh_ref[0], hl_ref[0])
    unit = x_ref[...].astype(F32) * scale
    out = back[:, :share] + back[:, share:] + scale * (grad * g_ref[...] - unit * (column / D))
    out_ref[...] = out.astype(BF)


def input_call(tokens, scale, dots, keep, near, far, gain, onehot, seeds):
    count, share = tokens.shape
    windows, rows, _ = onehot.shape
    tiles = SEQ // TILE
    tile = lambda w, i: (w * tiles + i, 0)
    return pl.pallas_call(
        input_kernel,
        name="input_grad",
        grid=(windows, tiles),
        in_specs=[
            cut((TILE, share), tile),
            cut((TILE, 1), tile),
            cut((1, TILE), lambda w, i: (0, w * tiles + i)),
            cut((TILE, share), tile),
            cut((TILE, share), tile),
            cut((TILE, share), tile),
            cut((1, share), lambda w, i: (0, 0)),
            cut((1, rows, TILE), lambda w, i: (w, 0, i)),
            cut((1, rows, 2 * share), lambda w, i: (w, 0, 0)),
        ],
        out_specs=cut((TILE, share), tile),
        out_shape=jax.ShapeDtypeStruct((count, share), BF),
        compiler_params=params(24),
        cost_estimate=pl.CostEstimate(
            flops=1000, bytes_accessed=1000, transcendentals=0
        ),
    )(tokens, scale, dots, keep, near, far, gain, onehot, seeds)


def adam_step(summed, master, first_old, second, average, step_rate, weight_decay):
    new_first = BETA_ONE * first_old + (1.0 - BETA_ONE) * summed
    new_second = BETA_TWO * second + (1.0 - BETA_TWO) * summed * summed
    update = (
        new_first
        / (1.0 - BETA_ONE**STEP)
        / (jnp.sqrt(new_second / (1.0 - BETA_TWO**STEP)) + ADAM_EPS)
    )
    new_master = master - step_rate * (update + weight_decay * master)
    new_average = EMA_RATE * average + (1.0 - EMA_RATE) * new_master
    return (summed, new_master, new_first, new_second, new_average, new_master.astype(BF))


def adam_cols_kernel(sets, rate, *refs):
    terms, (m, f, s, a), outs = refs[:sets], refs[sets : sets + 4], refs[sets + 4 :]
    grad = sum((t[...].astype(F32) for t in terms[1:]), terms[0][...].astype(F32))
    values = adam_step(grad, m[0], f[0], s[0], a[0], rate, DECAY_RATE)
    for out, value in zip(outs[:6], values, strict=True):
        out[0] = value
    if len(outs) > 6:
        used = m[0].astype(BF).astype(F32)
        part = jnp.broadcast_to(jnp.sum(used * grad, axis=1, keepdims=True), outs[6].shape)

        @pl.when((pl.program_id(0) == 0) & (pl.program_id(1) == 0))
        def _():
            outs[6][...] = jnp.zeros_like(outs[6])

        outs[6][...] += part


def adam_cols(terms, arrays, rate, name, rows=False):
    k, bs, n = arrays[0].shape
    part = min(n, 512)
    tiles = n // part
    term = cut((bs, part), lambda t, j: (0, t * tiles + j))
    spot = cut((1, bs, part), lambda t, j: (t, 0, j))
    return pl.pallas_call(
        functools.partial(adam_cols_kernel, len(terms), rate),
        name="adam_" + name,
        grid=(k, tiles),
        in_specs=[term] * len(terms) + [spot] * 4,
        out_specs=[spot] * 6 + [cut((bs, LANES), lambda t, j: (0, 0))] * rows,
        out_shape=[jax.ShapeDtypeStruct((k, bs, n), BF if i == 5 else F32) for i in range(6)]
        + [jax.ShapeDtypeStruct((bs, LANES), F32)] * rows,
        compiler_params=params(24),
    )(*terms, *arrays)


def adam_rows_kernel(rate, *refs):
    terms, (m, f, s, a), outs = refs[:4], refs[4:8], refs[8:]
    grad = sum((t[...].astype(F32) for t in terms[1:]), terms[0][...]).T
    values = adam_step(grad, m[...], f[...], s[...], a[...], rate, DECAY_RATE)
    for out, value in zip(outs, values, strict=True):
        out[...] = value


def adam_rows(terms, offset, arrays, rate, name):
    n, bs = arrays[0].shape
    term = cut((bs, TILE), lambda i: (0, offset // TILE + i))
    spot = cut((TILE, bs), lambda i: (i, 0))
    return pl.pallas_call(
        functools.partial(adam_rows_kernel, rate),
        name="adam_" + name,
        grid=(n // TILE,),
        in_specs=[term] * 4 + [spot] * 4,
        out_specs=[spot] * 6,
        out_shape=[jax.ShapeDtypeStruct((n, bs), BF if i == 5 else F32) for i in range(6)],
        compiler_params=params(24),
    )(*terms, *arrays)


def at_once(*values):
    return lax.optimization_barrier(values)


def tie(x, *others):
    return lax.optimization_barrier((x, *others))[0]


def local(
    tokens,
    cotangent,
    mask_rows,
    genome,
    group_tokens,
    owner,
    qkv_master,
    qkv_first,
    qkv_second,
    qkv_average,
    proj_master,
    proj_first,
    proj_second,
    proj_average,
    gate_up_master,
    gate_up_first,
    gate_up_second,
    gate_up_average,
    down_master,
    down_first,
    down_second,
    down_average,
    gains_master,
    gains_first,
    gains_second,
    gains_average,
    short=None,
):
    ndp = lax.axis_size("dp")
    me = lax.axis_index("dp")
    m = lax.axis_index("mp")
    count, share = tokens.shape
    block = qkv_master.shape[1]
    windows, masked = mask_rows.shape
    rows = -(-masked // 32) * 32
    if short is None:
        short = ndp == 8 and block == LANES

    def start(b):
        at = b * block
        return ((at // share) ^ m) * share + at % share

    device = jnp.arange(ndp, dtype=jnp.int32)
    owner_x = jnp.sum(
        jnp.where((device[:, None] ^ me) == device[None, :], owner[None, :], 0), axis=1
    )
    pos = start(owner)
    pos_x = start(owner_x)

    attn_block = [qkv_master[0], qkv_master[1], qkv_master[2], proj_master.T]
    ffn_block = jnp.concatenate(
        [gate_up_master.astype(BF), down_master.T.astype(BF)[None]], axis=0
    )
    far = swap(tokens, "mp", 2)
    near = swap(tokens, "mp", 1)
    if short:
        extra = jnp.pad(gains_master, ((0, 14), (0, share - block)))
        message = jnp.concatenate(attn_block + [extra], axis=0).astype(BF)
        z_pieces = [message] + [swap(message, "dp", bit) for bit in (2, 4, 6)]
        x_pieces = [swap(piece, "dp", 1) for piece in z_pieces]
        order = [None] * 8
        for k in range(4):
            order[2 * k], order[2 * k + 1] = z_pieces[k], x_pieces[k]
        attn_w, gains = place_pieces(pos_x, order, block)
        gains = gains.reshape(2, 1, D)
    else:
        attn_block = jnp.stack(attn_block).astype(BF)
        attn_w = place_stack(pos, lax.all_gather(attn_block, "dp", axis=0, tiled=False))
        all_gains = lax.all_gather(gains_master.astype(BF), "dp", axis=1, tiled=False)
        slot = (device * block)[:, None] == pos[None, :]
        gains = jnp.sum(
            jnp.where(slot[None, :, :, None], all_gains.astype(F32)[:, None], 0.0), axis=2
        ).reshape(2, 1, D)
    ffn_stack = lax.all_gather(ffn_block, "dp", axis=0, tiled=False)

    tokens_p = [tokens, near, far, swap(far, "mp", 1)]
    padded = jnp.pad(mask_rows, ((0, 0), (0, rows - masked)), constant_values=-1)
    onehot = (
        padded[:, :, None] == lax.broadcasted_iota(jnp.int32, (1, 1, SEQ), 2)
    ).astype(BF)
    cos, sin = rotary_tables(jnp.arange(SEQ))
    cosm, sinm = rotary_tables(padded.reshape(-1))
    counts = group_tokens.astype(F32)
    picked = jnp.sum(
        jnp.where(
            genome[:, None] == jnp.arange(NGROUP, dtype=jnp.int32)[None, :], counts[None, :], 0.0
        ),
        axis=1,
    )
    window_scale = NGROUP * picked / jnp.sum(counts)
    attn_t = flip(attn_w)
    wo_far = swap(attn_t[3], "mp", 2)
    qkv, norm_one, scale_one, token_rows, q_rows = qkv_call(
        tokens_p, gains[0], tie(attn_w, attn_t), cos, sin, onehot
    )
    context, context_rows = attend_call(tie(qkv, wo_far), onehot)
    wo_p = [attn_t[3], swap(attn_t[3], "mp", 1), wo_far, swap(wo_far, "mp", 1)]
    cot = jnp.pad(cotangent.reshape(windows, masked, share), ((0, 0), (0, rows - masked), (0, 0)))
    both = jnp.concatenate([context_rows, cot.reshape(windows * rows, share)], axis=0)
    both_p = gather_mp(both)
    context_rows_p = [piece[: windows * rows] for piece in both_p]
    cot = jnp.concatenate([piece[windows * rows :] for piece in both_p], axis=1)
    context = tie(context, both_p[3])
    context_far = swap(context, "mp", 2)
    seed = jnp.repeat(window_scale, rows)[:, None] * cot.astype(F32)
    seed_low = seed.astype(BF)
    norm_rows, unit, scale_rows = rows_first_call(token_rows, context_rows_p, wo_p, gains[1])

    ffn_stack = tie(ffn_stack, norm_rows)
    if short:
        wide_w, down_w = place_ffn(pos, ffn_stack)
    else:
        wide_w = place_stack(pos, ffn_stack)
        wide_w, down_w = wide_w[:2], wide_w[2].T
    hidden_rows, gate_grad, up_grad, n2_send, n2_keep, n2_far = rows_call(
        norm_rows, seed_low, wide_w, down_w
    )

    context_near, context_far = at_once(context, context_far, n2_send)[:2]
    context_p = [context, swap(context_near, "mp", 1), context_far, swap(context_far, "mp", 1)]

    def reduce_all(lhs, rhs):
        grad = dot_l(lhs, rhs).reshape(ndp, block, rhs.shape[1])
        grad = jnp.take(grad, pos // block, axis=0, mode="clip")
        return lax.psum_scatter(grad, "dp", scatter_dimension=0, tiled=True)[0]

    n2_near = swap(n2_send, "mp", 1)
    if short:
        sides = jnp.concatenate([pos_x[1::2], pos_x[0::2]])
        (wide_blocks,) = pack(pos, norm_rows, [gate_grad, up_grad], 1, "wide")
        wide_sum = lax.psum_scatter(wide_blocks, "dp", scatter_dimension=0, tiled=False)
        n2_near, hidden_rows = at_once(n2_near, hidden_rows, wide_blocks)[:2]
    n2_near = n2_near.astype(F32)
    n2_half = jnp.concatenate(
        [n2_keep.astype(F32) + n2_near[:, :share], n2_far.astype(F32) + n2_near[:, share:]], axis=1
    ).astype(BF)
    n2_back = swap(n2_half, "mp", 2)
    if short:
        down_send, down_keep = pack(sides, seed_low, [hidden_rows], 2, "down")
        down_x = swap(down_send, "dp", 1)
        n2_back, context_p = at_once(n2_back, context_p, down_send)[:2]
    n2_back = n2_back.astype(F32)
    n2_own = (
        n2_half.astype(F32) + jnp.concatenate([n2_back[:, share:], n2_back[:, :share]], axis=1)
    ).astype(BF)
    attn_seed, own_seed, context_grad, gain_two = seed_call(
        n2_own, swap(n2_own, "mp", 1), seed, unit, scale_rows, gains[1], attn_w
    )
    own_seed = own_seed.reshape(windows, rows, 2 * share)

    dqkv, row_dot = back_call(q_rows, context_grad, qkv, onehot, cosm, sinm, cos, sin)
    n_send, n_keep, n_far = first_grad_call(dqkv, attn_t)
    row_dot = row_dot + swap(row_dot, "mp", 1)
    if short:
        down_added = add_terms(down_keep, down_x, "down")
        n_send, row_dot, down_added = at_once(n_send, row_dot, down_added)
    n_near = swap(n_send, "mp", 1)
    row_far = swap(row_dot, "mp", 2)
    if short:
        attn_send, attn_keep = pack_attention(
            sides, norm_one, tie(dqkv, n_send), attn_seed, context_rows, gain_two
        )
        n_near, row_far, attn_send, down_added = at_once(n_near, row_far, attn_send, down_added)
    row_dot = row_dot + row_far
    n_half = (n_far.astype(F32) + n_near[:, share:].astype(F32)).astype(BF)

    if short:
        n_half, attn_send, down_added, ffn_in = at_once(n_half, attn_send, down_added, context_p)
        attn_x = swap(attn_send, "dp", 1)
        down_terms = [down_added[0]] + [swap(down_added[k], "dp", 2 * k) for k in range(1, 4)]
        n_back = swap(n_half, "mp", 2)
        ffn_out = ffn_call(tokens_p, ffn_in, wo_p, gains[1], wide_w, down_w)
        ffn_out, attn_x, down_terms, n_back = at_once(ffn_out, attn_x, down_terms, n_back)
        attn_added = add_terms(attn_keep, attn_x, "attention")
    else:
        n_back = swap(n_half, "mp", 2)
        ffn_out = ffn_call(tokens_p, context_p, wo_p, gains[1], wide_w, down_w)
    f_send, f_keep, f_far, residual = ffn_out
    f_near = swap(f_send, "mp", 1)
    down_old = (down_master, down_first, down_second, down_average)
    down_rate = FF ** (-0.5)
    if short:
        down_out = adam_rows(down_terms, 0, down_old, down_rate, "down")
        f_near, attn_added, down_out = at_once(f_near, attn_added, down_out)
    f_half = (f_far.astype(F32) + f_near[:, share:].astype(F32)).astype(BF)
    f_part = residual + f_keep.astype(F32) + f_near[:, :share].astype(F32)
    if short:
        f_half, attn_added, f_part = at_once(f_half, attn_added, f_part)
    f_back = swap(f_half, "mp", 2)
    if short:
        attn_terms = [attn_added[0]] + [swap(attn_added[k], "dp", 2 * k) for k in range(1, 4)]
    input_grad = input_call(
        tokens,
        scale_one,
        row_dot,
        n_keep,
        n_near[:, :share],
        n_back,
        gains[0][:, :share],
        onehot,
        own_seed,
    )
    if short:
        gate_up_old = (gate_up_master, gate_up_first, gate_up_second, gate_up_average)
        gate_up_out = adam_cols([wide_sum], gate_up_old, D ** (-0.5), "gate_up")
        f_back, attn_terms, input_grad, gate_up_out = at_once(
            f_back, attn_terms, input_grad, gate_up_out
        )
    output = (f_part + f_back.astype(F32)).astype(BF)
    qkv_old = (qkv_master, qkv_first, qkv_second, qkv_average)
    proj_old = (proj_master, proj_first, proj_second, proj_average)
    gate_up_old = (gate_up_master, gate_up_first, gate_up_second, gate_up_average)
    wide_rate = D ** (-0.5)
    proj_rate = (3.0 * D / SEQ) ** (-0.5)
    if short:
        *qkv_out, first_rows = adam_cols(attn_terms, qkv_old, wide_rate, "qkv", True)
        proj_out = adam_rows(attn_terms, 3 * share, proj_old, proj_rate, "proj")
        gain_two = sum(term[LANES : LANES + 1, :LANES].astype(F32) for term in attn_terms)
        gain_one = first_rows[:, :1].T
    else:
        qkv_sum = reduce_all(norm_one, dqkv)
        qkv_sum = jnp.moveaxis(qkv_sum.reshape(block, 3, share), 1, 0)
        gate_up_sum = jnp.stack([reduce_all(norm_rows, gate_grad), reduce_all(norm_rows, up_grad)])
        proj_sum = reduce_all(attn_seed, context_rows).T
        down_sum = reduce_all(seed_low, hidden_rows).T
        gain_one = jnp.sum(
            qkv_master.astype(BF).astype(F32) * qkv_sum, axis=(0, 2)
        )[None]
        all_two = jnp.take(gain_two.reshape(ndp, block), pos // block, axis=0, mode="clip")
        gain_two = lax.psum_scatter(all_two, "dp", scatter_dimension=0, tiled=True)
        down_out = adam_step(down_sum, *down_old, down_rate, DECAY_RATE)
        gate_up_out = adam_step(gate_up_sum, *gate_up_old, wide_rate, DECAY_RATE)
        qkv_out = adam_step(qkv_sum, *qkv_old, wide_rate, DECAY_RATE)
        proj_out = adam_step(proj_sum, *proj_old, proj_rate, DECAY_RATE)
    gain_one = gain_one + swap(gain_one, "mp", 1)
    gain_one = (gain_one + swap(gain_one, "mp", 2)) / gains_master[:1].astype(BF).astype(F32)
    gains_sum = jnp.concatenate([gain_one, gain_two], axis=0)
    gains_out = adam_step(
        gains_sum, gains_master, gains_first, gains_second, gains_average, GAIN_RATE, 0.0
    )
    return (output, input_grad, *qkv_out, *proj_out, *gate_up_out, *down_out, *gains_out)


def solution(mesh, short=None):
    tokens = P("dp", "mp")
    cols = P(None, "dp", "mp")
    lines = P("mp", "dp")
    gains = P(None, "dp")
    in_specs = (tokens, tokens, P("dp", None), P("dp"), P(), P())
    in_specs += (cols,) * 4 + (lines,) * 4 + (cols,) * 4 + (lines,) * 4 + (gains,) * 4
    out_specs = (tokens, tokens)
    out_specs += (cols,) * 6 + (lines,) * 6 + (cols,) * 6 + (lines,) * 6 + (gains,) * 6
    return jax.shard_map(
        functools.partial(local, short=short),
        mesh=mesh,
        in_specs=in_specs,
        out_specs=out_specs,
        check_vma=False,
    )
```

```python
import functools

import jax
import jax.numpy as jnp
from jax import lax
from jax.experimental import pallas as pl
from jax.experimental.pallas import tpu as pltpu
from jax.sharding import PartitionSpec as P

D = 1024
FF = 4096
HEAD_DIM = 64
SEQ = 1024
NGROUP = 16
STEP = 7

EPS = 1e-05
THETA = 10000.0
BETA_ONE = 0.5
BETA_TWO = 0.5
ADAM_EPS = 1e-08
DECAY_RATE = 0.1
EMA_RATE = 0.6
GAIN_RATE = 0.4

BF = jnp.bfloat16
F32 = jnp.float32
LANES = 128
TILE = 256
TALL = 512
MIB = 1024 * 1024
SOFT = 1.4426950408889634 * HEAD_DIM**-0.5


def dot(a, b):
    return lax.dot_general(a, b, (((1,), (0,)), ((), ())), preferred_element_type=F32)


def dot_t(a, b):
    return lax.dot_general(a, b, (((1,), (1,)), ((), ())), preferred_element_type=F32)


def dot_l(a, b):
    return lax.dot_general(a, b, (((0,), (0,)), ((), ())), preferred_element_type=F32)


def params(mib, dims=None):
    return pltpu.CompilerParams(vmem_limit_bytes=mib * MIB, dimension_semantics=dims)


def swap(x, axis, bit):
    n = lax.axis_size(axis)
    return lax.ppermute(x, axis, [(i, i ^ bit) for i in range(n)])


def gather_mp(x):
    far = swap(x, "mp", 2)
    near = swap(x, "mp", 1)
    return [x, near, far, swap(far, "mp", 1)]


def whole(shape):
    return pl.BlockSpec(shape, lambda *_: (0,) * len(shape), pipeline_mode=pl.Buffered(1))


def cut(block, where):
    return pl.BlockSpec(block, where)


def rotary_tables(positions):
    half_dim = HEAD_DIM // 2
    frequency = THETA ** (-jnp.arange(half_dim, dtype=F32) / half_dim)
    angles = positions.astype(F32)[:, None] * frequency[None, :]
    cosine, sine = jnp.cos(angles), jnp.sin(angles)
    return (
        jnp.concatenate([cosine] * 4, axis=1),
        jnp.concatenate([-sine, sine, -sine, sine], axis=1),
    )


def turn(x, cos, sin, sign):
    lane = lax.broadcasted_iota(jnp.int32, (x.shape[0], LANES), 1)
    low = (lane % HEAD_DIM) < HEAD_DIM // 2
    parts = []
    for start in range(0, x.shape[1], LANES):
        v = x[:, start : start + LANES]
        other = jnp.where(
            low, pltpu.roll(v, LANES - HEAD_DIM // 2, 1), pltpu.roll(v, HEAD_DIM // 2, 1)
        )
        parts.append(v * cos + (sign * sin) * other)
    return jnp.concatenate(parts, axis=1)


def place_kernel(pos_ref, *refs):
    out, gains = refs[-2:]
    for p, piece in enumerate(refs[:-2]):
        bs = out.shape[1] // (len(refs) - 2)
        at = pl.multiple_of(pos_ref[len(refs) - 3 - p], bs)
        for k in range(4):
            out[k, pl.ds(at, bs), :] = piece[k * bs : (k + 1) * bs, :]
        gains[:, pl.ds(at, bs)] = piece[4 * bs : 4 * bs + 16, :bs].astype(F32)[:2, :]


def place_pieces(pos, pieces, bs):
    rows, n = pieces[0].shape
    total = bs * len(pieces)
    return pl.pallas_call(
        place_kernel,
        name="place_attention",
        grid_spec=pltpu.PrefetchScalarGridSpec(
            num_scalar_prefetch=1,
            grid=(1,),
            in_specs=[pl.BlockSpec((rows, n), lambda i, pos: (0, 0))] * len(pieces),
            out_specs=[
                pl.BlockSpec((4, total, n), lambda i, pos: (0, 0, 0)),
                pl.BlockSpec((2, total), lambda i, pos: (0, 0)),
            ],
        ),
        out_shape=[
            jax.ShapeDtypeStruct((4, total, n), BF),
            jax.ShapeDtypeStruct((2, total), F32),
        ],
        compiler_params=params(24),
    )(pos, *pieces)


def flip_kernel(in_ref, out_ref):
    out_ref[0] = in_ref[0].T


def flip(stack):
    k, a, b = stack.shape
    return pl.pallas_call(
        flip_kernel,
        name="flip",
        grid=(k,),
        in_specs=[cut((1, a, b), lambda i: (i, 0, 0))],
        out_specs=cut((1, b, a), lambda i: (i, 0, 0)),
        out_shape=jax.ShapeDtypeStruct((k, b, a), stack.dtype),
        compiler_params=params(16),
    )(stack)


def place_ffn_kernel(pos_ref, in_ref, wide_ref, down_ref):
    wide_ref[...] = in_ref[0, :2]
    down_ref[...] = in_ref[0, 2].T


def place_ffn(pos, stack):
    count, k, bs, n = stack.shape
    return pl.pallas_call(
        place_ffn_kernel,
        name="place_feed_forward",
        grid_spec=pltpu.PrefetchScalarGridSpec(
            num_scalar_prefetch=1,
            grid=(count,),
            in_specs=[pl.BlockSpec((1, k, bs, n), lambda j, pos: (j, 0, 0, 0))],
            out_specs=[
                pl.BlockSpec((2, bs, n), lambda j, pos: (0, pos[j] // bs, 0)),
                pl.BlockSpec((n, bs), lambda j, pos: (0, pos[j] // bs)),
            ],
        ),
        out_shape=[
            jax.ShapeDtypeStruct((2, count * bs, n), stack.dtype),
            jax.ShapeDtypeStruct((n, count * bs), stack.dtype),
        ],
        compiler_params=params(16),
    )(pos, stack)


def place_stack_kernel(pos_ref, in_ref, out_ref):
    out_ref[0] = in_ref[0, 0]


def place_stack(pos, stack):
    count, k, bs, n = stack.shape
    return pl.pallas_call(
        place_stack_kernel,
        name="place_stack",
        grid_spec=pltpu.PrefetchScalarGridSpec(
            num_scalar_prefetch=1,
            grid=(count, k),
            in_specs=[pl.BlockSpec((1, 1, bs, n), lambda j, w, pos: (j, w, 0, 0))],
            out_specs=pl.BlockSpec((1, bs, n), lambda j, w, pos: (w, pos[j] // bs, 0)),
        ),
        out_shape=jax.ShapeDtypeStruct((k, count * bs, n), stack.dtype),
        compiler_params=params(16),
    )(pos, stack)


def qkv_kernel(x0, x1, x2, x3, g_ref, w_ref, cos_ref, sin_ref, oh_ref,
               qkv_ref, norm_ref, scale_ref, trow_ref, qrow_ref, tacc, qacc):
    step = pl.program_id(1)
    x = jnp.concatenate([x0[...], x1[...], x2[...], x3[...]], axis=1)
    xf = x.astype(F32)
    scale = lax.rsqrt(jnp.mean(xf * xf, axis=1, keepdims=True) + EPS)
    scale_ref[...] = scale
    norm = (xf * scale * g_ref[...]).astype(BF)
    norm_ref[...] = norm
    cos, sin = cos_ref[...], sin_ref[...]
    q = turn(dot(norm, w_ref[0]), cos, sin, 1.0).astype(BF)
    qkv_ref[0] = q
    qkv_ref[1] = turn(dot(norm, w_ref[1]), cos, sin, 1.0).astype(BF)
    qkv_ref[2] = dot(norm, w_ref[2]).astype(BF)
    oh = oh_ref[0]

    @pl.when(step == 0)
    def _():
        tacc[...] = jnp.zeros_like(tacc)
        qacc[...] = jnp.zeros_like(qacc)

    tacc[...] += dot(oh, x)
    qacc[...] += dot(oh, q)

    @pl.when(step == pl.num_programs(1) - 1)
    def _():
        trow_ref[...] = tacc[...].astype(BF)
        qrow_ref[...] = qacc[...].astype(BF)


def qkv_call(pieces, gain, weights, cos, sin, onehot):
    count, share = pieces[0].shape
    windows, rows, _ = onehot.shape
    tiles = SEQ // TALL
    tile = lambda w, i: (w * tiles + i, 0)
    return pl.pallas_call(
        qkv_kernel,
        name="qkv",
        grid=(windows, tiles),
        in_specs=[cut((TALL, share), tile)] * 4
        + [
            whole((1, D)),
            whole((4, D, share)),
            cut((TALL, LANES), lambda w, i: (i, 0)),
            cut((TALL, LANES), lambda w, i: (i, 0)),
            cut((1, rows, TALL), lambda w, i: (w, 0, i)),
        ],
        out_specs=[
            cut((3, TALL, share), lambda w, i: (0, w * tiles + i, 0)),
            cut((TALL, D), tile),
            cut((TALL, 1), tile),
            cut((rows, D), lambda w, i: (w, 0)),
            cut((rows, share), lambda w, i: (w, 0)),
        ],
        out_shape=[
            jax.ShapeDtypeStruct((3, count, share), BF),
            jax.ShapeDtypeStruct((count, D), BF),
            jax.ShapeDtypeStruct((count, 1), F32),
            jax.ShapeDtypeStruct((windows * rows, D), BF),
            jax.ShapeDtypeStruct((windows * rows, share), BF),
        ],
        scratch_shapes=[pltpu.VMEM((rows, D), F32), pltpu.VMEM((rows, share), F32)],
        compiler_params=params(32),
        cost_estimate=pl.CostEstimate(
            flops=1000, bytes_accessed=1000, transcendentals=0
        ),
    )(*pieces, gain, weights, cos, sin, onehot)


def attend_kernel(q_ref, k_ref, v_ref, oh_ref, ctx_ref, crow_ref, acc, turned):
    step = pl.program_id(1)
    lane = lax.broadcasted_iota(jnp.int32, (TILE, LANES), 1)
    first = lane < HEAD_DIM
    ones = jnp.ones((SEQ, LANES), BF)

    @pl.when(step == 0)
    def _():
        acc[...] = jnp.zeros_like(acc)
        turned[...] = k_ref[0].T

    parts = []
    for start in range(0, q_ref.shape[2], LANES):
        q = q_ref[0, :, start : start + LANES]
        k = turned[start : start + LANES, :]
        v = jnp.concatenate([v_ref[0, :, start : start + LANES], ones], axis=1)
        heads = []
        for mine in (first, jnp.logical_not(first)):
            scores = dot(jnp.where(mine, q, jnp.zeros_like(q)), k)
            top = jnp.max(scores, axis=1, keepdims=True)
            weight = jnp.exp2((scores - top) * SOFT).astype(BF)
            mixed = dot(weight, v)
            heads.append(mixed[:, :LANES] / mixed[:, LANES:])
        parts.append(jnp.where(first, heads[0], heads[1]))
    context = jnp.concatenate(parts, axis=1).astype(BF)
    ctx_ref[...] = context
    acc[...] += dot(oh_ref[0], context)

    @pl.when(step == pl.num_programs(1) - 1)
    def _():
        crow_ref[...] = acc[...].astype(BF)


def attend_call(qkv, onehot):
    count, share = qkv.shape[1:]
    windows, rows, _ = onehot.shape
    tiles = SEQ // TILE
    return pl.pallas_call(
        attend_kernel,
        name="attend",
        grid=(windows, tiles),
        in_specs=[
            cut((1, TILE, share), lambda w, i: (0, w * tiles + i, 0)),
            cut((1, SEQ, share), lambda w, i: (1, w, 0)),
            cut((1, SEQ, share), lambda w, i: (2, w, 0)),
            cut((1, rows, TILE), lambda w, i: (w, 0, i)),
        ],
        out_specs=[
            cut((TILE, share), lambda w, i: (w * tiles + i, 0)),
            cut((rows, share), lambda w, i: (w, 0)),
        ],
        out_shape=[
            jax.ShapeDtypeStruct((count, share), BF),
            jax.ShapeDtypeStruct((windows * rows, share), BF),
        ],
        scratch_shapes=[pltpu.VMEM((rows, share), F32), pltpu.VMEM((share, SEQ), BF)],
        compiler_params=params(32),
        cost_estimate=pl.CostEstimate(
            flops=1000, bytes_accessed=1000, transcendentals=0
        ),
    )(qkv, qkv, qkv, onehot)


def split_chunks(value, send_ref, keep_ref, far_ref):
    share = keep_ref.shape[1]
    out = value.astype(BF)
    send_ref[:, :share] = out[:, share : 2 * share]
    send_ref[:, share:] = out[:, 3 * share :]
    keep_ref[...] = out[:, :share]
    far_ref[...] = out[:, 2 * share : 3 * share]


def join_wo(out, pieces):
    share = pieces[0].shape[0]
    for r, piece in enumerate(pieces):
        for c in range(4):
            out[r * share : (r + 1) * share, c * share : (c + 1) * share] = piece[
                :, (c ^ r) * share : ((c ^ r) + 1) * share
            ]


def rows_first_kernel(t_ref, c0, c1, c2, c3, o0, o1, o2, o3, g_ref, norm_ref, unit_ref, scale_ref, wo):
    join_wo(wo, (o0, o1, o2, o3))
    context = jnp.concatenate([c0[...], c1[...], c2[...], c3[...]], axis=1)
    residual = t_ref[...].astype(F32) + dot(context, wo[...])
    scale = lax.rsqrt(jnp.mean(residual * residual, axis=1, keepdims=True) + EPS)
    unit = residual * scale
    unit_ref[...] = unit
    scale_ref[...] = jnp.broadcast_to(scale, scale_ref.shape)
    norm_ref[...] = (unit * g_ref[...]).astype(BF)


def rows_first_call(token_rows, contexts, wo, gain):
    rows = token_rows.shape[0]
    fixed = lambda shape: pl.BlockSpec(shape, lambda i: (0,) * len(shape))
    args = (token_rows, *contexts, *wo, gain)
    return pl.pallas_call(
        rows_first_kernel,
        name="rows_first",
        grid=(1,),
        in_specs=[fixed(a.shape) for a in args],
        out_specs=[fixed((rows, D)), fixed((rows, D)), fixed((rows, LANES))],
        out_shape=[
            jax.ShapeDtypeStruct((rows, D), BF),
            jax.ShapeDtypeStruct((rows, D), F32),
            jax.ShapeDtypeStruct((rows, LANES), F32),
        ],
        scratch_shapes=[pltpu.VMEM((D, D), BF)],
        compiler_params=params(24),
        cost_estimate=pl.CostEstimate(
            flops=1000, bytes_accessed=1000, transcendentals=0
        ),
    )(*args)


def ffn_kernel(x0, x1, x2, x3, c0, c1, c2, c3, o0, o1, o2, o3, g_ref, w_ref, d_ref,
               send_ref, keep_ref, far_ref, res_ref, wo):
    share = x0.shape[1]

    @pl.when(pl.program_id(0) == 0)
    def _():
        join_wo(wo, (o0, o1, o2, o3))

    x = jnp.concatenate([x0[...], x1[...], x2[...], x3[...]], axis=1).astype(F32)
    context = jnp.concatenate([c0[...], c1[...], c2[...], c3[...]], axis=1)
    residual = x + dot(context, wo[...])
    scale = lax.rsqrt(jnp.mean(residual * residual, axis=1, keepdims=True) + EPS)
    norm = (residual * scale * g_ref[...]).astype(BF)
    res_ref[...] = residual[:, :share]
    total = None
    width = w_ref.shape[2]
    for start in range(0, width, TILE):
        gate = dot(norm, w_ref[0, :, start : start + TILE])
        up = dot(norm, w_ref[1, :, start : start + TILE])
        hidden = (gate * jax.nn.sigmoid(gate) * up).astype(BF)
        term = dot(hidden, d_ref[start : start + TILE, :])
        total = term if total is None else total + term
    split_chunks(total, send_ref, keep_ref, far_ref)


def ffn_call(pieces, contexts, wo, gain, weights, down):
    count, share = pieces[0].shape
    width = weights.shape[2]
    tile = lambda i: (i, 0)
    return pl.pallas_call(
        ffn_kernel,
        name="feed_forward",
        grid=(count // TALL,),
        in_specs=[cut((TALL, share), tile)] * 8
        + [whole((share, D))] * 4
        + [whole((1, D)), whole((2, D, width)), whole((width, D))],
        out_specs=[
            cut((TALL, 2 * share), tile),
            cut((TALL, share), tile),
            cut((TALL, share), tile),
            cut((TALL, share), tile),
        ],
        out_shape=[
            jax.ShapeDtypeStruct((count, 2 * share), BF),
            jax.ShapeDtypeStruct((count, share), BF),
            jax.ShapeDtypeStruct((count, share), BF),
            jax.ShapeDtypeStruct((count, share), F32),
        ],
        scratch_shapes=[pltpu.VMEM((D, D), BF)],
        compiler_params=params(48),
        cost_estimate=pl.CostEstimate(
            flops=1000, bytes_accessed=1000, transcendentals=0
        ),
    )(*pieces, *contexts, *wo, gain, weights, down)


def rows_kernel(n_ref, seed_ref, w_ref, d_ref,
                hid_ref, gg_ref, ug_ref, send_ref, keep_ref, far_ref, acc):
    step = pl.program_id(0)

    @pl.when(step == 0)
    def _():
        acc[...] = jnp.zeros_like(acc)

    norm = n_ref[...]
    gate = dot(norm, w_ref[0])
    up = dot(norm, w_ref[1])
    sigmoid = jax.nn.sigmoid(gate)
    silu = gate * sigmoid
    hid_ref[...] = (silu * up).astype(BF)
    hidden_grad = dot_t(seed_ref[...], d_ref[...])
    gate_grad = (hidden_grad * up * sigmoid * (1.0 + gate * (1.0 - sigmoid))).astype(BF)
    up_grad = (hidden_grad * silu).astype(BF)
    gg_ref[...] = gate_grad
    ug_ref[...] = up_grad
    acc[...] += dot_t(gate_grad, w_ref[0]) + dot_t(up_grad, w_ref[1])

    @pl.when(step == pl.num_programs(0) - 1)
    def _():
        split_chunks(acc[...], send_ref, keep_ref, far_ref)


def rows_call(norm_rows, seed, weights, down):
    rows = norm_rows.shape[0]
    width = weights.shape[2]
    share = D // 4
    part = 256
    fixed = lambda shape: pl.BlockSpec(shape, lambda i: (0,) * len(shape))
    return pl.pallas_call(
        rows_kernel,
        name="masked_rows",
        grid=(width // part,),
        in_specs=[whole((rows, D)), whole((rows, D))]
        + [cut((2, D, part), lambda i: (0, 0, i)), cut((part, D), lambda i: (i, 0))],
        out_specs=[
            cut((rows, part), lambda i: (0, i)),
            cut((rows, part), lambda i: (0, i)),
            cut((rows, part), lambda i: (0, i)),
            fixed((rows, 2 * share)),
            fixed((rows, share)),
            fixed((rows, share)),
        ],
        out_shape=[
            jax.ShapeDtypeStruct((rows, width), BF),
            jax.ShapeDtypeStruct((rows, width), BF),
            jax.ShapeDtypeStruct((rows, width), BF),
            jax.ShapeDtypeStruct((rows, 2 * share), BF),
            jax.ShapeDtypeStruct((rows, share), BF),
            jax.ShapeDtypeStruct((rows, share), BF),
        ],
        scratch_shapes=[pltpu.VMEM((rows, D), F32)],
        compiler_params=params(32),
        cost_estimate=pl.CostEstimate(
            flops=1000, bytes_accessed=1000, transcendentals=0
        ),
    )(norm_rows, seed, weights, down)


def rows_pack_kernel(pos_ref, n_ref, seed_ref, w_ref, d_ref,
                     wide_ref, dsend_ref, dkeep_ref, send_ref, keep_ref, far_ref, acc, wide_t, down_t):
    step = pl.program_id(0)

    @pl.when(step == 0)
    def _():
        acc[...] = jnp.zeros_like(acc)
        wide_t[...] = chosen(n_ref, pos_ref, range(8)).T
        down_t[...] = chosen(seed_ref, pos_ref, range(8, 16)).T

    norm = n_ref[...]
    gate = dot(norm, w_ref[0])
    up = dot(norm, w_ref[1])
    sigmoid = jax.nn.sigmoid(gate)
    silu = gate * sigmoid
    hidden = (silu * up).astype(BF)
    hidden_grad = dot_t(seed_ref[...], d_ref[...])
    gate_grad = (hidden_grad * up * sigmoid * (1.0 + gate * (1.0 - sigmoid))).astype(BF)
    up_grad = (hidden_grad * silu).astype(BF)
    acc[...] += dot_t(gate_grad, w_ref[0]) + dot_t(up_grad, w_ref[1])
    left = wide_t[...]
    part = hidden.shape[1]
    for k, grad in enumerate((gate_grad, up_grad)):
        value = dot(left, grad).astype(BF)
        for b in range(8):
            wide_ref[b, :, k * part : (k + 1) * part] = value[b * LANES : (b + 1) * LANES]
    value = dot(down_t[...], hidden).astype(BF)
    for b in range(8):
        (dsend_ref, dkeep_ref)[b // 4][b % 4] = value[b * LANES : (b + 1) * LANES]

    @pl.when(step == pl.num_programs(0) - 1)
    def _():
        split_chunks(acc[...], send_ref, keep_ref, far_ref)


def rows_pack_call(pos, norm_rows, seed, weights, down):
    rows = norm_rows.shape[0]
    width = weights.shape[2]
    share = D // 4
    part = TALL
    fixed = lambda shape: pl.BlockSpec(shape, lambda i, pos: (0,) * len(shape))
    blocks = lambda shape: pl.BlockSpec(shape, lambda i, pos: (0, 0, i))
    return pl.pallas_call(
        rows_pack_kernel,
        name="masked_rows",
        grid_spec=pltpu.PrefetchScalarGridSpec(
            num_scalar_prefetch=1,
            grid=(width // part,),
            in_specs=[fixed((rows, D)), fixed((rows, D))]
            + [blocks((2, D, part)), pl.BlockSpec((part, D), lambda i, pos: (i, 0))],
            out_specs=[
                blocks((8, LANES, 2 * part)),
                blocks((4, LANES, part)),
                blocks((4, LANES, part)),
                fixed((rows, 2 * share)),
                fixed((rows, share)),
                fixed((rows, share)),
            ],
            scratch_shapes=[
                pltpu.VMEM((rows, D), F32),
                pltpu.VMEM((D, rows), BF),
                pltpu.VMEM((D, rows), BF),
            ],
        ),
        out_shape=[
            jax.ShapeDtypeStruct((8, LANES, 2 * width), BF),
            jax.ShapeDtypeStruct((4, LANES, width), BF),
            jax.ShapeDtypeStruct((4, LANES, width), BF),
            jax.ShapeDtypeStruct((rows, 2 * share), BF),
            jax.ShapeDtypeStruct((rows, share), BF),
            jax.ShapeDtypeStruct((rows, share), BF),
        ],
        compiler_params=params(40),
        cost_estimate=pl.CostEstimate(flops=1000, bytes_accessed=1000, transcendentals=0),
    )(pos, norm_rows, seed, weights, down)


def seed_kernel(own_ref, near_ref, seed_ref, unit_ref, scale_ref, g_ref, w_ref,
                low_ref, own_seed_ref, ctx_ref, gain_ref):
    share = own_ref.shape[1] // 2
    own, near = own_ref[...], near_ref[...]
    grad = jnp.concatenate(
        [own[:, :share], near[:, :share], own[:, share:], near[:, share:]], axis=1
    ).astype(F32)
    unit = unit_ref[...].astype(F32)
    gain_ref[...] = jnp.sum(grad * unit, axis=0, keepdims=True)
    scaled = grad * g_ref[...]
    back = seed_ref[...] + scale_ref[:, :1] * (
        scaled - unit * jnp.mean(scaled * unit, axis=1, keepdims=True)
    )
    low = back.astype(BF)
    low_ref[...] = low
    high = low[:, :share]
    own_seed_ref[:, :share] = high
    own_seed_ref[:, share:] = (back[:, :share] - high.astype(F32)).astype(BF)
    ctx_ref[...] = dot(low, w_ref[0]).astype(BF)


def seed_call(own, near, seed, unit, scale, gain, weights):
    rows = own.shape[0]
    share = own.shape[1] // 2
    fixed = lambda shape: pl.BlockSpec(shape, lambda i: (0,) * len(shape))
    return pl.pallas_call(
        seed_kernel,
        name="seed_back",
        grid=(1,),
        in_specs=[fixed(a.shape) for a in (own, near, seed, unit, scale, gain)]
        + [pl.BlockSpec((1, D, share), lambda i: (3, 0, 0))],
        out_specs=[fixed((rows, D)), fixed((rows, 2 * share)), fixed((rows, share)), fixed((1, D))],
        out_shape=[
            jax.ShapeDtypeStruct((rows, D), BF),
            jax.ShapeDtypeStruct((rows, 2 * share), BF),
            jax.ShapeDtypeStruct((rows, share), BF),
            jax.ShapeDtypeStruct((1, D), F32),
        ],
        compiler_params=params(24),
        cost_estimate=pl.CostEstimate(
            flops=1000, bytes_accessed=1000, transcendentals=0
        ),
    )(own, near, seed, unit, scale, gain, weights)


def chosen(ref, pos_ref, blocks):
    return jnp.concatenate(
        [ref[:, pl.ds(pl.multiple_of(pos_ref[b], LANES), LANES)] for b in blocks], axis=1
    )


def pack_attention_kernel(pos_ref, norm_ref, d_ref, seed_ref, ctx_ref, gain_ref, send_ref, keep_ref, acc):
    step = pl.program_id(0)
    n = d_ref.shape[1]
    value = dot_l(chosen(norm_ref, pos_ref, range(8)), d_ref[...])

    @pl.when(step == 0)
    def _():
        acc[...] = value
        proj = dot_l(chosen(seed_ref, pos_ref, range(8)), ctx_ref[...]).astype(BF)
        for b in range(8):
            out = (send_ref, keep_ref)[b // 4]
            out[b % 4, :LANES, n:] = proj[b * LANES : (b + 1) * LANES]
            gain = gain_ref[:, pl.ds(pl.multiple_of(pos_ref[b], LANES), LANES)].astype(BF)
            out[b % 4, LANES:, :] = jnp.zeros((16, out.shape[2]), BF)
            out[b % 4, LANES:, :LANES] = jnp.broadcast_to(gain, (16, LANES))

    @pl.when(step > 0)
    def _():
        acc[...] += value

    @pl.when(step == pl.num_programs(0) - 1)
    def _():
        for b in range(8):
            out = (send_ref, keep_ref)[b // 4]
            out[b % 4, :LANES, :n] = acc[b * LANES : (b + 1) * LANES, :].astype(BF)


def pack_attention(pos, norm, dqkv, seed, context_rows, gain):
    count = norm.shape[0]
    rows, share = context_rows.shape
    n = dqkv.shape[1]
    tile = lambda i, pos: (i, 0)
    zero = lambda i, pos: (0, 0)
    return pl.pallas_call(
        pack_attention_kernel,
        name="pack_attention",
        grid_spec=pltpu.PrefetchScalarGridSpec(
            num_scalar_prefetch=1,
            grid=(count // TALL,),
            in_specs=[
                pl.BlockSpec((TALL, D), tile),
                pl.BlockSpec((TALL, n), tile),
                pl.BlockSpec((rows, D), zero),
                pl.BlockSpec((rows, share), zero),
                pl.BlockSpec((1, D), zero),
            ],
            out_specs=[pl.BlockSpec((4, LANES + 16, n + share), lambda i, pos: (0, 0, 0))] * 2,
            scratch_shapes=[pltpu.VMEM((D, n), F32)],
        ),
        out_shape=[jax.ShapeDtypeStruct((4, LANES + 16, n + share), BF)] * 2,
        compiler_params=params(32),
        cost_estimate=pl.CostEstimate(
            flops=1000, bytes_accessed=1000, transcendentals=0
        ),
    )(pos, norm, dqkv, seed, context_rows, gain)


def add_terms_kernel(parts, keep_ref, *refs):
    recv, outs = refs[:parts], refs[parts:]
    size = len(outs) // parts
    for k, out in enumerate(outs):
        other = recv[k // size][k % size]
        out[...] = (keep_ref[k].astype(F32) + other.astype(F32)).astype(out.dtype)


def add_terms(keep, received, name):
    count, rows, n = keep.shape
    block = lambda k: pl.BlockSpec((k, rows, 512), lambda i: (0, 0, i))
    return pl.pallas_call(
        functools.partial(add_terms_kernel, len(received)),
        name="add_" + name,
        grid=(n // 512,),
        in_specs=[block(a.shape[0]) for a in (keep, *received)],
        out_specs=[pl.BlockSpec((rows, 512), lambda i: (0, i))] * count,
        out_shape=[jax.ShapeDtypeStruct((rows, n), F32 if k == 0 else BF) for k in range(count)],
        compiler_params=params(16),
    )(keep, *received)


def back_kernel(q_ref, do_ref, a_ref, k_ref, v_ref, oh_ref, cosm_ref, sinm_ref, cos_ref, sin_ref,
                out_ref, dot_ref):
    rows, share = q_ref.shape
    lane = lax.broadcasted_iota(jnp.int32, (rows, LANES), 1)
    first = lane < HEAD_DIM
    scale = HEAD_DIM**-0.5
    dq_parts, dk_parts, dv_parts = [], [], []
    for start in range(0, share, LANES):
        q = q_ref[:, start : start + LANES]
        do = do_ref[:, start : start + LANES]
        k = k_ref[0, :, start : start + LANES]
        v = v_ref[0, :, start : start + LANES]
        dqs, dk, dv = [], None, None
        for mine in (first, jnp.logical_not(first)):
            qm = jnp.where(mine, q, jnp.zeros_like(q))
            dm = jnp.where(mine, do, jnp.zeros_like(do))
            scores = dot_t(qm, k)
            top = jnp.max(scores, axis=1, keepdims=True)
            weight = jnp.exp2((scores - top) * SOFT)
            prob = weight * (1.0 / jnp.sum(weight, axis=1, keepdims=True))
            prob_grad = dot_t(dm, v)
            delta = jnp.sum(prob * prob_grad, axis=1, keepdims=True)
            score_grad = (prob * (prob_grad - delta)).astype(BF)
            dqs.append(dot(score_grad, k))
            term = dot_l(score_grad, qm)
            dk = term if dk is None else dk + term
            term = dot_l(prob.astype(BF), dm)
            dv = term if dv is None else dv + term
        dq_parts.append(jnp.where(first, dqs[0], dqs[1]) * scale)
        dk_parts.append(dk * scale)
        dv_parts.append(dv)
    dq = jnp.concatenate(dq_parts, axis=1)
    dk = jnp.concatenate(dk_parts, axis=1)
    dv = jnp.concatenate(dv_parts, axis=1)
    both = jnp.concatenate(
        [turn(dq, cosm_ref[...], sinm_ref[...], -1.0).astype(BF), dq.astype(BF)], axis=1
    )
    both = dot_l(oh_ref[0], both)
    out_ref[:, :share] = both[:, :share].astype(BF)
    out_ref[:, share : 2 * share] = turn(dk, cos_ref[...], sin_ref[...], -1.0).astype(BF)
    out_ref[:, 2 * share :] = dv.astype(BF)
    terms = both[:, share:] * a_ref[0].astype(F32)
    terms = terms + dk * k_ref[0].astype(F32) + dv * v_ref[0].astype(F32)
    high = terms.astype(BF)
    low = (terms - high.astype(F32)).astype(BF)
    ones = jnp.ones((16, share), BF)
    dot_ref[...] = (dot_t(ones, high) + dot_t(ones, low))[:1]


def back_call(q_rows, context_grad, qkv, onehot, cosm, sinm, cos, sin):
    windows, rows, _ = onehot.shape
    count, share = qkv.shape[1:]
    mine = lambda w: (w, 0)
    fixed = lambda w: (0, 0)
    return pl.pallas_call(
        back_kernel,
        name="attend_back",
        grid=(windows,),
        in_specs=[
            cut((rows, share), mine),
            cut((rows, share), mine),
            cut((1, SEQ, share), lambda w: (0, w, 0)),
            cut((1, SEQ, share), lambda w: (1, w, 0)),
            cut((1, SEQ, share), lambda w: (2, w, 0)),
            cut((1, rows, SEQ), lambda w: (w, 0, 0)),
            cut((rows, LANES), mine),
            cut((rows, LANES), mine),
            cut((SEQ, LANES), fixed),
            cut((SEQ, LANES), fixed),
        ],
        out_specs=[cut((SEQ, 3 * share), mine), cut((1, SEQ), lambda w: (0, w))],
        out_shape=[
            jax.ShapeDtypeStruct((count, 3 * share), BF),
            jax.ShapeDtypeStruct((1, count), F32),
        ],
        compiler_params=params(40),
        cost_estimate=pl.CostEstimate(
            flops=1000, bytes_accessed=1000, transcendentals=0
        ),
    )(q_rows, context_grad, qkv, qkv, qkv, onehot, cosm, sinm, cos, sin)


def first_grad_kernel(d_ref, w_ref, send_ref, keep_ref, far_ref):
    share = keep_ref.shape[1]
    grad = None
    for t in range(3):
        term = dot(d_ref[:, t * share : (t + 1) * share], w_ref[t])
        grad = term if grad is None else grad + term
    split_chunks(grad, send_ref, keep_ref, far_ref)


def first_grad_call(dqkv, weights):
    count = dqkv.shape[0]
    share = dqkv.shape[1] // 3
    tile = lambda i: (i, 0)
    return pl.pallas_call(
        first_grad_kernel,
        name="first_grad",
        grid=(count // TALL,),
        in_specs=[cut((TALL, 3 * share), tile), whole((3, share, D))],
        out_specs=[
            cut((TALL, 2 * share), tile),
            cut((TALL, share), tile),
            cut((TALL, share), tile),
        ],
        out_shape=[
            jax.ShapeDtypeStruct((count, 2 * share), BF),
            jax.ShapeDtypeStruct((count, share), BF),
            jax.ShapeDtypeStruct((count, share), BF),
        ],
        compiler_params=params(32),
        cost_estimate=pl.CostEstimate(
            flops=1000, bytes_accessed=1000, transcendentals=0
        ),
    )(dqkv, weights)


def input_kernel(x_ref, s_ref, dot_ref, keep_ref, near_ref, far_ref, g_ref, oh_ref, hl_ref, out_ref):
    share = x_ref.shape[1]
    grad = keep_ref[...].astype(F32) + near_ref[...].astype(F32) + far_ref[...].astype(F32)
    scale = s_ref[...]
    column = jnp.broadcast_to(dot_ref[...], (8, dot_ref.shape[1])).T[:, :1]
    back = dot_l(oh_ref[0], hl_ref[0])
    unit = x_ref[...].astype(F32) * scale
    out = back[:, :share] + back[:, share:] + scale * (grad * g_ref[...] - unit * (column / D))
    out_ref[...] = out.astype(BF)


def input_call(tokens, scale, dots, keep, near, far, gain, onehot, seeds):
    count, share = tokens.shape
    windows, rows, _ = onehot.shape
    tiles = SEQ // TILE
    tile = lambda w, i: (w * tiles + i, 0)
    return pl.pallas_call(
        input_kernel,
        name="input_grad",
        grid=(windows, tiles),
        in_specs=[
            cut((TILE, share), tile),
            cut((TILE, 1), tile),
            cut((1, TILE), lambda w, i: (0, w * tiles + i)),
            cut((TILE, share), tile),
            cut((TILE, share), tile),
            cut((TILE, share), tile),
            cut((1, share), lambda w, i: (0, 0)),
            cut((1, rows, TILE), lambda w, i: (w, 0, i)),
            cut((1, rows, 2 * share), lambda w, i: (w, 0, 0)),
        ],
        out_specs=cut((TILE, share), tile),
        out_shape=jax.ShapeDtypeStruct((count, share), BF),
        compiler_params=params(24),
        cost_estimate=pl.CostEstimate(
            flops=1000, bytes_accessed=1000, transcendentals=0
        ),
    )(tokens, scale, dots, keep, near, far, gain, onehot, seeds)


def adam_step(summed, master, first_old, second, average, step_rate, weight_decay):
    new_first = BETA_ONE * first_old + (1.0 - BETA_ONE) * summed
    new_second = BETA_TWO * second + (1.0 - BETA_TWO) * summed * summed
    update = (
        new_first
        / (1.0 - BETA_ONE**STEP)
        / (jnp.sqrt(new_second / (1.0 - BETA_TWO**STEP)) + ADAM_EPS)
    )
    new_master = master - step_rate * (update + weight_decay * master)
    new_average = EMA_RATE * average + (1.0 - EMA_RATE) * new_master
    return (summed, new_master, new_first, new_second, new_average, new_master.astype(BF))


def adam_cols_kernel(sets, rate, *refs):
    terms, (m, f, s, a), outs = refs[:sets], refs[sets : sets + 4], refs[sets + 4 :]
    grad = sum((t[...].astype(F32) for t in terms[1:]), terms[0][...].astype(F32))
    values = adam_step(grad, m[0], f[0], s[0], a[0], rate, DECAY_RATE)
    for out, value in zip(outs[:6], values, strict=True):
        out[0] = value
    if len(outs) > 6:
        used = m[0].astype(BF).astype(F32)
        part = jnp.broadcast_to(jnp.sum(used * grad, axis=1, keepdims=True), outs[6].shape)

        @pl.when((pl.program_id(0) == 0) & (pl.program_id(1) == 0))
        def _():
            outs[6][...] = jnp.zeros_like(outs[6])

        outs[6][...] += part


def adam_cols(terms, arrays, rate, name, rows=False, mixed=False):
    k, bs, n = arrays[0].shape
    part = min(n, TALL)
    tiles = n // part
    term = cut((bs, part), lambda t, j: (0, j * k + t if mixed else t * tiles + j))
    spot = cut((1, bs, part), lambda t, j: (t, 0, j))
    return pl.pallas_call(
        functools.partial(adam_cols_kernel, len(terms), rate),
        name="adam_" + name,
        grid=(k, tiles),
        in_specs=[term] * len(terms) + [spot] * 4,
        out_specs=[spot] * 6 + [cut((bs, LANES), lambda t, j: (0, 0))] * rows,
        out_shape=[jax.ShapeDtypeStruct((k, bs, n), BF if i == 5 else F32) for i in range(6)]
        + [jax.ShapeDtypeStruct((bs, LANES), F32)] * rows,
        compiler_params=params(60 if mixed else 24),
    )(*terms, *arrays)


def adam_rows_kernel(rate, *refs):
    terms, (m, f, s, a), outs = refs[:4], refs[4:8], refs[8:]
    grad = sum((t[...].astype(F32) for t in terms[1:]), terms[0][...]).T
    values = adam_step(grad, m[...], f[...], s[...], a[...], rate, DECAY_RATE)
    for out, value in zip(outs, values, strict=True):
        out[...] = value


def adam_rows(terms, offset, arrays, rate, name):
    n, bs = arrays[0].shape
    term = cut((bs, TILE), lambda i: (0, offset // TILE + i))
    spot = cut((TILE, bs), lambda i: (i, 0))
    return pl.pallas_call(
        functools.partial(adam_rows_kernel, rate),
        name="adam_" + name,
        grid=(n // TILE,),
        in_specs=[term] * 4 + [spot] * 4,
        out_specs=[spot] * 6,
        out_shape=[jax.ShapeDtypeStruct((n, bs), BF if i == 5 else F32) for i in range(6)],
        compiler_params=params(24),
    )(*terms, *arrays)


def at_once(*values):
    return lax.optimization_barrier(values)


def tie(x, *others):
    return lax.optimization_barrier((x, *others))[0]


def local(
    tokens,
    cotangent,
    mask_rows,
    genome,
    group_tokens,
    owner,
    qkv_master,
    qkv_first,
    qkv_second,
    qkv_average,
    proj_master,
    proj_first,
    proj_second,
    proj_average,
    gate_up_master,
    gate_up_first,
    gate_up_second,
    gate_up_average,
    down_master,
    down_first,
    down_second,
    down_average,
    gains_master,
    gains_first,
    gains_second,
    gains_average,
    short=None,
):
    ndp = lax.axis_size("dp")
    me = lax.axis_index("dp")
    m = lax.axis_index("mp")
    count, share = tokens.shape
    block = qkv_master.shape[1]
    windows, masked = mask_rows.shape
    rows = -(-masked // 32) * 32
    if short is None:
        short = ndp == 8 and block == LANES

    def start(b):
        at = b * block
        return ((at // share) ^ m) * share + at % share

    device = jnp.arange(ndp, dtype=jnp.int32)
    owner_x = jnp.sum(
        jnp.where((device[:, None] ^ me) == device[None, :], owner[None, :], 0), axis=1
    )
    pos = start(owner)
    pos_x = start(owner_x)

    attn_block = [qkv_master[0], qkv_master[1], qkv_master[2], proj_master.T]
    ffn_block = jnp.concatenate(
        [gate_up_master.astype(BF), down_master.T.astype(BF)[None]], axis=0
    )
    far = swap(tokens, "mp", 2)
    near = swap(tokens, "mp", 1)
    if short:
        extra = jnp.pad(gains_master, ((0, 14), (0, share - block)))
        message = jnp.concatenate(attn_block + [extra], axis=0).astype(BF)
        z_pieces = [message] + [swap(message, "dp", bit) for bit in (2, 4, 6)]
        x_pieces = [swap(piece, "dp", 1) for piece in z_pieces]
        order = [None] * 8
        for k in range(4):
            order[2 * k], order[2 * k + 1] = z_pieces[k], x_pieces[k]
        attn_w, gains = place_pieces(pos_x, order[::-1], block)
        gains = gains.reshape(2, 1, D)
    else:
        attn_block = jnp.stack(attn_block).astype(BF)
        attn_w = place_stack(pos, lax.all_gather(attn_block, "dp", axis=0, tiled=False))
        all_gains = lax.all_gather(gains_master.astype(BF), "dp", axis=1, tiled=False)
        slot = (device * block)[:, None] == pos[None, :]
        gains = jnp.sum(
            jnp.where(slot[None, :, :, None], all_gains.astype(F32)[:, None], 0.0), axis=2
        ).reshape(2, 1, D)
    ffn_stack = lax.all_gather(ffn_block, "dp", axis=0, tiled=False)

    tokens_p = [tokens, near, far, swap(far, "mp", 1)]
    padded = jnp.pad(mask_rows, ((0, 0), (0, rows - masked)), constant_values=-1)
    onehot = (
        padded[:, :, None] == lax.broadcasted_iota(jnp.int32, (1, 1, SEQ), 2)
    ).astype(BF)
    cos, sin = rotary_tables(jnp.arange(SEQ))
    cosm, sinm = rotary_tables(padded.reshape(-1))
    counts = group_tokens.astype(F32)
    picked = jnp.sum(
        jnp.where(
            genome[:, None] == jnp.arange(NGROUP, dtype=jnp.int32)[None, :], counts[None, :], 0.0
        ),
        axis=1,
    )
    window_scale = NGROUP * picked / jnp.sum(counts)
    attn_t = flip(attn_w)
    wo_far = swap(attn_t[3], "mp", 2)
    qkv, norm_one, scale_one, token_rows, q_rows = qkv_call(
        tokens_p, gains[0], tie(attn_w, attn_t), cos, sin, onehot
    )
    context, context_rows = attend_call(tie(qkv, wo_far), onehot)
    wo_p = [attn_t[3], swap(attn_t[3], "mp", 1), wo_far, swap(wo_far, "mp", 1)]
    cot = jnp.pad(cotangent.reshape(windows, masked, share), ((0, 0), (0, rows - masked), (0, 0)))
    both = jnp.concatenate([context_rows, cot.reshape(windows * rows, share)], axis=0)
    both_p = gather_mp(both)
    context_rows_p = [piece[: windows * rows] for piece in both_p]
    cot = jnp.concatenate([piece[windows * rows :] for piece in both_p], axis=1)
    context = tie(context, both_p[3])
    context_far = swap(context, "mp", 2)
    seed = jnp.repeat(window_scale, rows)[:, None] * cot.astype(F32)
    seed_low = seed.astype(BF)
    norm_rows, unit, scale_rows = rows_first_call(token_rows, context_rows_p, wo_p, gains[1])

    ffn_stack = tie(ffn_stack, norm_rows)
    if short:
        wide_w, down_w = place_ffn(pos, ffn_stack)
    else:
        wide_w = place_stack(pos, ffn_stack)
        wide_w, down_w = wide_w[:2], wide_w[2].T
    if short:
        sides = jnp.concatenate([pos_x[1::2], pos_x[0::2]])
        wide_blocks, down_send, down_keep, n2_send, n2_keep, n2_far = rows_pack_call(
            jnp.concatenate([pos, sides]), norm_rows, seed_low, wide_w, down_w
        )
    else:
        hidden_rows, gate_grad, up_grad, n2_send, n2_keep, n2_far = rows_call(
            norm_rows, seed_low, wide_w, down_w
        )

    context_near, context_far = at_once(context, context_far, n2_send)[:2]
    context_p = [context, swap(context_near, "mp", 1), context_far, swap(context_far, "mp", 1)]

    def reduce_all(lhs, rhs):
        grad = dot_l(lhs, rhs).reshape(ndp, block, rhs.shape[1])
        grad = jnp.take(grad, pos // block, axis=0, mode="clip")
        return lax.psum_scatter(grad, "dp", scatter_dimension=0, tiled=True)[0]

    n2_near = swap(n2_send, "mp", 1)
    if short:
        wide_sum = lax.psum_scatter(wide_blocks, "dp", scatter_dimension=0, tiled=False)
        down_x = swap(down_send[:2], "dp", 1)
        down_x = (down_x, swap(tie(down_send[2:], down_x), "dp", 1))
    n2_near = n2_near.astype(F32)
    n2_half = jnp.concatenate(
        [n2_keep.astype(F32) + n2_near[:, :share], n2_far.astype(F32) + n2_near[:, share:]], axis=1
    ).astype(BF)
    n2_back = swap(n2_half, "mp", 2)
    if short:
        n2_back, context_p = at_once(n2_back, context_p)
    n2_back = n2_back.astype(F32)
    n2_own = (
        n2_half.astype(F32) + jnp.concatenate([n2_back[:, share:], n2_back[:, :share]], axis=1)
    ).astype(BF)
    attn_seed, own_seed, context_grad, gain_two = seed_call(
        n2_own, swap(n2_own, "mp", 1), seed, unit, scale_rows, gains[1], attn_w
    )
    own_seed = own_seed.reshape(windows, rows, 2 * share)

    dqkv, row_dot = back_call(q_rows, context_grad, qkv, onehot, cosm, sinm, cos, sin)
    first_in = dqkv
    if short:
        down_added = add_terms(down_keep, at_once(*down_x, dqkv)[:2], "down")
        attn_send, attn_keep = pack_attention(
            sides, norm_one, dqkv, attn_seed, context_rows, gain_two
        )
        attn_send, down_added, first_in, row_dot = at_once(attn_send, down_added, dqkv, row_dot)
        attn_x = swap(attn_send, "dp", 1)
    n_send, n_keep, n_far = first_grad_call(first_in, attn_t)
    row_dot = row_dot + swap(row_dot, "mp", 1)
    if short:
        n_send, row_dot = at_once(n_send, row_dot)
    n_near = swap(n_send, "mp", 1)
    row_far = swap(row_dot, "mp", 2)
    if short:
        n_near, row_far = at_once(n_near, row_far)
    row_dot = row_dot + row_far
    n_half = (n_far.astype(F32) + n_near[:, share:].astype(F32)).astype(BF)

    if short:
        n_half, down_added, ffn_in = at_once(n_half, down_added, context_p)
        down_terms = [down_added[0]] + [swap(down_added[k], "dp", 2 * k) for k in range(1, 4)]
        n_back = swap(n_half, "mp", 2)
        ffn_out = ffn_call(tokens_p, ffn_in, wo_p, gains[1], wide_w, down_w)
        ffn_out, attn_x, down_terms, n_back = at_once(ffn_out, attn_x, down_terms, n_back)
        attn_added = add_terms(attn_keep, (attn_x,), "attention")
    else:
        n_back = swap(n_half, "mp", 2)
        ffn_out = ffn_call(tokens_p, context_p, wo_p, gains[1], wide_w, down_w)
    f_send, f_keep, f_far, residual = ffn_out
    f_near = swap(f_send, "mp", 1)
    down_old = (down_master, down_first, down_second, down_average)
    down_rate = FF ** (-0.5)
    if short:
        down_out = adam_rows(down_terms, 0, down_old, down_rate, "down")
        f_near, attn_added, down_out = at_once(f_near, attn_added, down_out)
    f_half = (f_far.astype(F32) + f_near[:, share:].astype(F32)).astype(BF)
    f_part = residual + f_keep.astype(F32) + f_near[:, :share].astype(F32)
    if short:
        f_half, attn_added, f_part = at_once(f_half, attn_added, f_part)
    f_back = swap(f_half, "mp", 2)
    if short:
        attn_terms = [attn_added[0]] + [swap(attn_added[k], "dp", 2 * k) for k in range(1, 4)]
    input_grad = input_call(
        tokens,
        scale_one,
        row_dot,
        n_keep,
        n_near[:, :share],
        n_back,
        gains[0][:, :share],
        onehot,
        own_seed,
    )
    if short:
        gate_up_old = (gate_up_master, gate_up_first, gate_up_second, gate_up_average)
        gate_up_out = adam_cols([wide_sum], gate_up_old, D ** (-0.5), "gate_up", mixed=True)
        f_back, attn_terms, input_grad, gate_up_out = at_once(
            f_back, attn_terms, input_grad, gate_up_out
        )
    output = (f_part + f_back.astype(F32)).astype(BF)
    qkv_old = (qkv_master, qkv_first, qkv_second, qkv_average)
    proj_old = (proj_master, proj_first, proj_second, proj_average)
    gate_up_old = (gate_up_master, gate_up_first, gate_up_second, gate_up_average)
    wide_rate = D ** (-0.5)
    proj_rate = (3.0 * D / SEQ) ** (-0.5)
    if short:
        *qkv_out, first_rows = adam_cols(attn_terms, qkv_old, wide_rate, "qkv", True)
        proj_out = adam_rows(attn_terms, 3 * share, proj_old, proj_rate, "proj")
        gain_two = sum(term[LANES : LANES + 1, :LANES].astype(F32) for term in attn_terms)
        gain_one = first_rows[:, :1].T
    else:
        qkv_sum = reduce_all(norm_one, dqkv)
        qkv_sum = jnp.moveaxis(qkv_sum.reshape(block, 3, share), 1, 0)
        gate_up_sum = jnp.stack([reduce_all(norm_rows, gate_grad), reduce_all(norm_rows, up_grad)])
        proj_sum = reduce_all(attn_seed, context_rows).T
        down_sum = reduce_all(seed_low, hidden_rows).T
        gain_one = jnp.sum(
            qkv_master.astype(BF).astype(F32) * qkv_sum, axis=(0, 2)
        )[None]
        all_two = jnp.take(gain_two.reshape(ndp, block), pos // block, axis=0, mode="clip")
        gain_two = lax.psum_scatter(all_two, "dp", scatter_dimension=0, tiled=True)
        down_out = adam_step(down_sum, *down_old, down_rate, DECAY_RATE)
        gate_up_out = adam_step(gate_up_sum, *gate_up_old, wide_rate, DECAY_RATE)
        qkv_out = adam_step(qkv_sum, *qkv_old, wide_rate, DECAY_RATE)
        proj_out = adam_step(proj_sum, *proj_old, proj_rate, DECAY_RATE)
    gain_one = gain_one + swap(gain_one, "mp", 1)
    gain_one = (gain_one + swap(gain_one, "mp", 2)) / gains_master[:1].astype(BF).astype(F32)
    gains_sum = jnp.concatenate([gain_one, gain_two], axis=0)
    gains_out = adam_step(
        gains_sum, gains_master, gains_first, gains_second, gains_average, GAIN_RATE, 0.0
    )
    return (output, input_grad, *qkv_out, *proj_out, *gate_up_out, *down_out, *gains_out)


def solution(mesh, short=None):
    tokens = P("dp", "mp")
    cols = P(None, "dp", "mp")
    lines = P("mp", "dp")
    gains = P(None, "dp")
    in_specs = (tokens, tokens, P("dp", None), P("dp"), P(), P())
    in_specs += (cols,) * 4 + (lines,) * 4 + (cols,) * 4 + (lines,) * 4 + (gains,) * 4
    out_specs = (tokens, tokens)
    out_specs += (cols,) * 6 + (lines,) * 6 + (cols,) * 6 + (lines,) * 6 + (gains,) * 6
    return jax.shard_map(
        functools.partial(local, short=short),
        mesh=mesh,
        in_specs=in_specs,
        out_specs=out_specs,
        check_vma=False,
    )
```

```python
import functools

import jax
import jax.numpy as jnp
from jax import lax
from jax.experimental import pallas as pl
from jax.experimental.pallas import tpu as pltpu
from jax.sharding import PartitionSpec as P

D = 1024
FF = 4096
HEAD_DIM = 64
SEQ = 1024
NGROUP = 16
STEP = 7

EPS = 1e-05
THETA = 10000.0
BETA_ONE = 0.5
BETA_TWO = 0.5
ADAM_EPS = 1e-08
DECAY_RATE = 0.1
EMA_RATE = 0.6
GAIN_RATE = 0.4

BF = jnp.bfloat16
F32 = jnp.float32
LANES = 128
TILE = 256
TALL = 512
MIB = 1024 * 1024
SOFT = 1.4426950408889634 * HEAD_DIM**-0.5


def dot(a, b):
    return lax.dot_general(a, b, (((1,), (0,)), ((), ())), preferred_element_type=F32)


def dot_t(a, b):
    return lax.dot_general(a, b, (((1,), (1,)), ((), ())), preferred_element_type=F32)


def dot_l(a, b):
    return lax.dot_general(a, b, (((0,), (0,)), ((), ())), preferred_element_type=F32)


def params(mib, dims=None):
    return pltpu.CompilerParams(vmem_limit_bytes=mib * MIB, dimension_semantics=dims)


def swap(x, axis, bit):
    n = lax.axis_size(axis)
    return lax.ppermute(x, axis, [(i, i ^ bit) for i in range(n)])


def gather_mp(x):
    far = swap(x, "mp", 2)
    near = swap(x, "mp", 1)
    return [x, near, far, swap(far, "mp", 1)]


def whole(shape):
    return pl.BlockSpec(shape, lambda *_: (0,) * len(shape), pipeline_mode=pl.Buffered(1))


def cut(block, where):
    return pl.BlockSpec(block, where)


def rotary_tables(positions):
    half_dim = HEAD_DIM // 2
    frequency = THETA ** (-jnp.arange(half_dim, dtype=F32) / half_dim)
    angles = positions.astype(F32)[:, None] * frequency[None, :]
    cosine, sine = jnp.cos(angles), jnp.sin(angles)
    return (
        jnp.concatenate([cosine] * 4, axis=1),
        jnp.concatenate([-sine, sine, -sine, sine], axis=1),
    )


def turn(x, cos, sin, sign):
    lane = lax.broadcasted_iota(jnp.int32, (x.shape[0], LANES), 1)
    low = (lane % HEAD_DIM) < HEAD_DIM // 2
    parts = []
    for start in range(0, x.shape[1], LANES):
        v = x[:, start : start + LANES]
        other = jnp.where(
            low, pltpu.roll(v, LANES - HEAD_DIM // 2, 1), pltpu.roll(v, HEAD_DIM // 2, 1)
        )
        parts.append(v * cos + (sign * sin) * other)
    return jnp.concatenate(parts, axis=1)


def place_kernel(pos_ref, *refs):
    out, gains = refs[-2:]
    for p, piece in enumerate(refs[:-2]):
        bs = out.shape[1] // (len(refs) - 2)
        at = pl.multiple_of(pos_ref[len(refs) - 3 - p], bs)
        for k in range(4):
            out[k, pl.ds(at, bs), :] = piece[k * bs : (k + 1) * bs, :]
        gains[:, pl.ds(at, bs)] = piece[4 * bs : 4 * bs + 16, :bs].astype(F32)[:2, :]


def place_pieces(pos, pieces, bs):
    rows, n = pieces[0].shape
    total = bs * len(pieces)
    return pl.pallas_call(
        place_kernel,
        name="place_attention",
        grid_spec=pltpu.PrefetchScalarGridSpec(
            num_scalar_prefetch=1,
            grid=(1,),
            in_specs=[pl.BlockSpec((rows, n), lambda i, pos: (0, 0))] * len(pieces),
            out_specs=[
                pl.BlockSpec((4, total, n), lambda i, pos: (0, 0, 0)),
                pl.BlockSpec((2, total), lambda i, pos: (0, 0)),
            ],
        ),
        out_shape=[
            jax.ShapeDtypeStruct((4, total, n), BF),
            jax.ShapeDtypeStruct((2, total), F32),
        ],
        compiler_params=params(24),
    )(pos, *pieces)


def flip_kernel(in_ref, out_ref):
    out_ref[0] = in_ref[0].T


def flip(stack):
    k, a, b = stack.shape
    return pl.pallas_call(
        flip_kernel,
        name="flip",
        grid=(k,),
        in_specs=[cut((1, a, b), lambda i: (i, 0, 0))],
        out_specs=cut((1, b, a), lambda i: (i, 0, 0)),
        out_shape=jax.ShapeDtypeStruct((k, b, a), stack.dtype),
        compiler_params=params(16),
    )(stack)


def place_ffn_kernel(pos_ref, in_ref, wide_ref, down_ref):
    wide_ref[...] = in_ref[0, :2]
    down_ref[...] = in_ref[0, 2].T


def place_ffn(pos, stack):
    count, k, bs, n = stack.shape
    return pl.pallas_call(
        place_ffn_kernel,
        name="place_feed_forward",
        grid_spec=pltpu.PrefetchScalarGridSpec(
            num_scalar_prefetch=1,
            grid=(count,),
            in_specs=[pl.BlockSpec((1, k, bs, n), lambda j, pos: (j, 0, 0, 0))],
            out_specs=[
                pl.BlockSpec((2, bs, n), lambda j, pos: (0, pos[j] // bs, 0)),
                pl.BlockSpec((n, bs), lambda j, pos: (0, pos[j] // bs)),
            ],
        ),
        out_shape=[
            jax.ShapeDtypeStruct((2, count * bs, n), stack.dtype),
            jax.ShapeDtypeStruct((n, count * bs), stack.dtype),
        ],
        compiler_params=params(16),
    )(pos, stack)


def place_stack_kernel(pos_ref, in_ref, out_ref):
    out_ref[0] = in_ref[0, 0]


def place_stack(pos, stack):
    count, k, bs, n = stack.shape
    return pl.pallas_call(
        place_stack_kernel,
        name="place_stack",
        grid_spec=pltpu.PrefetchScalarGridSpec(
            num_scalar_prefetch=1,
            grid=(count, k),
            in_specs=[pl.BlockSpec((1, 1, bs, n), lambda j, w, pos: (j, w, 0, 0))],
            out_specs=pl.BlockSpec((1, bs, n), lambda j, w, pos: (w, pos[j] // bs, 0)),
        ),
        out_shape=jax.ShapeDtypeStruct((k, count * bs, n), stack.dtype),
        compiler_params=params(16),
    )(pos, stack)


def qkv_kernel(x0, x1, x2, x3, g_ref, w_ref, cos_ref, sin_ref, oh_ref,
               qkv_ref, norm_ref, scale_ref, trow_ref, qrow_ref, tacc, qacc):
    step = pl.program_id(1)
    x = jnp.concatenate([x0[...], x1[...], x2[...], x3[...]], axis=1)
    xf = x.astype(F32)
    scale = lax.rsqrt(jnp.mean(xf * xf, axis=1, keepdims=True) + EPS)
    scale_ref[...] = scale
    norm = (xf * scale * g_ref[...]).astype(BF)
    norm_ref[...] = norm
    cos, sin = cos_ref[...], sin_ref[...]
    q = turn(dot(norm, w_ref[0]), cos, sin, 1.0).astype(BF)
    qkv_ref[0] = q
    qkv_ref[1] = turn(dot(norm, w_ref[1]), cos, sin, 1.0).astype(BF)
    qkv_ref[2] = dot(norm, w_ref[2]).astype(BF)
    oh = oh_ref[0]

    @pl.when(step == 0)
    def _():
        tacc[...] = jnp.zeros_like(tacc)
        qacc[...] = jnp.zeros_like(qacc)

    tacc[...] += dot(oh, x)
    qacc[...] += dot(oh, q)

    @pl.when(step == pl.num_programs(1) - 1)
    def _():
        trow_ref[...] = tacc[...].astype(BF)
        qrow_ref[...] = qacc[...].astype(BF)


def qkv_call(pieces, gain, weights, cos, sin, onehot):
    count, share = pieces[0].shape
    windows, rows, _ = onehot.shape
    tiles = SEQ // TALL
    tile = lambda w, i: (w * tiles + i, 0)
    return pl.pallas_call(
        qkv_kernel,
        name="qkv",
        grid=(windows, tiles),
        in_specs=[cut((TALL, share), tile)] * 4
        + [
            whole((1, D)),
            whole((4, D, share)),
            cut((TALL, LANES), lambda w, i: (i, 0)),
            cut((TALL, LANES), lambda w, i: (i, 0)),
            cut((1, rows, TALL), lambda w, i: (w, 0, i)),
        ],
        out_specs=[
            cut((3, TALL, share), lambda w, i: (0, w * tiles + i, 0)),
            cut((TALL, D), tile),
            cut((TALL, 1), tile),
            cut((rows, D), lambda w, i: (w, 0)),
            cut((rows, share), lambda w, i: (w, 0)),
        ],
        out_shape=[
            jax.ShapeDtypeStruct((3, count, share), BF),
            jax.ShapeDtypeStruct((count, D), BF),
            jax.ShapeDtypeStruct((count, 1), F32),
            jax.ShapeDtypeStruct((windows * rows, D), BF),
            jax.ShapeDtypeStruct((windows * rows, share), BF),
        ],
        scratch_shapes=[pltpu.VMEM((rows, D), F32), pltpu.VMEM((rows, share), F32)],
        compiler_params=params(32),
        cost_estimate=pl.CostEstimate(
            flops=1000, bytes_accessed=1000, transcendentals=0
        ),
    )(*pieces, gain, weights, cos, sin, onehot)


def attend_kernel(q_ref, k_ref, v_ref, oh_ref, ctx_ref, crow_ref, acc, turned):
    step = pl.program_id(1)
    lane = lax.broadcasted_iota(jnp.int32, (TILE, LANES), 1)
    first = lane < HEAD_DIM
    ones = jnp.ones((SEQ, LANES), BF)

    @pl.when(step == 0)
    def _():
        acc[...] = jnp.zeros_like(acc)
        turned[...] = k_ref[0].T

    parts = []
    for start in range(0, q_ref.shape[2], LANES):
        q = q_ref[0, :, start : start + LANES]
        k = turned[start : start + LANES, :]
        v = jnp.concatenate([v_ref[0, :, start : start + LANES], ones], axis=1)
        heads = []
        for mine in (first, jnp.logical_not(first)):
            scores = dot(jnp.where(mine, q, jnp.zeros_like(q)), k)
            top = jnp.max(scores, axis=1, keepdims=True)
            weight = jnp.exp2((scores - top) * SOFT).astype(BF)
            mixed = dot(weight, v)
            heads.append(mixed[:, :LANES] / mixed[:, LANES:])
        parts.append(jnp.where(first, heads[0], heads[1]))
    context = jnp.concatenate(parts, axis=1).astype(BF)
    ctx_ref[...] = context
    acc[...] += dot(oh_ref[0], context)

    @pl.when(step == pl.num_programs(1) - 1)
    def _():
        crow_ref[...] = acc[...].astype(BF)


def attend_call(qkv, onehot):
    count, share = qkv.shape[1:]
    windows, rows, _ = onehot.shape
    tiles = SEQ // TILE
    return pl.pallas_call(
        attend_kernel,
        name="attend",
        grid=(windows, tiles),
        in_specs=[
            cut((1, TILE, share), lambda w, i: (0, w * tiles + i, 0)),
            cut((1, SEQ, share), lambda w, i: (1, w, 0)),
            cut((1, SEQ, share), lambda w, i: (2, w, 0)),
            cut((1, rows, TILE), lambda w, i: (w, 0, i)),
        ],
        out_specs=[
            cut((TILE, share), lambda w, i: (w * tiles + i, 0)),
            cut((rows, share), lambda w, i: (w, 0)),
        ],
        out_shape=[
            jax.ShapeDtypeStruct((count, share), BF),
            jax.ShapeDtypeStruct((windows * rows, share), BF),
        ],
        scratch_shapes=[pltpu.VMEM((rows, share), F32), pltpu.VMEM((share, SEQ), BF)],
        compiler_params=params(32),
        cost_estimate=pl.CostEstimate(
            flops=1000, bytes_accessed=1000, transcendentals=0
        ),
    )(qkv, qkv, qkv, onehot)


def split_chunks(value, send_ref, keep_ref, far_ref):
    share = keep_ref.shape[1]
    out = value.astype(BF)
    send_ref[:, :share] = out[:, share : 2 * share]
    send_ref[:, share:] = out[:, 3 * share :]
    keep_ref[...] = out[:, :share]
    far_ref[...] = out[:, 2 * share : 3 * share]


def join_wo(out, pieces):
    share = pieces[0].shape[0]
    for r, piece in enumerate(pieces):
        for c in range(4):
            out[r * share : (r + 1) * share, c * share : (c + 1) * share] = piece[
                :, (c ^ r) * share : ((c ^ r) + 1) * share
            ]


def rows_first_kernel(t_ref, c0, c1, c2, c3, o0, o1, o2, o3, g_ref, norm_ref, unit_ref, scale_ref, wo):
    join_wo(wo, (o0, o1, o2, o3))
    context = jnp.concatenate([c0[...], c1[...], c2[...], c3[...]], axis=1)
    residual = t_ref[...].astype(F32) + dot(context, wo[...])
    scale = lax.rsqrt(jnp.mean(residual * residual, axis=1, keepdims=True) + EPS)
    unit = residual * scale
    unit_ref[...] = unit
    scale_ref[...] = jnp.broadcast_to(scale, scale_ref.shape)
    norm_ref[...] = (unit * g_ref[...]).astype(BF)


def rows_first_call(token_rows, contexts, wo, gain):
    rows = token_rows.shape[0]
    fixed = lambda shape: pl.BlockSpec(shape, lambda i: (0,) * len(shape))
    args = (token_rows, *contexts, *wo, gain)
    return pl.pallas_call(
        rows_first_kernel,
        name="rows_first",
        grid=(1,),
        in_specs=[fixed(a.shape) for a in args],
        out_specs=[fixed((rows, D)), fixed((rows, D)), fixed((rows, LANES))],
        out_shape=[
            jax.ShapeDtypeStruct((rows, D), BF),
            jax.ShapeDtypeStruct((rows, D), F32),
            jax.ShapeDtypeStruct((rows, LANES), F32),
        ],
        scratch_shapes=[pltpu.VMEM((D, D), BF)],
        compiler_params=params(24),
        cost_estimate=pl.CostEstimate(
            flops=1000, bytes_accessed=1000, transcendentals=0
        ),
    )(*args)


def ffn_kernel(x0, x1, x2, x3, c0, c1, c2, c3, o0, o1, o2, o3, g_ref, w_ref, d_ref,
               send_ref, keep_ref, far_ref, res_ref, wo):
    share = x0.shape[1]

    @pl.when(pl.program_id(0) == 0)
    def _():
        join_wo(wo, (o0, o1, o2, o3))

    x = jnp.concatenate([x0[...], x1[...], x2[...], x3[...]], axis=1).astype(F32)
    context = jnp.concatenate([c0[...], c1[...], c2[...], c3[...]], axis=1)
    residual = x + dot(context, wo[...])
    scale = lax.rsqrt(jnp.mean(residual * residual, axis=1, keepdims=True) + EPS)
    norm = (residual * scale * g_ref[...]).astype(BF)
    res_ref[...] = residual[:, :share]
    total = None
    width = w_ref.shape[2]
    for start in range(0, width, TILE):
        gate = dot(norm, w_ref[0, :, start : start + TILE])
        up = dot(norm, w_ref[1, :, start : start + TILE])
        hidden = (gate * jax.nn.sigmoid(gate) * up).astype(BF)
        term = dot(hidden, d_ref[start : start + TILE, :])
        total = term if total is None else total + term
    split_chunks(total, send_ref, keep_ref, far_ref)


def ffn_call(pieces, contexts, wo, gain, weights, down):
    count, share = pieces[0].shape
    width = weights.shape[2]
    tile = lambda i: (i, 0)
    return pl.pallas_call(
        ffn_kernel,
        name="feed_forward",
        grid=(count // TALL,),
        in_specs=[cut((TALL, share), tile)] * 8
        + [whole((share, D))] * 4
        + [whole((1, D)), whole((2, D, width)), whole((width, D))],
        out_specs=[
            cut((TALL, 2 * share), tile),
            cut((TALL, share), tile),
            cut((TALL, share), tile),
            cut((TALL, share), tile),
        ],
        out_shape=[
            jax.ShapeDtypeStruct((count, 2 * share), BF),
            jax.ShapeDtypeStruct((count, share), BF),
            jax.ShapeDtypeStruct((count, share), BF),
            jax.ShapeDtypeStruct((count, share), F32),
        ],
        scratch_shapes=[pltpu.VMEM((D, D), BF)],
        compiler_params=params(48),
        cost_estimate=pl.CostEstimate(
            flops=1000, bytes_accessed=1000, transcendentals=0
        ),
    )(*pieces, *contexts, *wo, gain, weights, down)


def rows_kernel(n_ref, seed_ref, w_ref, d_ref,
                hid_ref, gg_ref, ug_ref, send_ref, keep_ref, far_ref, acc):
    step = pl.program_id(0)

    @pl.when(step == 0)
    def _():
        acc[...] = jnp.zeros_like(acc)

    norm = n_ref[...]
    gate = dot(norm, w_ref[0])
    up = dot(norm, w_ref[1])
    sigmoid = jax.nn.sigmoid(gate)
    silu = gate * sigmoid
    hid_ref[...] = (silu * up).astype(BF)
    hidden_grad = dot_t(seed_ref[...], d_ref[...])
    gate_grad = (hidden_grad * up * sigmoid * (1.0 + gate * (1.0 - sigmoid))).astype(BF)
    up_grad = (hidden_grad * silu).astype(BF)
    gg_ref[...] = gate_grad
    ug_ref[...] = up_grad
    acc[...] += dot_t(gate_grad, w_ref[0]) + dot_t(up_grad, w_ref[1])

    @pl.when(step == pl.num_programs(0) - 1)
    def _():
        split_chunks(acc[...], send_ref, keep_ref, far_ref)


def rows_call(norm_rows, seed, weights, down):
    rows = norm_rows.shape[0]
    width = weights.shape[2]
    share = D // 4
    part = 256
    fixed = lambda shape: pl.BlockSpec(shape, lambda i: (0,) * len(shape))
    return pl.pallas_call(
        rows_kernel,
        name="masked_rows",
        grid=(width // part,),
        in_specs=[whole((rows, D)), whole((rows, D))]
        + [cut((2, D, part), lambda i: (0, 0, i)), cut((part, D), lambda i: (i, 0))],
        out_specs=[
            cut((rows, part), lambda i: (0, i)),
            cut((rows, part), lambda i: (0, i)),
            cut((rows, part), lambda i: (0, i)),
            fixed((rows, 2 * share)),
            fixed((rows, share)),
            fixed((rows, share)),
        ],
        out_shape=[
            jax.ShapeDtypeStruct((rows, width), BF),
            jax.ShapeDtypeStruct((rows, width), BF),
            jax.ShapeDtypeStruct((rows, width), BF),
            jax.ShapeDtypeStruct((rows, 2 * share), BF),
            jax.ShapeDtypeStruct((rows, share), BF),
            jax.ShapeDtypeStruct((rows, share), BF),
        ],
        scratch_shapes=[pltpu.VMEM((rows, D), F32)],
        compiler_params=params(32),
        cost_estimate=pl.CostEstimate(
            flops=1000, bytes_accessed=1000, transcendentals=0
        ),
    )(norm_rows, seed, weights, down)


def rows_pack_kernel(pos_ref, n_ref, seed_ref, w_ref, d_ref,
                     wide_ref, dsend_ref, dkeep_ref, send_ref, keep_ref, far_ref, acc, wide_t, down_t):
    step = pl.program_id(0)

    @pl.when(step == 0)
    def _():
        acc[...] = jnp.zeros_like(acc)
        wide_t[...] = chosen(n_ref, pos_ref, range(8)).T
        down_t[...] = chosen(seed_ref, pos_ref, range(8, 16)).T

    norm = n_ref[...]
    gate = dot(norm, w_ref[0])
    up = dot(norm, w_ref[1])
    sigmoid = jax.nn.sigmoid(gate)
    silu = gate * sigmoid
    hidden = (silu * up).astype(BF)
    hidden_grad = dot_t(seed_ref[...], d_ref[...])
    gate_grad = (hidden_grad * up * sigmoid * (1.0 + gate * (1.0 - sigmoid))).astype(BF)
    up_grad = (hidden_grad * silu).astype(BF)
    acc[...] += dot_t(gate_grad, w_ref[0]) + dot_t(up_grad, w_ref[1])
    left = wide_t[...]
    part = hidden.shape[1]
    for k, grad in enumerate((gate_grad, up_grad)):
        value = dot(left, grad).astype(BF)
        for b in range(8):
            wide_ref[b, :, k * part : (k + 1) * part] = value[b * LANES : (b + 1) * LANES]
    value = dot(down_t[...], hidden).astype(BF)
    for b in range(8):
        (dsend_ref, dkeep_ref)[b // 4][b % 4] = value[b * LANES : (b + 1) * LANES]

    @pl.when(step == pl.num_programs(0) - 1)
    def _():
        split_chunks(acc[...], send_ref, keep_ref, far_ref)


def rows_pack_call(pos, norm_rows, seed, weights, down):
    rows = norm_rows.shape[0]
    width = weights.shape[2]
    share = D // 4
    part = TALL
    fixed = lambda shape: pl.BlockSpec(shape, lambda i, pos: (0,) * len(shape))
    blocks = lambda shape: pl.BlockSpec(shape, lambda i, pos: (0, 0, i))
    return pl.pallas_call(
        rows_pack_kernel,
        name="masked_rows",
        grid_spec=pltpu.PrefetchScalarGridSpec(
            num_scalar_prefetch=1,
            grid=(width // part,),
            in_specs=[fixed((rows, D)), fixed((rows, D))]
            + [blocks((2, D, part)), pl.BlockSpec((part, D), lambda i, pos: (i, 0))],
            out_specs=[
                blocks((8, LANES, 2 * part)),
                blocks((4, LANES, part)),
                blocks((4, LANES, part)),
                fixed((rows, 2 * share)),
                fixed((rows, share)),
                fixed((rows, share)),
            ],
            scratch_shapes=[
                pltpu.VMEM((rows, D), F32),
                pltpu.VMEM((D, rows), BF),
                pltpu.VMEM((D, rows), BF),
            ],
        ),
        out_shape=[
            jax.ShapeDtypeStruct((8, LANES, 2 * width), BF),
            jax.ShapeDtypeStruct((4, LANES, width), BF),
            jax.ShapeDtypeStruct((4, LANES, width), BF),
            jax.ShapeDtypeStruct((rows, 2 * share), BF),
            jax.ShapeDtypeStruct((rows, share), BF),
            jax.ShapeDtypeStruct((rows, share), BF),
        ],
        compiler_params=params(40),
        cost_estimate=pl.CostEstimate(flops=1000, bytes_accessed=1000, transcendentals=0),
    )(pos, norm_rows, seed, weights, down)


def seed_kernel(own_ref, near_ref, seed_ref, unit_ref, scale_ref, g_ref, w_ref,
                low_ref, own_seed_ref, ctx_ref, gain_ref):
    share = own_ref.shape[1] // 2
    own, near = own_ref[...], near_ref[...]
    grad = jnp.concatenate(
        [own[:, :share], near[:, :share], own[:, share:], near[:, share:]], axis=1
    ).astype(F32)
    unit = unit_ref[...].astype(F32)
    gain_ref[...] = jnp.sum(grad * unit, axis=0, keepdims=True)
    scaled = grad * g_ref[...]
    back = seed_ref[...] + scale_ref[:, :1] * (
        scaled - unit * jnp.mean(scaled * unit, axis=1, keepdims=True)
    )
    low = back.astype(BF)
    low_ref[...] = low
    high = low[:, :share]
    own_seed_ref[:, :share] = high
    own_seed_ref[:, share:] = (back[:, :share] - high.astype(F32)).astype(BF)
    ctx_ref[...] = dot(low, w_ref[0]).astype(BF)


def seed_call(own, near, seed, unit, scale, gain, weights):
    rows = own.shape[0]
    share = own.shape[1] // 2
    fixed = lambda shape: pl.BlockSpec(shape, lambda i: (0,) * len(shape))
    return pl.pallas_call(
        seed_kernel,
        name="seed_back",
        grid=(1,),
        in_specs=[fixed(a.shape) for a in (own, near, seed, unit, scale, gain)]
        + [pl.BlockSpec((1, D, share), lambda i: (3, 0, 0))],
        out_specs=[fixed((rows, D)), fixed((rows, 2 * share)), fixed((rows, share)), fixed((1, D))],
        out_shape=[
            jax.ShapeDtypeStruct((rows, D), BF),
            jax.ShapeDtypeStruct((rows, 2 * share), BF),
            jax.ShapeDtypeStruct((rows, share), BF),
            jax.ShapeDtypeStruct((1, D), F32),
        ],
        compiler_params=params(24),
        cost_estimate=pl.CostEstimate(
            flops=1000, bytes_accessed=1000, transcendentals=0
        ),
    )(own, near, seed, unit, scale, gain, weights)


def chosen(ref, pos_ref, blocks):
    return jnp.concatenate(
        [ref[:, pl.ds(pl.multiple_of(pos_ref[b], LANES), LANES)] for b in blocks], axis=1
    )


def pack_attention_kernel(pos_ref, norm_ref, d_ref, seed_ref, ctx_ref, gain_ref, send_ref, keep_ref, acc):
    step = pl.program_id(0)
    n = d_ref.shape[1]
    value = dot_l(chosen(norm_ref, pos_ref, range(8)), d_ref[...])

    @pl.when(step == 0)
    def _():
        acc[...] = value
        proj = dot_l(chosen(seed_ref, pos_ref, range(8)), ctx_ref[...]).astype(BF)
        for b in range(8):
            out = (send_ref, keep_ref)[b // 4]
            out[b % 4, :LANES, n:] = proj[b * LANES : (b + 1) * LANES]
            gain = gain_ref[:, pl.ds(pl.multiple_of(pos_ref[b], LANES), LANES)].astype(BF)
            out[b % 4, LANES:, :] = jnp.zeros((16, out.shape[2]), BF)
            out[b % 4, LANES:, :LANES] = jnp.broadcast_to(gain, (16, LANES))

    @pl.when(step > 0)
    def _():
        acc[...] += value

    @pl.when(step == pl.num_programs(0) - 1)
    def _():
        for b in range(8):
            out = (send_ref, keep_ref)[b // 4]
            out[b % 4, :LANES, :n] = acc[b * LANES : (b + 1) * LANES, :].astype(BF)


def pack_attention(pos, norm, dqkv, seed, context_rows, gain):
    count = norm.shape[0]
    rows, share = context_rows.shape
    n = dqkv.shape[1]
    tile = lambda i, pos: (i, 0)
    zero = lambda i, pos: (0, 0)
    return pl.pallas_call(
        pack_attention_kernel,
        name="pack_attention",
        grid_spec=pltpu.PrefetchScalarGridSpec(
            num_scalar_prefetch=1,
            grid=(count // TALL,),
            in_specs=[
                pl.BlockSpec((TALL, D), tile),
                pl.BlockSpec((TALL, n), tile),
                pl.BlockSpec((rows, D), zero),
                pl.BlockSpec((rows, share), zero),
                pl.BlockSpec((1, D), zero),
            ],
            out_specs=[pl.BlockSpec((4, LANES + 16, n + share), lambda i, pos: (0, 0, 0))] * 2,
            scratch_shapes=[pltpu.VMEM((D, n), F32)],
        ),
        out_shape=[jax.ShapeDtypeStruct((4, LANES + 16, n + share), BF)] * 2,
        compiler_params=params(32),
        cost_estimate=pl.CostEstimate(
            flops=1000, bytes_accessed=1000, transcendentals=0
        ),
    )(pos, norm, dqkv, seed, context_rows, gain)


def add_terms_kernel(parts, keep_ref, *refs):
    recv, outs = refs[:parts], refs[parts:]
    size = len(outs) // parts
    for k, out in enumerate(outs):
        other = recv[k // size][k % size]
        out[...] = (keep_ref[k].astype(F32) + other.astype(F32)).astype(out.dtype)


def add_terms(keep, received, name):
    count, rows, n = keep.shape
    block = lambda k: pl.BlockSpec((k, rows, 512), lambda i: (0, 0, i))
    return pl.pallas_call(
        functools.partial(add_terms_kernel, len(received)),
        name="add_" + name,
        grid=(n // 512,),
        in_specs=[block(a.shape[0]) for a in (keep, *received)],
        out_specs=[pl.BlockSpec((rows, 512), lambda i: (0, i))] * count,
        out_shape=[jax.ShapeDtypeStruct((rows, n), F32 if k == 0 else BF) for k in range(count)],
        compiler_params=params(16),
    )(keep, *received)


def back_kernel(q_ref, do_ref, a_ref, k_ref, v_ref, oh_ref, cosm_ref, sinm_ref, cos_ref, sin_ref,
                out_ref, dot_ref):
    rows, share = q_ref.shape
    lane = lax.broadcasted_iota(jnp.int32, (rows, LANES), 1)
    first = lane < HEAD_DIM
    scale = HEAD_DIM**-0.5
    dq_parts, dk_parts, dv_parts = [], [], []
    for start in range(0, share, LANES):
        q = q_ref[:, start : start + LANES]
        do = do_ref[:, start : start + LANES]
        k = k_ref[0, :, start : start + LANES]
        v = v_ref[0, :, start : start + LANES]
        dqs, dk, dv = [], None, None
        for mine in (first, jnp.logical_not(first)):
            qm = jnp.where(mine, q, jnp.zeros_like(q))
            dm = jnp.where(mine, do, jnp.zeros_like(do))
            scores = dot_t(qm, k)
            top = jnp.max(scores, axis=1, keepdims=True)
            weight = jnp.exp2((scores - top) * SOFT)
            prob = weight * (1.0 / jnp.sum(weight, axis=1, keepdims=True))
            prob_grad = dot_t(dm, v)
            delta = jnp.sum(prob * prob_grad, axis=1, keepdims=True)
            score_grad = (prob * (prob_grad - delta)).astype(BF)
            dqs.append(dot(score_grad, k))
            term = dot_l(score_grad, qm)
            dk = term if dk is None else dk + term
            term = dot_l(prob.astype(BF), dm)
            dv = term if dv is None else dv + term
        dq_parts.append(jnp.where(first, dqs[0], dqs[1]) * scale)
        dk_parts.append(dk * scale)
        dv_parts.append(dv)
    dq = jnp.concatenate(dq_parts, axis=1)
    dk = jnp.concatenate(dk_parts, axis=1)
    dv = jnp.concatenate(dv_parts, axis=1)
    both = jnp.concatenate(
        [turn(dq, cosm_ref[...], sinm_ref[...], -1.0).astype(BF), dq.astype(BF)], axis=1
    )
    both = dot_l(oh_ref[0], both)
    out_ref[:, :share] = both[:, :share].astype(BF)
    out_ref[:, share : 2 * share] = turn(dk, cos_ref[...], sin_ref[...], -1.0).astype(BF)
    out_ref[:, 2 * share :] = dv.astype(BF)
    terms = both[:, share:] * a_ref[0].astype(F32)
    terms = terms + dk * k_ref[0].astype(F32) + dv * v_ref[0].astype(F32)
    high = terms.astype(BF)
    low = (terms - high.astype(F32)).astype(BF)
    ones = jnp.ones((16, share), BF)
    dot_ref[...] = (dot_t(ones, high) + dot_t(ones, low))[:1]


def back_call(q_rows, context_grad, qkv, onehot, cosm, sinm, cos, sin):
    windows, rows, _ = onehot.shape
    count, share = qkv.shape[1:]
    mine = lambda w: (w, 0)
    fixed = lambda w: (0, 0)
    return pl.pallas_call(
        back_kernel,
        name="attend_back",
        grid=(windows,),
        in_specs=[
            cut((rows, share), mine),
            cut((rows, share), mine),
            cut((1, SEQ, share), lambda w: (0, w, 0)),
            cut((1, SEQ, share), lambda w: (1, w, 0)),
            cut((1, SEQ, share), lambda w: (2, w, 0)),
            cut((1, rows, SEQ), lambda w: (w, 0, 0)),
            cut((rows, LANES), mine),
            cut((rows, LANES), mine),
            cut((SEQ, LANES), fixed),
            cut((SEQ, LANES), fixed),
        ],
        out_specs=[cut((SEQ, 3 * share), mine), cut((1, SEQ), lambda w: (0, w))],
        out_shape=[
            jax.ShapeDtypeStruct((count, 3 * share), BF),
            jax.ShapeDtypeStruct((1, count), F32),
        ],
        compiler_params=params(40),
        cost_estimate=pl.CostEstimate(
            flops=1000, bytes_accessed=1000, transcendentals=0
        ),
    )(q_rows, context_grad, qkv, qkv, qkv, onehot, cosm, sinm, cos, sin)


def first_grad_kernel(d_ref, w_ref, send_ref, keep_ref, far_ref):
    share = keep_ref.shape[1]
    grad = None
    for t in range(3):
        term = dot(d_ref[:, t * share : (t + 1) * share], w_ref[t])
        grad = term if grad is None else grad + term
    split_chunks(grad, send_ref, keep_ref, far_ref)


def first_grad_call(dqkv, weights):
    count = dqkv.shape[0]
    share = dqkv.shape[1] // 3
    tile = lambda i: (i, 0)
    return pl.pallas_call(
        first_grad_kernel,
        name="first_grad",
        grid=(count // TALL,),
        in_specs=[cut((TALL, 3 * share), tile), whole((3, share, D))],
        out_specs=[
            cut((TALL, 2 * share), tile),
            cut((TALL, share), tile),
            cut((TALL, share), tile),
        ],
        out_shape=[
            jax.ShapeDtypeStruct((count, 2 * share), BF),
            jax.ShapeDtypeStruct((count, share), BF),
            jax.ShapeDtypeStruct((count, share), BF),
        ],
        compiler_params=params(32),
        cost_estimate=pl.CostEstimate(
            flops=1000, bytes_accessed=1000, transcendentals=0
        ),
    )(dqkv, weights)


def input_kernel(x_ref, s_ref, dot_ref, keep_ref, near_ref, far_ref, g_ref, oh_ref, hl_ref, out_ref):
    share = x_ref.shape[1]
    grad = keep_ref[...].astype(F32) + near_ref[...].astype(F32) + far_ref[...].astype(F32)
    scale = s_ref[...]
    column = jnp.broadcast_to(dot_ref[...], (8, dot_ref.shape[1])).T[:, :1]
    back = dot_l(oh_ref[0], hl_ref[0])
    unit = x_ref[...].astype(F32) * scale
    out = back[:, :share] + back[:, share:] + scale * (grad * g_ref[...] - unit * (column / D))
    out_ref[...] = out.astype(BF)


def input_call(tokens, scale, dots, keep, near, far, gain, onehot, seeds):
    count, share = tokens.shape
    windows, rows, _ = onehot.shape
    tiles = SEQ // TILE
    tile = lambda w, i: (w * tiles + i, 0)
    return pl.pallas_call(
        input_kernel,
        name="input_grad",
        grid=(windows, tiles),
        in_specs=[
            cut((TILE, share), tile),
            cut((TILE, 1), tile),
            cut((1, TILE), lambda w, i: (0, w * tiles + i)),
            cut((TILE, share), tile),
            cut((TILE, share), tile),
            cut((TILE, share), tile),
            cut((1, share), lambda w, i: (0, 0)),
            cut((1, rows, TILE), lambda w, i: (w, 0, i)),
            cut((1, rows, 2 * share), lambda w, i: (w, 0, 0)),
        ],
        out_specs=cut((TILE, share), tile),
        out_shape=jax.ShapeDtypeStruct((count, share), BF),
        compiler_params=params(24),
        cost_estimate=pl.CostEstimate(
            flops=1000, bytes_accessed=1000, transcendentals=0
        ),
    )(tokens, scale, dots, keep, near, far, gain, onehot, seeds)


def adam_step(summed, master, first_old, second, average, step_rate, weight_decay):
    new_first = BETA_ONE * first_old + (1.0 - BETA_ONE) * summed
    new_second = BETA_TWO * second + (1.0 - BETA_TWO) * summed * summed
    update = (
        new_first
        / (1.0 - BETA_ONE**STEP)
        / (jnp.sqrt(new_second / (1.0 - BETA_TWO**STEP)) + ADAM_EPS)
    )
    new_master = master - step_rate * (update + weight_decay * master)
    new_average = EMA_RATE * average + (1.0 - EMA_RATE) * new_master
    return (summed, new_master, new_first, new_second, new_average, new_master.astype(BF))


def adam_cols_kernel(sets, rate, *refs):
    terms, (m, f, s, a), outs = refs[:sets], refs[sets : sets + 4], refs[sets + 4 :]
    grad = sum((t[...].astype(F32) for t in terms[1:]), terms[0][...].astype(F32))
    values = adam_step(grad, m[0], f[0], s[0], a[0], rate, DECAY_RATE)
    for out, value in zip(outs[:6], values, strict=True):
        out[0] = value
    if len(outs) > 6:
        used = m[0].astype(BF).astype(F32)
        part = jnp.broadcast_to(jnp.sum(used * grad, axis=1, keepdims=True), outs[6].shape)

        @pl.when((pl.program_id(0) == 0) & (pl.program_id(1) == 0))
        def _():
            outs[6][...] = jnp.zeros_like(outs[6])

        outs[6][...] += part


def adam_cols(terms, arrays, rate, name, rows=False, mixed=False):
    k, bs, n = arrays[0].shape
    part = min(n, TALL)
    tiles = n // part
    term = cut((bs, part), lambda t, j: (0, j * k + t if mixed else t * tiles + j))
    spot = cut((1, bs, part), lambda t, j: (t, 0, j))
    return pl.pallas_call(
        functools.partial(adam_cols_kernel, len(terms), rate),
        name="adam_" + name,
        grid=(k, tiles),
        in_specs=[term] * len(terms) + [spot] * 4,
        out_specs=[spot] * 6 + [cut((bs, LANES), lambda t, j: (0, 0))] * rows,
        out_shape=[jax.ShapeDtypeStruct((k, bs, n), BF if i == 5 else F32) for i in range(6)]
        + [jax.ShapeDtypeStruct((bs, LANES), F32)] * rows,
        compiler_params=params(60 if mixed else 24),
    )(*terms, *arrays)


def adam_rows_kernel(rate, *refs):
    terms, (m, f, s, a), outs = refs[:4], refs[4:8], refs[8:]
    grad = sum((t[...].astype(F32) for t in terms[1:]), terms[0][...]).T
    values = adam_step(grad, m[...], f[...], s[...], a[...], rate, DECAY_RATE)
    for out, value in zip(outs, values, strict=True):
        out[...] = value


def adam_rows(terms, offset, arrays, rate, name):
    n, bs = arrays[0].shape
    term = cut((bs, TILE), lambda i: (0, offset // TILE + i))
    spot = cut((TILE, bs), lambda i: (i, 0))
    return pl.pallas_call(
        functools.partial(adam_rows_kernel, rate),
        name="adam_" + name,
        grid=(n // TILE,),
        in_specs=[term] * 4 + [spot] * 4,
        out_specs=[spot] * 6,
        out_shape=[jax.ShapeDtypeStruct((n, bs), BF if i == 5 else F32) for i in range(6)],
        compiler_params=params(24),
    )(*terms, *arrays)


def at_once(*values):
    return lax.optimization_barrier(values)


def tie(x, *others):
    return lax.optimization_barrier((x, *others))[0]


def local(
    tokens,
    cotangent,
    mask_rows,
    genome,
    group_tokens,
    owner,
    qkv_master,
    qkv_first,
    qkv_second,
    qkv_average,
    proj_master,
    proj_first,
    proj_second,
    proj_average,
    gate_up_master,
    gate_up_first,
    gate_up_second,
    gate_up_average,
    down_master,
    down_first,
    down_second,
    down_average,
    gains_master,
    gains_first,
    gains_second,
    gains_average,
    short=None,
):
    ndp = lax.axis_size("dp")
    me = lax.axis_index("dp")
    m = lax.axis_index("mp")
    count, share = tokens.shape
    block = qkv_master.shape[1]
    windows, masked = mask_rows.shape
    rows = -(-masked // 32) * 32
    if short is None:
        short = ndp == 8 and block == LANES

    def start(b):
        at = b * block
        return ((at // share) ^ m) * share + at % share

    device = jnp.arange(ndp, dtype=jnp.int32)
    owner_x = jnp.sum(
        jnp.where((device[:, None] ^ me) == device[None, :], owner[None, :], 0), axis=1
    )
    pos = start(owner)
    pos_x = start(owner_x)

    attn_block = [qkv_master[0], qkv_master[1], qkv_master[2], proj_master.T]
    ffn_block = jnp.concatenate(
        [gate_up_master.astype(BF), down_master.T.astype(BF)[None]], axis=0
    )
    far = swap(tokens, "mp", 2)
    near = swap(tokens, "mp", 1)
    if short:
        extra = jnp.pad(gains_master, ((0, 14), (0, share - block)))
        message = jnp.concatenate(attn_block + [extra], axis=0).astype(BF)
        z_pieces = [message] + [swap(message, "dp", bit) for bit in (2, 4, 6)]
        x_pieces = [swap(piece, "dp", 1) for piece in z_pieces]
        order = [None] * 8
        for k in range(4):
            order[2 * k], order[2 * k + 1] = z_pieces[k], x_pieces[k]
        attn_w, gains = place_pieces(pos_x, order[::-1], block)
        gains = gains.reshape(2, 1, D)
    else:
        attn_block = jnp.stack(attn_block).astype(BF)
        attn_w = place_stack(pos, lax.all_gather(attn_block, "dp", axis=0, tiled=False))
        all_gains = lax.all_gather(gains_master.astype(BF), "dp", axis=1, tiled=False)
        slot = (device * block)[:, None] == pos[None, :]
        gains = jnp.sum(
            jnp.where(slot[None, :, :, None], all_gains.astype(F32)[:, None], 0.0), axis=2
        ).reshape(2, 1, D)
    ffn_stack = lax.all_gather(ffn_block, "dp", axis=0, tiled=False)

    tokens_p = [tokens, near, far, swap(far, "mp", 1)]
    padded = jnp.pad(mask_rows, ((0, 0), (0, rows - masked)), constant_values=-1)
    onehot = (
        padded[:, :, None] == lax.broadcasted_iota(jnp.int32, (1, 1, SEQ), 2)
    ).astype(BF)
    cos, sin = rotary_tables(jnp.arange(SEQ))
    cosm, sinm = rotary_tables(padded.reshape(-1))
    counts = group_tokens.astype(F32)
    picked = jnp.sum(
        jnp.where(
            genome[:, None] == jnp.arange(NGROUP, dtype=jnp.int32)[None, :], counts[None, :], 0.0
        ),
        axis=1,
    )
    window_scale = NGROUP * picked / jnp.sum(counts)
    attn_t = flip(attn_w)
    wo_far = swap(attn_t[3], "mp", 2)
    qkv, norm_one, scale_one, token_rows, q_rows = qkv_call(
        tokens_p, gains[0], tie(attn_w, attn_t), cos, sin, onehot
    )
    context, context_rows = attend_call(tie(qkv, wo_far), onehot)
    wo_p = [attn_t[3], swap(attn_t[3], "mp", 1), wo_far, swap(wo_far, "mp", 1)]
    cot = jnp.pad(cotangent.reshape(windows, masked, share), ((0, 0), (0, rows - masked), (0, 0)))
    both = jnp.concatenate([context_rows, cot.reshape(windows * rows, share)], axis=0)
    both_p = gather_mp(both)
    context_rows_p = [piece[: windows * rows] for piece in both_p]
    cot = jnp.concatenate([piece[windows * rows :] for piece in both_p], axis=1)
    context = tie(context, both_p[3])
    context_far = swap(context, "mp", 2)
    seed = jnp.repeat(window_scale, rows)[:, None] * cot.astype(F32)
    seed_low = seed.astype(BF)
    norm_rows, unit, scale_rows = rows_first_call(token_rows, context_rows_p, wo_p, gains[1])

    ffn_stack = tie(ffn_stack, norm_rows)
    if short:
        wide_w, down_w = place_ffn(pos, ffn_stack)
    else:
        wide_w = place_stack(pos, ffn_stack)
        wide_w, down_w = wide_w[:2], wide_w[2].T
    if short:
        sides = jnp.concatenate([pos_x[1::2], pos_x[0::2]])
        wide_blocks, down_send, down_keep, n2_send, n2_keep, n2_far = rows_pack_call(
            jnp.concatenate([pos, sides]), norm_rows, seed_low, wide_w, down_w
        )
    else:
        hidden_rows, gate_grad, up_grad, n2_send, n2_keep, n2_far = rows_call(
            norm_rows, seed_low, wide_w, down_w
        )

    context_near, context_far = at_once(context, context_far, n2_send)[:2]
    context_p = [context, swap(context_near, "mp", 1), context_far, swap(context_far, "mp", 1)]

    def reduce_all(lhs, rhs):
        grad = dot_l(lhs, rhs).reshape(ndp, block, rhs.shape[1])
        grad = jnp.take(grad, pos // block, axis=0, mode="clip")
        return lax.psum_scatter(grad, "dp", scatter_dimension=0, tiled=True)[0]

    n2_near = swap(n2_send, "mp", 1)
    if short:
        wide_sum = lax.psum_scatter(wide_blocks, "dp", scatter_dimension=0, tiled=False)
        down_x = swap(down_send[:2], "dp", 1)
        down_x = (down_x, swap(tie(down_send[2:], down_x), "dp", 1))
    n2_near = n2_near.astype(F32)
    n2_half = jnp.concatenate(
        [n2_keep.astype(F32) + n2_near[:, :share], n2_far.astype(F32) + n2_near[:, share:]], axis=1
    ).astype(BF)
    n2_back = swap(n2_half, "mp", 2)
    if short:
        n2_back, context_p = at_once(n2_back, context_p)
    n2_back = n2_back.astype(F32)
    n2_own = (
        n2_half.astype(F32) + jnp.concatenate([n2_back[:, share:], n2_back[:, :share]], axis=1)
    ).astype(BF)
    attn_seed, own_seed, context_grad, gain_two = seed_call(
        n2_own, swap(n2_own, "mp", 1), seed, unit, scale_rows, gains[1], attn_w
    )
    own_seed = own_seed.reshape(windows, rows, 2 * share)

    dqkv, row_dot = back_call(q_rows, context_grad, qkv, onehot, cosm, sinm, cos, sin)
    first_in = dqkv
    if short:
        down_added = add_terms(down_keep, at_once(*down_x, dqkv)[:2], "down")
        attn_send, attn_keep = pack_attention(
            sides, norm_one, dqkv, attn_seed, context_rows, gain_two
        )
        attn_send, down_added, first_in, row_dot = at_once(attn_send, down_added, dqkv, row_dot)
        attn_x = swap(attn_send, "dp", 1)
    n_send, n_keep, n_far = first_grad_call(first_in, attn_t)
    row_dot = row_dot + swap(row_dot, "mp", 1)
    if short:
        n_send, row_dot = at_once(n_send, row_dot)
    n_near = swap(n_send, "mp", 1)
    row_far = swap(row_dot, "mp", 2)
    if short:
        n_near, row_far = at_once(n_near, row_far)
    row_dot = row_dot + row_far
    n_half = (n_far.astype(F32) + n_near[:, share:].astype(F32)).astype(BF)

    if short:
        n_half, down_added, ffn_in = at_once(n_half, down_added, context_p)
        down_terms = [down_added[0]] + [swap(down_added[k], "dp", 2 * k) for k in range(1, 4)]
        n_back = swap(n_half, "mp", 2)
        ffn_out = ffn_call(tokens_p, ffn_in, wo_p, gains[1], wide_w, down_w)
        ffn_out, attn_x, down_terms, n_back = at_once(ffn_out, attn_x, down_terms, n_back)
        attn_added = add_terms(attn_keep, (attn_x,), "attention")
    else:
        n_back = swap(n_half, "mp", 2)
        ffn_out = ffn_call(tokens_p, context_p, wo_p, gains[1], wide_w, down_w)
    f_send, f_keep, f_far, residual = ffn_out
    f_near = swap(f_send, "mp", 1)
    down_old = (down_master, down_first, down_second, down_average)
    down_rate = FF ** (-0.5)
    if short:
        down_out = adam_rows(down_terms, 0, down_old, down_rate, "down")
        f_near, attn_added, down_out = at_once(f_near, attn_added, down_out)
    f_half = (f_far.astype(F32) + f_near[:, share:].astype(F32)).astype(BF)
    f_part = residual + f_keep.astype(F32) + f_near[:, :share].astype(F32)
    if short:
        f_half, attn_added, f_part = at_once(f_half, attn_added, f_part)
    f_back = swap(f_half, "mp", 2)
    if short:
        attn_terms = [attn_added[0]] + [swap(attn_added[k], "dp", 2 * k) for k in range(1, 4)]
    if short:
        gate_up_old = (gate_up_master, gate_up_first, gate_up_second, gate_up_average)
        gate_up_out = adam_cols([wide_sum], gate_up_old, D ** (-0.5), "gate_up", mixed=True)
        n_back = tie(n_back, gate_up_out[0])
    input_grad = input_call(
        tokens,
        scale_one,
        row_dot,
        n_keep,
        n_near[:, :share],
        n_back,
        gains[0][:, :share],
        onehot,
        own_seed,
    )
    if short:
        f_back, input_grad = at_once(f_back, input_grad)
    output = (f_part + f_back.astype(F32)).astype(BF)
    if short:
        attn_terms, output, input_grad = at_once(attn_terms, output, input_grad)
    qkv_old = (qkv_master, qkv_first, qkv_second, qkv_average)
    proj_old = (proj_master, proj_first, proj_second, proj_average)
    gate_up_old = (gate_up_master, gate_up_first, gate_up_second, gate_up_average)
    wide_rate = D ** (-0.5)
    proj_rate = (3.0 * D / SEQ) ** (-0.5)
    if short:
        *qkv_out, first_rows = adam_cols(attn_terms, qkv_old, wide_rate, "qkv", True)
        proj_out = adam_rows(attn_terms, 3 * share, proj_old, proj_rate, "proj")
        gain_two = sum(term[LANES : LANES + 1, :LANES].astype(F32) for term in attn_terms)
        gain_one = first_rows[:, :1].T
    else:
        qkv_sum = reduce_all(norm_one, dqkv)
        qkv_sum = jnp.moveaxis(qkv_sum.reshape(block, 3, share), 1, 0)
        gate_up_sum = jnp.stack([reduce_all(norm_rows, gate_grad), reduce_all(norm_rows, up_grad)])
        proj_sum = reduce_all(attn_seed, context_rows).T
        down_sum = reduce_all(seed_low, hidden_rows).T
        gain_one = jnp.sum(
            qkv_master.astype(BF).astype(F32) * qkv_sum, axis=(0, 2)
        )[None]
        all_two = jnp.take(gain_two.reshape(ndp, block), pos // block, axis=0, mode="clip")
        gain_two = lax.psum_scatter(all_two, "dp", scatter_dimension=0, tiled=True)
        down_out = adam_step(down_sum, *down_old, down_rate, DECAY_RATE)
        gate_up_out = adam_step(gate_up_sum, *gate_up_old, wide_rate, DECAY_RATE)
        qkv_out = adam_step(qkv_sum, *qkv_old, wide_rate, DECAY_RATE)
        proj_out = adam_step(proj_sum, *proj_old, proj_rate, DECAY_RATE)
    gain_one = gain_one + swap(gain_one, "mp", 1)
    gain_one = (gain_one + swap(gain_one, "mp", 2)) / gains_master[:1].astype(BF).astype(F32)
    gains_sum = jnp.concatenate([gain_one, gain_two], axis=0)
    gains_out = adam_step(
        gains_sum, gains_master, gains_first, gains_second, gains_average, GAIN_RATE, 0.0
    )
    return (output, input_grad, *qkv_out, *proj_out, *gate_up_out, *down_out, *gains_out)


def solution(mesh, short=None):
    tokens = P("dp", "mp")
    cols = P(None, "dp", "mp")
    lines = P("mp", "dp")
    gains = P(None, "dp")
    in_specs = (tokens, tokens, P("dp", None), P("dp"), P(), P())
    in_specs += (cols,) * 4 + (lines,) * 4 + (cols,) * 4 + (lines,) * 4 + (gains,) * 4
    out_specs = (tokens, tokens)
    out_specs += (cols,) * 6 + (lines,) * 6 + (cols,) * 6 + (lines,) * 6 + (gains,) * 6
    return jax.shard_map(
        functools.partial(local, short=short),
        mesh=mesh,
        in_specs=in_specs,
        out_specs=out_specs,
        check_vma=False,
    )
```

```python
import functools

import jax
import jax.numpy as jnp
from jax import lax
from jax.experimental import pallas as pl
from jax.experimental.pallas import tpu as pltpu
from jax.sharding import PartitionSpec as P

D = 1024
FF = 4096
HEAD_DIM = 64
SEQ = 1024
NGROUP = 16
STEP = 7

EPS = 1e-05
THETA = 10000.0
BETA_ONE = 0.5
BETA_TWO = 0.5
ADAM_EPS = 1e-08
DECAY_RATE = 0.1
EMA_RATE = 0.6
GAIN_RATE = 0.4

BF = jnp.bfloat16
F32 = jnp.float32
LANES = 128
TILE = 256
TALL = 512
MIB = 1024 * 1024
SOFT = 1.4426950408889634 * HEAD_DIM**-0.5


def dot(a, b):
    return lax.dot_general(a, b, (((1,), (0,)), ((), ())), preferred_element_type=F32)


def dot_t(a, b):
    return lax.dot_general(a, b, (((1,), (1,)), ((), ())), preferred_element_type=F32)


def dot_l(a, b):
    return lax.dot_general(a, b, (((0,), (0,)), ((), ())), preferred_element_type=F32)


def params(mib, dims=None):
    return pltpu.CompilerParams(vmem_limit_bytes=mib * MIB, dimension_semantics=dims)


def swap(x, axis, bit):
    n = lax.axis_size(axis)
    return lax.ppermute(x, axis, [(i, i ^ bit) for i in range(n)])


def gather_mp(x):
    far = swap(x, "mp", 2)
    near = swap(x, "mp", 1)
    return [x, near, far, swap(far, "mp", 1)]


def whole(shape):
    return pl.BlockSpec(shape, lambda *_: (0,) * len(shape), pipeline_mode=pl.Buffered(1))


def cut(block, where):
    return pl.BlockSpec(block, where)


def rotary_tables(positions):
    half_dim = HEAD_DIM // 2
    frequency = THETA ** (-jnp.arange(half_dim, dtype=F32) / half_dim)
    angles = positions.astype(F32)[:, None] * frequency[None, :]
    cosine, sine = jnp.cos(angles), jnp.sin(angles)
    return (
        jnp.concatenate([cosine] * 4, axis=1),
        jnp.concatenate([-sine, sine, -sine, sine], axis=1),
    )


def turn(x, cos, sin, sign):
    lane = lax.broadcasted_iota(jnp.int32, (x.shape[0], LANES), 1)
    low = (lane % HEAD_DIM) < HEAD_DIM // 2
    parts = []
    for start in range(0, x.shape[1], LANES):
        v = x[:, start : start + LANES]
        other = jnp.where(
            low, pltpu.roll(v, LANES - HEAD_DIM // 2, 1), pltpu.roll(v, HEAD_DIM // 2, 1)
        )
        parts.append(v * cos + (sign * sin) * other)
    return jnp.concatenate(parts, axis=1)


def place_kernel(pos_ref, *refs):
    out, gains = refs[-2:]
    for p, piece in enumerate(refs[:-2]):
        bs = out.shape[1] // (len(refs) - 2)
        at = pl.multiple_of(pos_ref[len(refs) - 3 - p], bs)
        for k in range(4):
            out[k, pl.ds(at, bs), :] = piece[k * bs : (k + 1) * bs, :]
        gains[:, pl.ds(at, bs)] = piece[4 * bs : 4 * bs + 16, :bs].astype(F32)[:2, :]


def place_pieces(pos, pieces, bs):
    rows, n = pieces[0].shape
    total = bs * len(pieces)
    return pl.pallas_call(
        place_kernel,
        name="place_attention",
        grid_spec=pltpu.PrefetchScalarGridSpec(
            num_scalar_prefetch=1,
            grid=(1,),
            in_specs=[pl.BlockSpec((rows, n), lambda i, pos: (0, 0))] * len(pieces),
            out_specs=[
                pl.BlockSpec((4, total, n), lambda i, pos: (0, 0, 0)),
                pl.BlockSpec((2, total), lambda i, pos: (0, 0)),
            ],
        ),
        out_shape=[
            jax.ShapeDtypeStruct((4, total, n), BF),
            jax.ShapeDtypeStruct((2, total), F32),
        ],
        compiler_params=params(24),
    )(pos, *pieces)


def flip_kernel(in_ref, out_ref):
    out_ref[0] = in_ref[0].T


def flip(stack):
    k, a, b = stack.shape
    return pl.pallas_call(
        flip_kernel,
        name="flip",
        grid=(k,),
        in_specs=[cut((1, a, b), lambda i: (i, 0, 0))],
        out_specs=cut((1, b, a), lambda i: (i, 0, 0)),
        out_shape=jax.ShapeDtypeStruct((k, b, a), stack.dtype),
        compiler_params=params(16),
    )(stack)


def place_ffn_kernel(pos_ref, in_ref, wide_ref, down_ref):
    wide_ref[...] = in_ref[0, :2]
    down_ref[...] = in_ref[0, 2].T


def place_ffn(pos, stack):
    count, k, bs, n = stack.shape
    return pl.pallas_call(
        place_ffn_kernel,
        name="place_feed_forward",
        grid_spec=pltpu.PrefetchScalarGridSpec(
            num_scalar_prefetch=1,
            grid=(count,),
            in_specs=[pl.BlockSpec((1, k, bs, n), lambda j, pos: (j, 0, 0, 0))],
            out_specs=[
                pl.BlockSpec((2, bs, n), lambda j, pos: (0, pos[j] // bs, 0)),
                pl.BlockSpec((n, bs), lambda j, pos: (0, pos[j] // bs)),
            ],
        ),
        out_shape=[
            jax.ShapeDtypeStruct((2, count * bs, n), stack.dtype),
            jax.ShapeDtypeStruct((n, count * bs), stack.dtype),
        ],
        compiler_params=params(16),
    )(pos, stack)


def place_stack_kernel(pos_ref, in_ref, out_ref):
    out_ref[0] = in_ref[0, 0]


def place_stack(pos, stack):
    count, k, bs, n = stack.shape
    return pl.pallas_call(
        place_stack_kernel,
        name="place_stack",
        grid_spec=pltpu.PrefetchScalarGridSpec(
            num_scalar_prefetch=1,
            grid=(count, k),
            in_specs=[pl.BlockSpec((1, 1, bs, n), lambda j, w, pos: (j, w, 0, 0))],
            out_specs=pl.BlockSpec((1, bs, n), lambda j, w, pos: (w, pos[j] // bs, 0)),
        ),
        out_shape=jax.ShapeDtypeStruct((k, count * bs, n), stack.dtype),
        compiler_params=params(16),
    )(pos, stack)


def qkv_kernel(x0, x1, x2, x3, g_ref, w_ref, cos_ref, sin_ref, oh_ref,
               qkv_ref, norm_ref, scale_ref, trow_ref, qrow_ref, tacc, qacc):
    step = pl.program_id(1)
    x = jnp.concatenate([x0[...], x1[...], x2[...], x3[...]], axis=1)
    xf = x.astype(F32)
    scale = lax.rsqrt(jnp.mean(xf * xf, axis=1, keepdims=True) + EPS)
    scale_ref[...] = scale
    norm = (xf * scale * g_ref[...]).astype(BF)
    norm_ref[...] = norm
    cos, sin = cos_ref[...], sin_ref[...]
    q = turn(dot(norm, w_ref[0]), cos, sin, 1.0).astype(BF)
    qkv_ref[0] = q
    qkv_ref[1] = turn(dot(norm, w_ref[1]), cos, sin, 1.0).astype(BF)
    qkv_ref[2] = dot(norm, w_ref[2]).astype(BF)
    oh = oh_ref[0]

    @pl.when(step == 0)
    def _():
        tacc[...] = jnp.zeros_like(tacc)
        qacc[...] = jnp.zeros_like(qacc)

    tacc[...] += dot(oh, x)
    qacc[...] += dot(oh, q)

    @pl.when(step == pl.num_programs(1) - 1)
    def _():
        trow_ref[...] = tacc[...].astype(BF)
        qrow_ref[...] = qacc[...].astype(BF)


def qkv_call(pieces, gain, weights, cos, sin, onehot):
    count, share = pieces[0].shape
    windows, rows, _ = onehot.shape
    tiles = SEQ // TALL
    tile = lambda w, i: (w * tiles + i, 0)
    return pl.pallas_call(
        qkv_kernel,
        name="qkv",
        grid=(windows, tiles),
        in_specs=[cut((TALL, share), tile)] * 4
        + [
            whole((1, D)),
            whole((4, D, share)),
            cut((TALL, LANES), lambda w, i: (i, 0)),
            cut((TALL, LANES), lambda w, i: (i, 0)),
            cut((1, rows, TALL), lambda w, i: (w, 0, i)),
        ],
        out_specs=[
            cut((3, TALL, share), lambda w, i: (0, w * tiles + i, 0)),
            cut((TALL, D), tile),
            cut((TALL, 1), tile),
            cut((rows, D), lambda w, i: (w, 0)),
            cut((rows, share), lambda w, i: (w, 0)),
        ],
        out_shape=[
            jax.ShapeDtypeStruct((3, count, share), BF),
            jax.ShapeDtypeStruct((count, D), BF),
            jax.ShapeDtypeStruct((count, 1), F32),
            jax.ShapeDtypeStruct((windows * rows, D), BF),
            jax.ShapeDtypeStruct((windows * rows, share), BF),
        ],
        scratch_shapes=[pltpu.VMEM((rows, D), F32), pltpu.VMEM((rows, share), F32)],
        compiler_params=params(32),
        cost_estimate=pl.CostEstimate(
            flops=1000, bytes_accessed=1000, transcendentals=0
        ),
    )(*pieces, gain, weights, cos, sin, onehot)


def attend_kernel(q_ref, k_ref, v_ref, oh_ref, ctx_ref, crow_ref, acc, turned):
    step = pl.program_id(1)
    lane = lax.broadcasted_iota(jnp.int32, (TILE, LANES), 1)
    first = lane < HEAD_DIM
    ones = jnp.ones((SEQ, LANES), BF)

    @pl.when(step == 0)
    def _():
        acc[...] = jnp.zeros_like(acc)
        turned[...] = k_ref[0].T

    parts = []
    for start in range(0, q_ref.shape[2], LANES):
        q = q_ref[0, :, start : start + LANES]
        k = turned[start : start + LANES, :]
        v = jnp.concatenate([v_ref[0, :, start : start + LANES], ones], axis=1)
        heads = []
        for mine in (first, jnp.logical_not(first)):
            scores = dot(jnp.where(mine, q, jnp.zeros_like(q)), k)
            top = jnp.max(scores, axis=1, keepdims=True)
            weight = jnp.exp2((scores - top) * SOFT).astype(BF)
            mixed = dot(weight, v)
            heads.append(mixed[:, :LANES] / mixed[:, LANES:])
        parts.append(jnp.where(first, heads[0], heads[1]))
    context = jnp.concatenate(parts, axis=1).astype(BF)
    ctx_ref[...] = context
    acc[...] += dot(oh_ref[0], context)

    @pl.when(step == pl.num_programs(1) - 1)
    def _():
        crow_ref[...] = acc[...].astype(BF)


def attend_call(qkv, onehot):
    count, share = qkv.shape[1:]
    windows, rows, _ = onehot.shape
    tiles = SEQ // TILE
    return pl.pallas_call(
        attend_kernel,
        name="attend",
        grid=(windows, tiles),
        in_specs=[
            cut((1, TILE, share), lambda w, i: (0, w * tiles + i, 0)),
            cut((1, SEQ, share), lambda w, i: (1, w, 0)),
            cut((1, SEQ, share), lambda w, i: (2, w, 0)),
            cut((1, rows, TILE), lambda w, i: (w, 0, i)),
        ],
        out_specs=[
            cut((TILE, share), lambda w, i: (w * tiles + i, 0)),
            cut((rows, share), lambda w, i: (w, 0)),
        ],
        out_shape=[
            jax.ShapeDtypeStruct((count, share), BF),
            jax.ShapeDtypeStruct((windows * rows, share), BF),
        ],
        scratch_shapes=[pltpu.VMEM((rows, share), F32), pltpu.VMEM((share, SEQ), BF)],
        compiler_params=params(32),
        cost_estimate=pl.CostEstimate(
            flops=1000, bytes_accessed=1000, transcendentals=0
        ),
    )(qkv, qkv, qkv, onehot)


def split_chunks(value, send_ref, keep_ref, far_ref):
    share = keep_ref.shape[1]
    out = value.astype(BF)
    send_ref[:, :share] = out[:, share : 2 * share]
    send_ref[:, share:] = out[:, 3 * share :]
    keep_ref[...] = out[:, :share]
    far_ref[...] = out[:, 2 * share : 3 * share]


def join_wo(out, pieces):
    share = pieces[0].shape[0]
    for r, piece in enumerate(pieces):
        for c in range(4):
            out[r * share : (r + 1) * share, c * share : (c + 1) * share] = piece[
                :, (c ^ r) * share : ((c ^ r) + 1) * share
            ]


def rows_first_kernel(t_ref, c0, c1, c2, c3, o0, o1, o2, o3, g_ref, norm_ref, unit_ref, scale_ref, wo):
    join_wo(wo, (o0, o1, o2, o3))
    context = jnp.concatenate([c0[...], c1[...], c2[...], c3[...]], axis=1)
    residual = t_ref[...].astype(F32) + dot(context, wo[...])
    scale = lax.rsqrt(jnp.mean(residual * residual, axis=1, keepdims=True) + EPS)
    unit = residual * scale
    unit_ref[...] = unit
    scale_ref[...] = jnp.broadcast_to(scale, scale_ref.shape)
    norm_ref[...] = (unit * g_ref[...]).astype(BF)


def rows_first_call(token_rows, contexts, wo, gain):
    rows = token_rows.shape[0]
    fixed = lambda shape: pl.BlockSpec(shape, lambda i: (0,) * len(shape))
    args = (token_rows, *contexts, *wo, gain)
    return pl.pallas_call(
        rows_first_kernel,
        name="rows_first",
        grid=(1,),
        in_specs=[fixed(a.shape) for a in args],
        out_specs=[fixed((rows, D)), fixed((rows, D)), fixed((rows, LANES))],
        out_shape=[
            jax.ShapeDtypeStruct((rows, D), BF),
            jax.ShapeDtypeStruct((rows, D), F32),
            jax.ShapeDtypeStruct((rows, LANES), F32),
        ],
        scratch_shapes=[pltpu.VMEM((D, D), BF)],
        compiler_params=params(24),
        cost_estimate=pl.CostEstimate(
            flops=1000, bytes_accessed=1000, transcendentals=0
        ),
    )(*args)


def ffn_kernel(x0, x1, x2, x3, c0, c1, c2, c3, o0, o1, o2, o3, g_ref, w_ref, d_ref,
               send_ref, keep_ref, far_ref, res_ref, wo):
    share = x0.shape[1]

    @pl.when(pl.program_id(0) == 0)
    def _():
        join_wo(wo, (o0, o1, o2, o3))

    x = jnp.concatenate([x0[...], x1[...], x2[...], x3[...]], axis=1).astype(F32)
    context = jnp.concatenate([c0[...], c1[...], c2[...], c3[...]], axis=1)
    residual = x + dot(context, wo[...])
    scale = lax.rsqrt(jnp.mean(residual * residual, axis=1, keepdims=True) + EPS)
    norm = (residual * scale * g_ref[...]).astype(BF)
    res_ref[...] = residual[:, :share]
    total = None
    width = w_ref.shape[2]
    for start in range(0, width, TILE):
        gate = dot(norm, w_ref[0, :, start : start + TILE])
        up = dot(norm, w_ref[1, :, start : start + TILE])
        hidden = (gate * jax.nn.sigmoid(gate) * up).astype(BF)
        term = dot(hidden, d_ref[start : start + TILE, :])
        total = term if total is None else total + term
    split_chunks(total, send_ref, keep_ref, far_ref)


def ffn_call(pieces, contexts, wo, gain, weights, down):
    count, share = pieces[0].shape
    width = weights.shape[2]
    tile = lambda i: (i, 0)
    return pl.pallas_call(
        ffn_kernel,
        name="feed_forward",
        grid=(count // TALL,),
        in_specs=[cut((TALL, share), tile)] * 8
        + [whole((share, D))] * 4
        + [whole((1, D)), whole((2, D, width)), whole((width, D))],
        out_specs=[
            cut((TALL, 2 * share), tile),
            cut((TALL, share), tile),
            cut((TALL, share), tile),
            cut((TALL, share), tile),
        ],
        out_shape=[
            jax.ShapeDtypeStruct((count, 2 * share), BF),
            jax.ShapeDtypeStruct((count, share), BF),
            jax.ShapeDtypeStruct((count, share), BF),
            jax.ShapeDtypeStruct((count, share), F32),
        ],
        scratch_shapes=[pltpu.VMEM((D, D), BF)],
        compiler_params=params(48),
        cost_estimate=pl.CostEstimate(
            flops=1000, bytes_accessed=1000, transcendentals=0
        ),
    )(*pieces, *contexts, *wo, gain, weights, down)


def rows_kernel(n_ref, seed_ref, w_ref, d_ref,
                hid_ref, gg_ref, ug_ref, send_ref, keep_ref, far_ref, acc):
    step = pl.program_id(0)

    @pl.when(step == 0)
    def _():
        acc[...] = jnp.zeros_like(acc)

    norm = n_ref[...]
    gate = dot(norm, w_ref[0])
    up = dot(norm, w_ref[1])
    sigmoid = jax.nn.sigmoid(gate)
    silu = gate * sigmoid
    hid_ref[...] = (silu * up).astype(BF)
    hidden_grad = dot_t(seed_ref[...], d_ref[...])
    gate_grad = (hidden_grad * up * sigmoid * (1.0 + gate * (1.0 - sigmoid))).astype(BF)
    up_grad = (hidden_grad * silu).astype(BF)
    gg_ref[...] = gate_grad
    ug_ref[...] = up_grad
    acc[...] += dot_t(gate_grad, w_ref[0]) + dot_t(up_grad, w_ref[1])

    @pl.when(step == pl.num_programs(0) - 1)
    def _():
        split_chunks(acc[...], send_ref, keep_ref, far_ref)


def rows_call(norm_rows, seed, weights, down):
    rows = norm_rows.shape[0]
    width = weights.shape[2]
    share = D // 4
    part = 256
    fixed = lambda shape: pl.BlockSpec(shape, lambda i: (0,) * len(shape))
    return pl.pallas_call(
        rows_kernel,
        name="masked_rows",
        grid=(width // part,),
        in_specs=[whole((rows, D)), whole((rows, D))]
        + [cut((2, D, part), lambda i: (0, 0, i)), cut((part, D), lambda i: (i, 0))],
        out_specs=[
            cut((rows, part), lambda i: (0, i)),
            cut((rows, part), lambda i: (0, i)),
            cut((rows, part), lambda i: (0, i)),
            fixed((rows, 2 * share)),
            fixed((rows, share)),
            fixed((rows, share)),
        ],
        out_shape=[
            jax.ShapeDtypeStruct((rows, width), BF),
            jax.ShapeDtypeStruct((rows, width), BF),
            jax.ShapeDtypeStruct((rows, width), BF),
            jax.ShapeDtypeStruct((rows, 2 * share), BF),
            jax.ShapeDtypeStruct((rows, share), BF),
            jax.ShapeDtypeStruct((rows, share), BF),
        ],
        scratch_shapes=[pltpu.VMEM((rows, D), F32)],
        compiler_params=params(32),
        cost_estimate=pl.CostEstimate(
            flops=1000, bytes_accessed=1000, transcendentals=0
        ),
    )(norm_rows, seed, weights, down)


def rows_pack_kernel(pos_ref, n_ref, seed_ref, w_ref, d_ref,
                     wide_ref, dsend_ref, dkeep_ref, send_ref, keep_ref, far_ref, acc, wide_t, down_t):
    step = pl.program_id(0)

    @pl.when(step == 0)
    def _():
        acc[...] = jnp.zeros_like(acc)
        wide_t[...] = chosen(n_ref, pos_ref, range(8)).T
        down_t[...] = chosen(seed_ref, pos_ref, range(8, 16)).T

    norm = n_ref[...]
    gate = dot(norm, w_ref[0])
    up = dot(norm, w_ref[1])
    sigmoid = jax.nn.sigmoid(gate)
    silu = gate * sigmoid
    hidden = (silu * up).astype(BF)
    hidden_grad = dot_t(seed_ref[...], d_ref[...])
    gate_grad = (hidden_grad * up * sigmoid * (1.0 + gate * (1.0 - sigmoid))).astype(BF)
    up_grad = (hidden_grad * silu).astype(BF)
    acc[...] += dot_t(gate_grad, w_ref[0]) + dot_t(up_grad, w_ref[1])
    left = wide_t[...]
    part = hidden.shape[1]
    for k, grad in enumerate((gate_grad, up_grad)):
        value = dot(left, grad).astype(BF)
        for b in range(8):
            wide_ref[b, :, k * part : (k + 1) * part] = value[b * LANES : (b + 1) * LANES]
    value = dot(down_t[...], hidden).astype(BF)
    for b in range(8):
        (dsend_ref, dkeep_ref)[b // 4][b % 4] = value[b * LANES : (b + 1) * LANES]

    @pl.when(step == pl.num_programs(0) - 1)
    def _():
        split_chunks(acc[...], send_ref, keep_ref, far_ref)


def rows_pack_call(pos, norm_rows, seed, weights, down):
    rows = norm_rows.shape[0]
    width = weights.shape[2]
    share = D // 4
    part = TALL
    fixed = lambda shape: pl.BlockSpec(shape, lambda i, pos: (0,) * len(shape))
    blocks = lambda shape: pl.BlockSpec(shape, lambda i, pos: (0, 0, i))
    return pl.pallas_call(
        rows_pack_kernel,
        name="masked_rows",
        grid_spec=pltpu.PrefetchScalarGridSpec(
            num_scalar_prefetch=1,
            grid=(width // part,),
            in_specs=[fixed((rows, D)), fixed((rows, D))]
            + [blocks((2, D, part)), pl.BlockSpec((part, D), lambda i, pos: (i, 0))],
            out_specs=[
                blocks((8, LANES, 2 * part)),
                blocks((4, LANES, part)),
                blocks((4, LANES, part)),
                fixed((rows, 2 * share)),
                fixed((rows, share)),
                fixed((rows, share)),
            ],
            scratch_shapes=[
                pltpu.VMEM((rows, D), F32),
                pltpu.VMEM((D, rows), BF),
                pltpu.VMEM((D, rows), BF),
            ],
        ),
        out_shape=[
            jax.ShapeDtypeStruct((8, LANES, 2 * width), BF),
            jax.ShapeDtypeStruct((4, LANES, width), BF),
            jax.ShapeDtypeStruct((4, LANES, width), BF),
            jax.ShapeDtypeStruct((rows, 2 * share), BF),
            jax.ShapeDtypeStruct((rows, share), BF),
            jax.ShapeDtypeStruct((rows, share), BF),
        ],
        compiler_params=params(40),
        cost_estimate=pl.CostEstimate(flops=1000, bytes_accessed=1000, transcendentals=0),
    )(pos, norm_rows, seed, weights, down)


def seed_kernel(own_ref, near_ref, seed_ref, unit_ref, scale_ref, g_ref, w_ref,
                low_ref, own_seed_ref, ctx_ref, gain_ref):
    share = own_ref.shape[1] // 2
    own, near = own_ref[...], near_ref[...]
    grad = jnp.concatenate(
        [own[:, :share], near[:, :share], own[:, share:], near[:, share:]], axis=1
    ).astype(F32)
    unit = unit_ref[...].astype(F32)
    gain_ref[...] = jnp.sum(grad * unit, axis=0, keepdims=True)
    scaled = grad * g_ref[...]
    back = seed_ref[...] + scale_ref[:, :1] * (
        scaled - unit * jnp.mean(scaled * unit, axis=1, keepdims=True)
    )
    low = back.astype(BF)
    low_ref[...] = low
    high = low[:, :share]
    own_seed_ref[:, :share] = high
    own_seed_ref[:, share:] = (back[:, :share] - high.astype(F32)).astype(BF)
    ctx_ref[...] = dot(low, w_ref[0]).astype(BF)


def seed_call(own, near, seed, unit, scale, gain, weights):
    rows = own.shape[0]
    share = own.shape[1] // 2
    fixed = lambda shape: pl.BlockSpec(shape, lambda i: (0,) * len(shape))
    return pl.pallas_call(
        seed_kernel,
        name="seed_back",
        grid=(1,),
        in_specs=[fixed(a.shape) for a in (own, near, seed, unit, scale, gain)]
        + [pl.BlockSpec((1, D, share), lambda i: (3, 0, 0))],
        out_specs=[fixed((rows, D)), fixed((rows, 2 * share)), fixed((rows, share)), fixed((1, D))],
        out_shape=[
            jax.ShapeDtypeStruct((rows, D), BF),
            jax.ShapeDtypeStruct((rows, 2 * share), BF),
            jax.ShapeDtypeStruct((rows, share), BF),
            jax.ShapeDtypeStruct((1, D), F32),
        ],
        compiler_params=params(24),
        cost_estimate=pl.CostEstimate(
            flops=1000, bytes_accessed=1000, transcendentals=0
        ),
    )(own, near, seed, unit, scale, gain, weights)


def chosen(ref, pos_ref, blocks):
    return jnp.concatenate(
        [ref[:, pl.ds(pl.multiple_of(pos_ref[b], LANES), LANES)] for b in blocks], axis=1
    )


def pack_attention_kernel(pos_ref, norm_ref, d_ref, seed_ref, ctx_ref, gain_ref, send_ref, keep_ref, acc):
    step = pl.program_id(0)
    n = d_ref.shape[1]
    value = dot_l(chosen(norm_ref, pos_ref, range(8)), d_ref[...])

    @pl.when(step == 0)
    def _():
        acc[...] = value
        proj = dot_l(chosen(seed_ref, pos_ref, range(8)), ctx_ref[...]).astype(BF)
        for b in range(8):
            out = (send_ref, keep_ref)[b // 4]
            out[b % 4, :LANES, n:] = proj[b * LANES : (b + 1) * LANES]
            gain = gain_ref[:, pl.ds(pl.multiple_of(pos_ref[b], LANES), LANES)].astype(BF)
            out[b % 4, LANES:, :] = jnp.zeros((16, out.shape[2]), BF)
            out[b % 4, LANES:, :LANES] = jnp.broadcast_to(gain, (16, LANES))

    @pl.when(step > 0)
    def _():
        acc[...] += value

    @pl.when(step == pl.num_programs(0) - 1)
    def _():
        for b in range(8):
            out = (send_ref, keep_ref)[b // 4]
            out[b % 4, :LANES, :n] = acc[b * LANES : (b + 1) * LANES, :].astype(BF)


def pack_attention(pos, norm, dqkv, seed, context_rows, gain):
    count = norm.shape[0]
    rows, share = context_rows.shape
    n = dqkv.shape[1]
    tile = lambda i, pos: (i, 0)
    zero = lambda i, pos: (0, 0)
    return pl.pallas_call(
        pack_attention_kernel,
        name="pack_attention",
        grid_spec=pltpu.PrefetchScalarGridSpec(
            num_scalar_prefetch=1,
            grid=(count // TALL,),
            in_specs=[
                pl.BlockSpec((TALL, D), tile),
                pl.BlockSpec((TALL, n), tile),
                pl.BlockSpec((rows, D), zero),
                pl.BlockSpec((rows, share), zero),
                pl.BlockSpec((1, D), zero),
            ],
            out_specs=[pl.BlockSpec((4, LANES + 16, n + share), lambda i, pos: (0, 0, 0))] * 2,
            scratch_shapes=[pltpu.VMEM((D, n), F32)],
        ),
        out_shape=[jax.ShapeDtypeStruct((4, LANES + 16, n + share), BF)] * 2,
        compiler_params=params(32),
        cost_estimate=pl.CostEstimate(
            flops=1000, bytes_accessed=1000, transcendentals=0
        ),
    )(pos, norm, dqkv, seed, context_rows, gain)


def add_terms_kernel(parts, keep_ref, *refs):
    recv, outs = refs[:parts], refs[parts:]
    size = len(outs) // parts
    for k, out in enumerate(outs):
        other = recv[k // size][k % size]
        out[...] = (keep_ref[k].astype(F32) + other.astype(F32)).astype(out.dtype)


def add_terms(keep, received, name):
    count, rows, n = keep.shape
    block = lambda k: pl.BlockSpec((k, rows, 512), lambda i: (0, 0, i))
    return pl.pallas_call(
        functools.partial(add_terms_kernel, len(received)),
        name="add_" + name,
        grid=(n // 512,),
        in_specs=[block(a.shape[0]) for a in (keep, *received)],
        out_specs=[pl.BlockSpec((rows, 512), lambda i: (0, i))] * count,
        out_shape=[jax.ShapeDtypeStruct((rows, n), F32 if k == 0 else BF) for k in range(count)],
        compiler_params=params(16),
    )(keep, *received)


def back_kernel(q_ref, do_ref, a_ref, k_ref, v_ref, oh_ref, cosm_ref, sinm_ref, cos_ref, sin_ref,
                out_ref, dot_ref):
    rows, share = q_ref.shape
    lane = lax.broadcasted_iota(jnp.int32, (rows, LANES), 1)
    first = lane < HEAD_DIM
    scale = HEAD_DIM**-0.5
    dq_parts, dk_parts, dv_parts = [], [], []
    for start in range(0, share, LANES):
        q = q_ref[:, start : start + LANES]
        do = do_ref[:, start : start + LANES]
        k = k_ref[0, :, start : start + LANES]
        v = v_ref[0, :, start : start + LANES]
        dqs, dk, dv = [], None, None
        for mine in (first, jnp.logical_not(first)):
            qm = jnp.where(mine, q, jnp.zeros_like(q))
            dm = jnp.where(mine, do, jnp.zeros_like(do))
            scores = dot_t(qm, k)
            top = jnp.max(scores, axis=1, keepdims=True)
            weight = jnp.exp2((scores - top) * SOFT)
            prob = weight * (1.0 / jnp.sum(weight, axis=1, keepdims=True))
            prob_grad = dot_t(dm, v)
            delta = jnp.sum(prob * prob_grad, axis=1, keepdims=True)
            score_grad = (prob * (prob_grad - delta)).astype(BF)
            dqs.append(dot(score_grad, k))
            term = dot_l(score_grad, qm)
            dk = term if dk is None else dk + term
            term = dot_l(prob.astype(BF), dm)
            dv = term if dv is None else dv + term
        dq_parts.append(jnp.where(first, dqs[0], dqs[1]) * scale)
        dk_parts.append(dk * scale)
        dv_parts.append(dv)
    dq = jnp.concatenate(dq_parts, axis=1)
    dk = jnp.concatenate(dk_parts, axis=1)
    dv = jnp.concatenate(dv_parts, axis=1)
    both = jnp.concatenate(
        [turn(dq, cosm_ref[...], sinm_ref[...], -1.0).astype(BF), dq.astype(BF)], axis=1
    )
    both = dot_l(oh_ref[0], both)
    out_ref[:, :share] = both[:, :share].astype(BF)
    out_ref[:, share : 2 * share] = turn(dk, cos_ref[...], sin_ref[...], -1.0).astype(BF)
    out_ref[:, 2 * share :] = dv.astype(BF)
    terms = both[:, share:] * a_ref[0].astype(F32)
    terms = terms + dk * k_ref[0].astype(F32) + dv * v_ref[0].astype(F32)
    high = terms.astype(BF)
    low = (terms - high.astype(F32)).astype(BF)
    ones = jnp.ones((16, share), BF)
    dot_ref[...] = (dot_t(ones, high) + dot_t(ones, low))[:1]


def back_call(q_rows, context_grad, qkv, onehot, cosm, sinm, cos, sin):
    windows, rows, _ = onehot.shape
    count, share = qkv.shape[1:]
    mine = lambda w: (w, 0)
    fixed = lambda w: (0, 0)
    return pl.pallas_call(
        back_kernel,
        name="attend_back",
        grid=(windows,),
        in_specs=[
            cut((rows, share), mine),
            cut((rows, share), mine),
            cut((1, SEQ, share), lambda w: (0, w, 0)),
            cut((1, SEQ, share), lambda w: (1, w, 0)),
            cut((1, SEQ, share), lambda w: (2, w, 0)),
            cut((1, rows, SEQ), lambda w: (w, 0, 0)),
            cut((rows, LANES), mine),
            cut((rows, LANES), mine),
            cut((SEQ, LANES), fixed),
            cut((SEQ, LANES), fixed),
        ],
        out_specs=[cut((SEQ, 3 * share), mine), cut((1, SEQ), lambda w: (0, w))],
        out_shape=[
            jax.ShapeDtypeStruct((count, 3 * share), BF),
            jax.ShapeDtypeStruct((1, count), F32),
        ],
        compiler_params=params(40),
        cost_estimate=pl.CostEstimate(
            flops=1000, bytes_accessed=1000, transcendentals=0
        ),
    )(q_rows, context_grad, qkv, qkv, qkv, onehot, cosm, sinm, cos, sin)


def first_grad_kernel(d_ref, w_ref, send_ref, keep_ref, far_ref):
    share = keep_ref.shape[1]
    grad = None
    for t in range(3):
        term = dot(d_ref[:, t * share : (t + 1) * share], w_ref[t])
        grad = term if grad is None else grad + term
    split_chunks(grad, send_ref, keep_ref, far_ref)


def first_grad_call(dqkv, weights):
    count = dqkv.shape[0]
    share = dqkv.shape[1] // 3
    tile = lambda i: (i, 0)
    return pl.pallas_call(
        first_grad_kernel,
        name="first_grad",
        grid=(count // TALL,),
        in_specs=[cut((TALL, 3 * share), tile), whole((3, share, D))],
        out_specs=[
            cut((TALL, 2 * share), tile),
            cut((TALL, share), tile),
            cut((TALL, share), tile),
        ],
        out_shape=[
            jax.ShapeDtypeStruct((count, 2 * share), BF),
            jax.ShapeDtypeStruct((count, share), BF),
            jax.ShapeDtypeStruct((count, share), BF),
        ],
        compiler_params=params(32),
        cost_estimate=pl.CostEstimate(
            flops=1000, bytes_accessed=1000, transcendentals=0
        ),
    )(dqkv, weights)


def input_kernel(x_ref, s_ref, dot_ref, keep_ref, near_ref, far_ref, g_ref, oh_ref, hl_ref, out_ref):
    share = x_ref.shape[1]
    grad = keep_ref[...].astype(F32) + near_ref[...].astype(F32) + far_ref[...].astype(F32)
    scale = s_ref[...]
    column = jnp.broadcast_to(dot_ref[...], (8, dot_ref.shape[1])).T[:, :1]
    back = dot_l(oh_ref[0], hl_ref[0])
    unit = x_ref[...].astype(F32) * scale
    out = back[:, :share] + back[:, share:] + scale * (grad * g_ref[...] - unit * (column / D))
    out_ref[...] = out.astype(BF)


def input_call(tokens, scale, dots, keep, near, far, gain, onehot, seeds):
    count, share = tokens.shape
    windows, rows, _ = onehot.shape
    tiles = SEQ // TILE
    tile = lambda w, i: (w * tiles + i, 0)
    return pl.pallas_call(
        input_kernel,
        name="input_grad",
        grid=(windows, tiles),
        in_specs=[
            cut((TILE, share), tile),
            cut((TILE, 1), tile),
            cut((1, TILE), lambda w, i: (0, w * tiles + i)),
            cut((TILE, share), tile),
            cut((TILE, share), tile),
            cut((TILE, share), tile),
            cut((1, share), lambda w, i: (0, 0)),
            cut((1, rows, TILE), lambda w, i: (w, 0, i)),
            cut((1, rows, 2 * share), lambda w, i: (w, 0, 0)),
        ],
        out_specs=cut((TILE, share), tile),
        out_shape=jax.ShapeDtypeStruct((count, share), BF),
        compiler_params=params(24),
        cost_estimate=pl.CostEstimate(
            flops=1000, bytes_accessed=1000, transcendentals=0
        ),
    )(tokens, scale, dots, keep, near, far, gain, onehot, seeds)


def adam_step(summed, master, first_old, second, average, step_rate, weight_decay):
    new_first = BETA_ONE * first_old + (1.0 - BETA_ONE) * summed
    new_second = BETA_TWO * second + (1.0 - BETA_TWO) * summed * summed
    update = (
        new_first
        / (1.0 - BETA_ONE**STEP)
        / (jnp.sqrt(new_second / (1.0 - BETA_TWO**STEP)) + ADAM_EPS)
    )
    new_master = master - step_rate * (update + weight_decay * master)
    new_average = EMA_RATE * average + (1.0 - EMA_RATE) * new_master
    return (summed, new_master, new_first, new_second, new_average, new_master.astype(BF))


def adam_cols_kernel(sets, rate, *refs):
    terms, (m, f, s, a), outs = refs[:sets], refs[sets : sets + 4], refs[sets + 4 :]
    grad = sum((t[...].astype(F32) for t in terms[1:]), terms[0][...].astype(F32))
    values = adam_step(grad, m[0], f[0], s[0], a[0], rate, DECAY_RATE)
    for out, value in zip(outs[:6], values, strict=True):
        out[0] = value
    if len(outs) > 6:
        used = m[0].astype(BF).astype(F32)
        part = jnp.broadcast_to(jnp.sum(used * grad, axis=1, keepdims=True), outs[6].shape)

        @pl.when((pl.program_id(0) == 0) & (pl.program_id(1) == 0))
        def _():
            outs[6][...] = jnp.zeros_like(outs[6])

        outs[6][...] += part


def adam_cols(terms, arrays, rate, name, rows=False, mixed=False):
    k, bs, n = arrays[0].shape
    part = min(n, TALL)
    tiles = n // part
    term = cut((bs, part), lambda t, j: (0, j * k + t if mixed else t * tiles + j))
    spot = cut((1, bs, part), lambda t, j: (t, 0, j))
    return pl.pallas_call(
        functools.partial(adam_cols_kernel, len(terms), rate),
        name="adam_" + name,
        grid=(k, tiles),
        in_specs=[term] * len(terms) + [spot] * 4,
        out_specs=[spot] * 6 + [cut((bs, LANES), lambda t, j: (0, 0))] * rows,
        out_shape=[jax.ShapeDtypeStruct((k, bs, n), BF if i == 5 else F32) for i in range(6)]
        + [jax.ShapeDtypeStruct((bs, LANES), F32)] * rows,
        compiler_params=params(60 if mixed else 24),
    )(*terms, *arrays)


def adam_rows_kernel(rate, *refs):
    terms, (m, f, s, a), outs = refs[:4], refs[4:8], refs[8:]
    grad = sum((t[...].astype(F32) for t in terms[1:]), terms[0][...]).T
    values = adam_step(grad, m[...], f[...], s[...], a[...], rate, DECAY_RATE)
    for out, value in zip(outs, values, strict=True):
        out[...] = value


def adam_rows(terms, offset, arrays, rate, name):
    n, bs = arrays[0].shape
    term = cut((bs, TILE), lambda i: (0, offset // TILE + i))
    spot = cut((TILE, bs), lambda i: (i, 0))
    return pl.pallas_call(
        functools.partial(adam_rows_kernel, rate),
        name="adam_" + name,
        grid=(n // TILE,),
        in_specs=[term] * 4 + [spot] * 4,
        out_specs=[spot] * 6,
        out_shape=[jax.ShapeDtypeStruct((n, bs), BF if i == 5 else F32) for i in range(6)],
        compiler_params=params(24),
    )(*terms, *arrays)


def at_once(*values):
    return lax.optimization_barrier(values)


def tie(x, *others):
    return lax.optimization_barrier((x, *others))[0]


def local(
    tokens,
    cotangent,
    mask_rows,
    genome,
    group_tokens,
    owner,
    qkv_master,
    qkv_first,
    qkv_second,
    qkv_average,
    proj_master,
    proj_first,
    proj_second,
    proj_average,
    gate_up_master,
    gate_up_first,
    gate_up_second,
    gate_up_average,
    down_master,
    down_first,
    down_second,
    down_average,
    gains_master,
    gains_first,
    gains_second,
    gains_average,
    short=None,
):
    ndp = lax.axis_size("dp")
    me = lax.axis_index("dp")
    m = lax.axis_index("mp")
    count, share = tokens.shape
    block = qkv_master.shape[1]
    windows, masked = mask_rows.shape
    rows = -(-masked // 32) * 32
    if short is None:
        short = ndp == 8 and block == LANES

    def start(b):
        at = b * block
        return ((at // share) ^ m) * share + at % share

    device = jnp.arange(ndp, dtype=jnp.int32)
    owner_x = jnp.sum(
        jnp.where((device[:, None] ^ me) == device[None, :], owner[None, :], 0), axis=1
    )
    pos = start(owner)
    pos_x = start(owner_x)

    attn_block = [qkv_master[0], qkv_master[1], qkv_master[2], proj_master.T]
    ffn_block = jnp.concatenate(
        [gate_up_master.astype(BF), down_master.T.astype(BF)[None]], axis=0
    )
    far = swap(tokens, "mp", 2)
    near = swap(tokens, "mp", 1)
    if short:
        extra = jnp.pad(gains_master, ((0, 14), (0, share - block)))
        message = jnp.concatenate(attn_block + [extra], axis=0).astype(BF)
        z_pieces = [message] + [swap(message, "dp", bit) for bit in (2, 4, 6)]
        x_pieces = [swap(piece, "dp", 1) for piece in z_pieces]
        order = [None] * 8
        for k in range(4):
            order[2 * k], order[2 * k + 1] = z_pieces[k], x_pieces[k]
        attn_w, gains = place_pieces(pos_x, order[::-1], block)
        gains = gains.reshape(2, 1, D)
    else:
        attn_block = jnp.stack(attn_block).astype(BF)
        attn_w = place_stack(pos, lax.all_gather(attn_block, "dp", axis=0, tiled=False))
        all_gains = lax.all_gather(gains_master.astype(BF), "dp", axis=1, tiled=False)
        slot = (device * block)[:, None] == pos[None, :]
        gains = jnp.sum(
            jnp.where(slot[None, :, :, None], all_gains.astype(F32)[:, None], 0.0), axis=2
        ).reshape(2, 1, D)
    ffn_stack = lax.all_gather(ffn_block, "dp", axis=0, tiled=False)

    tokens_p = [tokens, near, far, swap(far, "mp", 1)]
    padded = jnp.pad(mask_rows, ((0, 0), (0, rows - masked)), constant_values=-1)
    onehot = (
        padded[:, :, None] == lax.broadcasted_iota(jnp.int32, (1, 1, SEQ), 2)
    ).astype(BF)
    cos, sin = rotary_tables(jnp.arange(SEQ))
    cosm, sinm = rotary_tables(padded.reshape(-1))
    counts = group_tokens.astype(F32)
    picked = jnp.sum(
        jnp.where(
            genome[:, None] == jnp.arange(NGROUP, dtype=jnp.int32)[None, :], counts[None, :], 0.0
        ),
        axis=1,
    )
    window_scale = NGROUP * picked / jnp.sum(counts)
    attn_t = flip(attn_w)
    wo_far = swap(attn_t[3], "mp", 2)
    qkv, norm_one, scale_one, token_rows, q_rows = qkv_call(
        tokens_p, gains[0], tie(attn_w, attn_t), cos, sin, onehot
    )
    context, context_rows = attend_call(tie(qkv, wo_far), onehot)
    wo_p = [attn_t[3], swap(attn_t[3], "mp", 1), wo_far, swap(wo_far, "mp", 1)]
    cot = jnp.pad(cotangent.reshape(windows, masked, share), ((0, 0), (0, rows - masked), (0, 0)))
    both = jnp.concatenate([context_rows, cot.reshape(windows * rows, share)], axis=0)
    both_p = gather_mp(both)
    context_rows_p = [piece[: windows * rows] for piece in both_p]
    cot = jnp.concatenate([piece[windows * rows :] for piece in both_p], axis=1)
    context = tie(context, both_p[3])
    context_far = swap(context, "mp", 2)
    seed = jnp.repeat(window_scale, rows)[:, None] * cot.astype(F32)
    seed_low = seed.astype(BF)
    norm_rows, unit, scale_rows = rows_first_call(token_rows, context_rows_p, wo_p, gains[1])

    ffn_stack = tie(ffn_stack, norm_rows)
    if short:
        wide_w, down_w = place_ffn(pos, ffn_stack)
    else:
        wide_w = place_stack(pos, ffn_stack)
        wide_w, down_w = wide_w[:2], wide_w[2].T
    if short:
        sides = jnp.concatenate([pos_x[1::2], pos_x[0::2]])
        wide_blocks, down_send, down_keep, n2_send, n2_keep, n2_far = rows_pack_call(
            jnp.concatenate([pos, sides]), norm_rows, seed_low, wide_w, down_w
        )
    else:
        hidden_rows, gate_grad, up_grad, n2_send, n2_keep, n2_far = rows_call(
            norm_rows, seed_low, wide_w, down_w
        )

    context_near, context_far = at_once(context, context_far, n2_send)[:2]
    context_p = [context, swap(context_near, "mp", 1), context_far, swap(context_far, "mp", 1)]

    def reduce_all(lhs, rhs):
        grad = dot_l(lhs, rhs).reshape(ndp, block, rhs.shape[1])
        grad = jnp.take(grad, pos // block, axis=0, mode="clip")
        return lax.psum_scatter(grad, "dp", scatter_dimension=0, tiled=True)[0]

    n2_near = swap(n2_send, "mp", 1)
    if short:
        wide_sum = lax.psum_scatter(wide_blocks, "dp", scatter_dimension=0, tiled=False)
        down_x = swap(down_send[:2], "dp", 1)
        down_x = (down_x, swap(tie(down_send[2:], down_x), "dp", 1))
    n2_near = n2_near.astype(F32)
    n2_half = jnp.concatenate(
        [n2_keep.astype(F32) + n2_near[:, :share], n2_far.astype(F32) + n2_near[:, share:]], axis=1
    ).astype(BF)
    n2_back = swap(n2_half, "mp", 2)
    if short:
        n2_back, context_p = at_once(n2_back, context_p)
    n2_back = n2_back.astype(F32)
    n2_own = (
        n2_half.astype(F32) + jnp.concatenate([n2_back[:, share:], n2_back[:, :share]], axis=1)
    ).astype(BF)
    attn_seed, own_seed, context_grad, gain_two = seed_call(
        n2_own, swap(n2_own, "mp", 1), seed, unit, scale_rows, gains[1], attn_w
    )
    own_seed = own_seed.reshape(windows, rows, 2 * share)

    dqkv, row_dot = back_call(q_rows, context_grad, qkv, onehot, cosm, sinm, cos, sin)
    first_in = dqkv
    if short:
        down_added = add_terms(down_keep, at_once(*down_x, dqkv)[:2], "down")
        attn_send, attn_keep = pack_attention(
            sides, norm_one, dqkv, attn_seed, context_rows, gain_two
        )
        attn_send, down_added, first_in, row_dot = at_once(attn_send, down_added, dqkv, row_dot)
        attn_x = swap(attn_send, "dp", 1)
    n_send, n_keep, n_far = first_grad_call(first_in, attn_t)
    row_dot = row_dot + swap(row_dot, "mp", 1)
    if short:
        n_send, row_dot = at_once(n_send, row_dot)
    n_near = swap(n_send, "mp", 1)
    row_far = swap(row_dot, "mp", 2)
    if short:
        n_near, row_far = at_once(n_near, row_far)
    row_dot = row_dot + row_far
    n_half = (n_far.astype(F32) + n_near[:, share:].astype(F32)).astype(BF)

    if short:
        n_half, down_added, ffn_in = at_once(n_half, down_added, context_p)
        down_terms = [down_added[0]] + [swap(down_added[k], "dp", 2 * k) for k in range(1, 4)]
        n_back = swap(n_half, "mp", 2)
        ffn_out = ffn_call(tokens_p, ffn_in, wo_p, gains[1], wide_w, down_w)
        ffn_out, attn_x, down_terms, n_back = at_once(ffn_out, attn_x, down_terms, n_back)
        attn_added = add_terms(attn_keep, (attn_x,), "attention")
    else:
        n_back = swap(n_half, "mp", 2)
        ffn_out = ffn_call(tokens_p, context_p, wo_p, gains[1], wide_w, down_w)
    f_send, f_keep, f_far, residual = ffn_out
    f_near = swap(f_send, "mp", 1)
    down_old = (down_master, down_first, down_second, down_average)
    down_rate = FF ** (-0.5)
    if short:
        down_out = adam_rows(down_terms, 0, down_old, down_rate, "down")
        f_near, attn_added = at_once(f_near, attn_added)
    f_half = (f_far.astype(F32) + f_near[:, share:].astype(F32)).astype(BF)
    if short:
        f_half, attn_added = at_once(f_half, attn_added)
    f_back = swap(f_half, "mp", 2)
    if short:
        attn_terms = [attn_added[0]] + [swap(attn_added[k], "dp", 2 * k) for k in range(1, 4)]
    if short:
        gate_up_old = (gate_up_master, gate_up_first, gate_up_second, gate_up_average)
        wide_sum = tie(wide_sum, down_out[0])
        gate_up_out = adam_cols([wide_sum], gate_up_old, D ** (-0.5), "gate_up", mixed=True)
        n_back = tie(n_back, gate_up_out[0])
    input_grad = input_call(
        tokens,
        scale_one,
        row_dot,
        n_keep,
        n_near[:, :share],
        n_back,
        gains[0][:, :share],
        onehot,
        own_seed,
    )
    if short:
        f_back, input_grad = at_once(f_back, input_grad)
    output = (
        residual + f_keep.astype(F32) + f_near[:, :share].astype(F32) + f_back.astype(F32)
    ).astype(BF)
    if short:
        attn_terms, output, input_grad = at_once(attn_terms, output, input_grad)
    qkv_old = (qkv_master, qkv_first, qkv_second, qkv_average)
    proj_old = (proj_master, proj_first, proj_second, proj_average)
    gate_up_old = (gate_up_master, gate_up_first, gate_up_second, gate_up_average)
    wide_rate = D ** (-0.5)
    proj_rate = (3.0 * D / SEQ) ** (-0.5)
    if short:
        *qkv_out, first_rows = adam_cols(attn_terms, qkv_old, wide_rate, "qkv", True)
        proj_out = adam_rows(attn_terms, 3 * share, proj_old, proj_rate, "proj")
        gain_two = sum(term[LANES : LANES + 1, :LANES].astype(F32) for term in attn_terms)
        gain_one = first_rows[:, :1].T
    else:
        qkv_sum = reduce_all(norm_one, dqkv)
        qkv_sum = jnp.moveaxis(qkv_sum.reshape(block, 3, share), 1, 0)
        gate_up_sum = jnp.stack([reduce_all(norm_rows, gate_grad), reduce_all(norm_rows, up_grad)])
        proj_sum = reduce_all(attn_seed, context_rows).T
        down_sum = reduce_all(seed_low, hidden_rows).T
        gain_one = jnp.sum(
            qkv_master.astype(BF).astype(F32) * qkv_sum, axis=(0, 2)
        )[None]
        all_two = jnp.take(gain_two.reshape(ndp, block), pos // block, axis=0, mode="clip")
        gain_two = lax.psum_scatter(all_two, "dp", scatter_dimension=0, tiled=True)
        down_out = adam_step(down_sum, *down_old, down_rate, DECAY_RATE)
        gate_up_out = adam_step(gate_up_sum, *gate_up_old, wide_rate, DECAY_RATE)
        qkv_out = adam_step(qkv_sum, *qkv_old, wide_rate, DECAY_RATE)
        proj_out = adam_step(proj_sum, *proj_old, proj_rate, DECAY_RATE)
    gain_one = gain_one + swap(gain_one, "mp", 1)
    gain_one = (gain_one + swap(gain_one, "mp", 2)) / gains_master[:1].astype(BF).astype(F32)
    gains_sum = jnp.concatenate([gain_one, gain_two], axis=0)
    gains_out = adam_step(
        gains_sum, gains_master, gains_first, gains_second, gains_average, GAIN_RATE, 0.0
    )
    return (output, input_grad, *qkv_out, *proj_out, *gate_up_out, *down_out, *gains_out)


def solution(mesh, short=None):
    tokens = P("dp", "mp")
    cols = P(None, "dp", "mp")
    lines = P("mp", "dp")
    gains = P(None, "dp")
    in_specs = (tokens, tokens, P("dp", None), P("dp"), P(), P())
    in_specs += (cols,) * 4 + (lines,) * 4 + (cols,) * 4 + (lines,) * 4 + (gains,) * 4
    out_specs = (tokens, tokens)
    out_specs += (cols,) * 6 + (lines,) * 6 + (cols,) * 6 + (lines,) * 6 + (gains,) * 6
    return jax.shard_map(
        functools.partial(local, short=short),
        mesh=mesh,
        in_specs=in_specs,
        out_specs=out_specs,
        check_vma=False,
    )
```
